128 devices in a mesh: gx: 8 (over z, x_hi), gy: 8 (over y, core), gz: 2 (over x_lo).
Axes of the slice: x: 4 (x_hi: 2, x_lo: 2; x = x_hi * 2 + x_lo), y: 4, z: 4, core: 2. Of those that a mesh axis runs over, the one named last changes fastest.
Arguments:
- populations: float32 [27, 32, 64, 512], P(None, 'gx', 'gy', 'gz'), may hold values from 0 to 1, as said below
- blockage: float32 [32, 64, 512], P('gx', 'gy', 'gz'), may hold values from 0.02 to 0.4
- solid_mask: int32 [32, 64, 512], P('gx', 'gy', 'gz'), may hold values 0 or 1
- cotangent: float32 [27, 32, 64, 512], P(None, 'gx', 'gy', 'gz'), may hold values from -6 to 6
Outputs:
- adjoint_start: float32 [27, 32, 64, 512], P(None, 'gx', 'gy', 'gz')
- grad_blockage: float32 [32, 64, 512], P('gx', 'gy', 'gz')
The draws below stay inside these ranges and needn't reach their ends.
Inputs may be any that keep to these rules, and one draw needn't show every extreme that they name: `populations`: every population is positive.
All inputs are finite; a program needn't handle non-finite values. No bound on the sum of `solid_mask` on one device may be relied on, other than what follows from the above.
Results may differ from the reference program's by a relative error of at most 0.0003.
Values sent between devices are 32-bit elements; how exact they have to be, the bound alone decides.
No kernel may reach another device: no remote copies, remote signals or barrier semaphores. Data moves between devices by JAX's collectives and lax.ppermute only.
A program may use at most 128 MiB of HBM per device.

```python
import math
import jax
import jax.numpy as jnp
from jax import lax

STEPS = 3
NX = 32
NY = 64
NZ = 512


def draw_populations(key, part):
    key = jax.random.fold_in(key, 7)
    key_drift, key_density, key_noise = jax.random.split(key, 3)
    velocities = [(comp_a, comp_b, comp_d) for comp_a in (-1, 0, 1) for comp_b in (-1, 0, 1) for comp_d in (-1, 0, 1)]
    weight_of = {0: 8.0 / 27.0, 1: 2.0 / 27.0, 2: 1.0 / 54.0, 3: 1.0 / 216.0}
    weight_vec = jnp.array([weight_of[abs(vec[0]) + abs(vec[1]) + abs(vec[2])] for vec in velocities], jnp.float32).reshape(27, 1, 1, 1)
    comp_x = jnp.array([vec[0] for vec in velocities], jnp.float32).reshape(27, 1, 1, 1)
    comp_y = jnp.array([vec[1] for vec in velocities], jnp.float32).reshape(27, 1, 1, 1)
    comp_z = jnp.array([vec[2] for vec in velocities], jnp.float32).reshape(27, 1, 1, 1)
    drift = jax.random.uniform(key_drift, (3, NX, NY, NZ), jnp.float32, -0.05, 0.05)
    noise = jax.random.uniform(key_noise, (27, NX, NY, NZ), jnp.float32, -0.3, 0.3)
    density = jnp.exp(jax.random.uniform(key_density, (NX, NY, NZ), jnp.float32, -0.2, 0.2))
    project = comp_x * drift[0] + comp_y * drift[1] + comp_z * drift[2]
    return weight_vec * density * (1.0 + 3.0 * project + noise)


def place_ends(entries, own_key, smallest, high):
    longest = entries.shape.index(max(entries.shape))
    spots = []
    for shift in (0, 1):
        where = [jax.random.randint(jax.random.fold_in(own_key, axis), (), 0, length) for axis, length in enumerate(entries.shape)]
        where[longest] = (where[longest] + shift) % entries.shape[longest]
        spots.append(tuple(where))
    return entries.at[spots[0]].set(smallest).at[spots[1]].set(high)


def steps_of(key, dims, cuts, smallest, largest):
    factor_of, own = 1.0, jax.random.fold_in(key, 6)
    for axis_at, blocks in cuts:
        draws = jnp.exp(jax.random.uniform(jax.random.fold_in(own, axis_at), (blocks,), jnp.float32, smallest / len(cuts), largest / len(cuts)))
        factor_of = factor_of * jnp.repeat(draws, dims[axis_at] // blocks).reshape([-1 if axis == axis_at else 1 for axis in range(len(dims))])
    return factor_of


def gaussian(rng, shape, spread, bound, cuts=(), kind=jnp.bfloat16):
    values = jax.random.normal(rng, shape, jnp.float32) * spread
    if len(cuts) > 0:
        values = steps_of(rng, shape, cuts, -0.22, 0.18) * values
    return jnp.clip(values, min=-bound, max=bound).astype(kind)


def setup_inputs(seed: int = 0) -> dict:
    arg_keys = jax.random.split(jax.random.key(seed), 5)
    populations = draw_populations(jax.random.fold_in(arg_keys[4], 71), 0)
    blockage = jnp.clip(jnp.exp(math.log(0.4) - 2.9957323 * jax.random.uniform(arg_keys[1], (NX, NY, NZ), jnp.float32) ** steps_of(arg_keys[1], (NX, NY, NZ), ((0, 8), (1, 8), (2, 2)), -0.2, 0.2)), 0.02, 0.4)
    solid_mask = place_ends((jax.random.randint(arg_keys[2], (NX, NY, NZ), 0, 8) < 1).astype(jnp.int32), jax.random.fold_in(arg_keys[2], 1), 0, 1)
    cotangent = gaussian(arg_keys[3], (27, NX, NY, NZ), 1.0, 6.0, ((1, 8), (2, 8), (3, 2)), jnp.float32)
    return dict(populations=populations, blockage=blockage, solid_mask=solid_mask, cotangent=cotangent)


relax_rate = 1.25

def lattice():
    velocities = [(comp_a, comp_b, comp_d) for comp_a in (-1, 0, 1) for comp_b in (-1, 0, 1) for comp_d in (-1, 0, 1)]
    weight_of = {0: 8.0 / 27.0, 1: 2.0 / 27.0, 2: 1.0 / 54.0, 3: 1.0 / 216.0}
    weights_table = [weight_of[abs(vec[0]) + abs(vec[1]) + abs(vec[2])] for vec in velocities]
    return (velocities, weights_table)

def collide(pops, solid):
    velocities, weights_table = lattice()
    vel_matrix = jnp.array(velocities, jnp.float32)
    weight_vec = jnp.array(weights_table, jnp.float32).reshape((27,) + (1,) * (pops.ndim - 1))
    density = lax.optimization_barrier(jnp.sum(pops, axis=0))
    momentum = jnp.tensordot(vel_matrix.T, pops, axes=1, precision=lax.Precision.HIGHEST)
    speed = momentum / density
    project = jnp.tensordot(vel_matrix, speed, axes=1, precision=lax.Precision.HIGHEST)
    sq_speed = lax.optimization_barrier(jnp.sum(speed * speed, axis=0))
    equilib = weight_vec * density * (1.0 + 3.0 * project + 4.5 * project * project - 1.5 * sq_speed)
    relaxed = pops - relax_rate * (pops - equilib)
    return (1.0 - solid) * relaxed + solid * pops[::-1]

def stream(pops, orient):
    velocities, _ = lattice()
    pieces = []
    for index in range(27):
        shift_x = orient * velocities[index][0]
        shift_y = orient * velocities[index][1]
        shift_z = orient * velocities[index][2]
        moved = jnp.roll(pops[index], (shift_x, shift_y, shift_z), axis=(0, 1, 2))
        if shift_z == 1:
            moved = moved.at[:, :, 0].set(pops[26 - index][:, :, 0])
        if shift_z == -1:
            moved = moved.at[:, :, -1].set(pops[26 - index][:, :, -1])
        pieces.append(moved)
    return jnp.stack(pieces)

def collide_slabs(pops, solid):
    slabs = jnp.moveaxis(pops, 1, 0)
    result = lax.map(lambda pair: collide(pair[0], pair[1]), (slabs, solid))
    return jnp.moveaxis(result, 0, 1)

def back_slab(triple):
    pops, solid, adjoint = triple
    _, pullback = jax.vjp(collide, pops, solid)
    return pullback(adjoint)

def reference(populations, blockage, solid_mask, cotangent):
    mask_float = solid_mask.astype(jnp.float32)
    solid = blockage * (1.0 - mask_float) + mask_float
    states = []
    pops = populations
    for section in range(STEPS):
        states.append(pops)
        pops = stream(collide_slabs(pops, solid), 1)
    adjoint = cotangent
    total = jnp.zeros(blockage.shape, jnp.float32)
    for section in reversed(range(STEPS)):
        pulled = stream(adjoint, -1)
        adj_slabs, blame = lax.map(back_slab, (jnp.moveaxis(states[section], 1, 0), solid, jnp.moveaxis(pulled, 1, 0)))
        adjoint = jnp.moveaxis(adj_slabs, 0, 1)
        total = total + blame
    return (adjoint, total * (1.0 - mask_float))
```

```python
import functools
import jax
import jax.numpy as jnp
from jax import lax
from jax.experimental import pallas as pl
from jax.experimental.pallas import tpu as pltpu
from jax.sharding import PartitionSpec as P

DIRS = [(a, b, d) for a in (-1, 0, 1) for b in (-1, 0, 1) for d in (-1, 0, 1)]
WEIGHTS = [(8.0 / 27.0, 2.0 / 27.0, 1.0 / 54.0, 1.0 / 216.0)[abs(a) + abs(b) + abs(d)] for a, b, d in DIRS]
OMEGA = 1.25
NT = 17
ROWS = NT * 8
MINI = pl.ds(128, 8)
F32 = jnp.float32


def tile(n):
    return pl.ds(n * 8, 8) if isinstance(n, int) else pl.ds(pl.multiple_of(n * 8, 8), 8)


def lanes():
    return lax.broadcasted_iota(jnp.int32, (8, 128), 1)


def subs():
    return lax.broadcasted_iota(jnp.int32, (8, 128), 0)


def roll_l(v, k):
    return pltpu.roll(v, k, 1)


def roll_s(v, k):
    return pltpu.roll(v, k, 0)


def mod128(k):
    return lax.rem(k + 256, 128)


def sides(axis):
    parity = lax.rem(lax.axis_index(axis), 2)
    return (1 - 2 * parity, 2 * parity - 1)


def moments(f):
    rho = f[13]
    mom = [None, None, None]
    for i in range(13):
        plus, minus = f[i] + f[26 - i], f[26 - i] - f[i]
        rho = rho + plus
        for k in range(3):
            c = DIRS[26 - i][k]
            if c:
                term = minus if c > 0 else -minus
                mom[k] = term if mom[k] is None else (mom[k] + minus if c > 0 else mom[k] - minus)
    inv = 1.0 / rho
    return rho, [m * inv for m in mom]


def dot_c(vec, comps):
    out = None
    for c, v in zip(vec, comps):
        if c:
            if out is None:
                out = v if c > 0 else -v
            else:
                out = out + v if c > 0 else out - v
    return out


def collide(f, solid, rho, u):
    fluid = 1.0 - solid
    own = (1.0 - OMEGA) * fluid
    base = OMEGA * fluid * rho
    rest = base * (1.0 - 1.5 * (u[0] * u[0] + u[1] * u[1] + u[2] * u[2]))
    out = [None] * 27
    for i in range(13):
        j = 26 - i
        w = WEIGHTS[i]
        cu = dot_c(DIRS[j], u)
        bc = base * cu
        even = w * (rest + 4.5 * (bc * cu))
        odd = (3.0 * w) * bc
        out[j] = own * f[j] + solid * f[i] + (even + odd)
        out[i] = own * f[i] + solid * f[j] + (even - odd)
    out[13] = (own + solid) * f[13] + WEIGHTS[13] * rest
    return out


def pull_back(p, solid, u, f=None, rho=None):
    w0 = WEIGHTS[13] * p[13]
    w1 = [None] * 3
    w2 = {}
    add = lambda x, y: y if x is None else x + y
    by_class = {}
    for i in range(13):
        j = 26 - i
        plus, minus = WEIGHTS[i] * (p[j] + p[i]), WEIGHTS[i] * (p[j] - p[i])
        w0 = w0 + plus
        c = DIRS[j]
        for k in range(3):
            if c[k]:
                w1[k] = add(w1[k], minus if c[k] > 0 else -minus)
            for m in range(k, 3):
                cc = c[k] * c[m]
                if cc:
                    w2[(k, m)] = add(w2.get((k, m)), plus if cc > 0 else -plus)
    at = lambda k, m: w2[(min(k, m), max(k, m))]
    w2u = [at(k, 0) * u[0] + at(k, 1) * u[1] + at(k, 2) * u[2] for k in range(3)]
    uwu = u[0] * w2u[0] + u[1] * w2u[1] + u[2] * w2u[2]
    uu = u[0] * u[0] + u[1] * u[1] + u[2] * u[2]
    fluid = 1.0 - solid
    own = (1.0 - OMEGA) * fluid
    gain = OMEGA * fluid
    g_rho = gain * (w0 * (1.0 + 1.5 * uu) - 4.5 * uwu)
    g_mom = [gain * (3.0 * w1[k] + 9.0 * w2u[k] - 3.0 * (u[k] * w0)) for k in range(3)]
    out = [None] * 27
    for i in range(13):
        j = 26 - i
        odd = dot_c(DIRS[j], g_mom)
        out[j] = own * p[j] + solid * p[i] + (g_rho + odd)
        out[i] = own * p[i] + solid * p[j] + (g_rho - odd)
    out[13] = (own + solid) * p[13] + g_rho
    if f is None:
        return out, None
    blame = OMEGA * (p[13] * f[13])
    for i in range(13):
        j = 26 - i
        blame = blame + (p[i] * (f[j] - (1.0 - OMEGA) * f[i]) + p[j] * (f[i] - (1.0 - OMEGA) * f[j]))
    w1u = w1[0] * u[0] + w1[1] * u[1] + w1[2] * u[2]
    blame = blame - (OMEGA * rho) * (w0 * (1.0 - 1.5 * uu) + 3.0 * w1u + 4.5 * uwu)
    return out, blame


def stream_main(own, yh, out_own, out_yh, orient, gz, low, high, put):
    lane, sub = lanes(), subs()
    floor = (lane == 0) & (gz == 0)
    roof = (lane == 127) & (gz == 1)

    def body(x, carry):
        for a in (-1, 0, 1):
            for b in (-1, 0, 1):
                xs = x - orient * a
                bp = orient * b
                both = out_yh is not None
                need = both or bp != 0
                into = 9 * (a + 1) + 3 * (b + 1) + 1 + orient * (2 * gz - 1)
                shift = 127 - 2 * gz - 4 * xs
                ins_own = roll_l(own[into, MINI, :], shift)
                ins_yh = roll_l(yh[into, MINI, :], shift) if need else None
                for d in (-1, 0, 1):
                    i = 9 * (a + 1) + 3 * (b + 1) + d + 1
                    dp = orient * d

                    def shifted(ref, ins):
                        t0, t1 = ref[i, tile(2 * xs), :], ref[i, tile(2 * xs + 1), :]
                        if dp == 1:
                            return (jnp.where(lane == 0, ins, roll_l(t0, 1)), roll_l(jnp.where(lane == 127, t0, t1), 1))
                        if dp == -1:
                            return (roll_l(jnp.where(lane == 0, t1, t0), 127), jnp.where(lane == 127, ins, roll_l(t1, 127)))
                        return t0, t1

                    mine = shifted(own, ins_own)
                    halo = shifted(yh, ins_yh) if need else (None, None)
                    for half in (0, 1):
                        vo, vy = mine[half], halo[half]
                        ny = vy
                        if bp == 1:
                            no = roll_s(jnp.where(sub == 7, vy, vo), 1)
                            if both:
                                ny = roll_s(jnp.where(sub == 7, vo, vy), 1)
                        elif bp == -1:
                            no = roll_s(jnp.where(sub == 0, vy, vo), 7)
                            if both:
                                ny = roll_s(jnp.where(sub == 0, vo, vy), 7)
                        else:
                            no = vo
                        wall = floor if (dp == 1 and half == 0) else roof if (dp == -1 and half == 1) else None
                        here = tile(2 * x + half)
                        if wall is not None:
                            no = jnp.where(wall, own[26 - i, here, :], no)
                            if both:
                                ny = jnp.where(wall, yh[26 - i, here, :], ny)
                        put(out_own, i, x, half, no)
                        if both:
                            out_yh[i, here, :] = ny
        return carry

    lax.fori_loop(low, high, body, 0)


def put_tile(ref, i, x, half, value):
    ref[i, tile(2 * x + half), :] = value


def stream_mini(own, yh, out_own, out_yh, orient, gz):
    lane, sub = lanes(), subs()
    slot = lax.rem(lane, 4)
    edge = 1 - gz
    for a in (-1, 0, 1):
        for b in (-1, 0, 1):
            bp = orient * b
            both = out_yh is not None
            need = both or bp != 0
            outof = 9 * (a + 1) + 3 * (b + 1) + 1 + orient * (1 - 2 * gz)

            def rim(ref):
                acc = jnp.zeros((8, 128), F32)
                for xe in range(8):
                    src = ref[outof, tile(2 * xe + edge), :]
                    acc = jnp.where(lane == 4 * xe + 3 * gz, roll_l(src, 4 * xe + 1 + 2 * gz), acc)
                return acc

            rim_own = rim(own)
            rim_yh = rim(yh) if need else None
            for d in (-1, 0, 1):
                i = 9 * (a + 1) + 3 * (b + 1) + d + 1
                dp = orient * d
                ap = orient * a

                def shifted(ref, edge_values):
                    v = ref[i, MINI, :]
                    if dp == 1:
                        v = jnp.where(slot == 0, edge_values, roll_l(v, 1))
                    if dp == -1:
                        v = jnp.where(slot == 3, edge_values, roll_l(v, 127))
                    if ap:
                        v = roll_l(v, (4 * ap) % 128)
                    return v

                vo = shifted(own, rim_own)
                vy = shifted(yh, rim_yh) if need else None
                ny = vy
                if bp == 1:
                    no = roll_s(jnp.where(sub == 7, vy, vo), 1)
                    if both:
                        ny = roll_s(jnp.where(sub == 7, vo, vy), 1)
                elif bp == -1:
                    no = roll_s(jnp.where(sub == 0, vy, vo), 7)
                    if both:
                        ny = roll_s(jnp.where(sub == 0, vo, vy), 7)
                else:
                    no = vo
                out_own[i, MINI, :] = no
                if both:
                    out_yh[i, MINI, :] = ny


def entries(e, orient, stride):
    others = [(r // 3) * 3 + r % 3 if stride == 9 else (r // 3) * 9 + r % 3 for r in range(9)]
    inward, outward = stride * (orient * e + 1), stride * (1 - orient * e)
    out = [(inward + c, 1, None, 0) for c in others]
    out += [(stride + c, 1, None, 0) for c in others]
    out += [(inward + c, 2, outward + c, orient * (r % 3 - 1)) for r, c in enumerate(others)]
    return out


def wall_masks(gz, by_half):
    lane, half = lanes(), lax.rem(subs(), 2)
    floor, roof = (lane == 0) & (gz == 0), (lane == 127) & (gz == 1)
    if by_half:
        return {-1: floor & (half == 0), 1: roof & (half == 1)}
    return {-1: floor, 1: roof}


def pack_x(msg, e, orient, gz, pops, adj=None, solid=None):
    near = 2 + 3 * ((e + 1) // 2)
    walls = wall_masks(gz, False)
    lane = lanes()
    items = [(pops, i, near if layer == 1 else near - e, st, dp) for i, layer, st, dp in entries(e, orient, 9)]
    if adj is not None:
        items += [(adj, 9 * (1 - e) + c, near, None, 0) for c in range(9)]
        items += [(solid, 0, near, None, 0)]
    strip = [jnp.zeros((8, 128), F32) for _ in range((len(items) + 31) // 32)]
    for k, (ref, i, plane, stash, dp) in enumerate(items):
        for half in (0, 1):
            v = ref[i, tile(2 * plane + half), :]
            if stash is not None and ((dp == -1 and half == 0) or (dp == 1 and half == 1)):
                v = jnp.where(walls[dp], ref[stash, tile(2 * near + half), :], v)
            msg[(2 * k + half) * 8 : (2 * k + half) * 8 + 8, :] = v
        s = 4 * (k % 32)
        moved = roll_l(ref[i, MINI, :], mod128(s - 4 * plane))
        strip[k // 32] = jnp.where((lane >= s) & (lane < s + 4), moved, strip[k // 32])
    for n, v in enumerate(strip):
        r = (2 * len(items) + n) * 8
        msg[r : r + 8, :] = v


def unpack_x(msg, s, orient, pops, adj=None, solid=None):
    near = 2 + 3 * ((s + 1) // 2) + s
    e = -s
    lane = lanes()
    plane_of = lax.div(lane, 4)
    outward = 9 * (1 - orient * e)
    items = [(pops, i, near if layer == 1 else near + s, st) for i, layer, st, _ in entries(e, orient, 9)]
    if adj is not None:
        items += [(adj, 9 * (1 - e) + c, near, None) for c in range(9)]
        items += [(solid, 0, near, None)]
    for k, (ref, i, plane, stash) in enumerate(items):
        for half in (0, 1):
            v = msg[(2 * k + half) * 8 : (2 * k + half) * 8 + 8, :]
            ref[i, tile(2 * plane + half), :] = v
            if stash is not None:
                ref[stash, tile(2 * near + half), :] = v
        r = (2 * len(items) + k // 32) * 8
        moved = roll_l(msg[r : r + 8, :], mod128(4 * plane - 4 * (k % 32)))
        ref[i, MINI, :] = jnp.where(plane_of == plane, moved, ref[i, MINI, :])


def pack_y(msg, e, orient, gz, pops, adj=None, solid=None):
    near = 7 * ((e + 1) // 2)
    walls = wall_masks(gz, True)
    items = [(pops, i, near if layer == 1 else near - e, st, dp) for i, layer, st, dp in entries(e, orient, 3)]
    if adj is not None:
        items += [(adj, 3 * (1 - e) + c, near, None, 0) for c in Y_OTHERS]
        items += [(solid, 0, near, None, 0)]
    for k, (ref, i, row, stash, dp) in enumerate(items):
        for part in (0, 1):
            v = ref[i, pl.ds(64 * part + row, 8, stride=8), :]
            if dp:
                v = jnp.where(walls[dp], ref[stash, pl.ds(64 * part + near, 8, stride=8), :], v)
            msg[(2 * k + part) * 8 : (2 * k + part) * 8 + 8, :] = v
        msg[16 * len(items) + k : 16 * len(items) + k + 1, :] = ref[i, pl.ds(128 + row, 1), :]


Y_OTHERS = [(r // 3) * 9 + r % 3 for r in range(9)]


def unpack_y(msg, s, orient, pops, adj=None, solid=None):
    near = 7 * ((1 - s) // 2)
    e = -s
    items = [(pops, i, near if layer == 1 else near + s, st) for i, layer, st, _ in entries(e, orient, 3)]
    if adj is not None:
        items += [(adj, 3 * (1 - e) + c, near, None) for c in Y_OTHERS]
        items += [(solid, 0, near, None)]
    for k, (ref, i, row, stash) in enumerate(items):
        for part in (0, 1):
            v = msg[(2 * k + part) * 8 : (2 * k + part) * 8 + 8, :]
            ref[i, pl.ds(64 * part + row, 8, stride=8), :] = v
            if stash is not None:
                ref[stash, pl.ds(64 * part + near, 8, stride=8), :] = v
        ref[i, pl.ds(128 + row, 1), :] = msg[16 * len(items) + k : 16 * len(items) + k + 1, :]


def solid_of(blockage, mask):
    m = mask.astype(F32)
    return blockage * (1.0 - m) + m


def cut_kernel(pops, block, mask, cot, msg):
    gz = lax.axis_index("gz")
    lane = lanes()
    top = gz == 0
    for n in range(7):
        acc = jnp.zeros((8, 128), F32)
        for j in range(8):
            slot = 8 * n + j
            if slot > 54:
                break
            for x in range(4):
                if slot == 54:
                    hi = solid_of(block[x, :, 128:256], mask[x, :, 128:256])
                    lo = solid_of(block[x, :, 0:128], mask[x, :, 0:128])
                else:
                    ref, i = (pops, slot) if slot < 27 else (cot, slot - 27)
                    hi, lo = ref[i, x, :, 128:256], ref[i, x, :, 0:128]
                at = 16 * j + 4 * x
                moved = roll_l(jnp.where(top, hi, lo), mod128(at + 4 - 4 * gz))
                acc = jnp.where((lane >= at) & (lane < at + 4), moved, acc)
        msg[8 * n : 8 * n + 8, :] = acc


def first_kernel(pops, block, mask, cot, cut, tx, ax, sx, msg0, msg1):
    gz = lax.axis_index("gz")

    def body(x, carry):
        for half in (0, 1):
            z = pl.ds(128 * half, 128)
            here = tile(2 * (x + 2) + half)
            s = solid_of(block[x, :, z], mask[x, :, z])
            sx[0, here, :] = s
            f = [pops[i, x, :, z] for i in range(27)]
            rho, u = moments(f)
            out = collide(f, s, rho, u)
            for i in range(27):
                tx[i, here, :] = out[i]
                ax[i, here, :] = cot[i, x, :, z]
        return carry

    lax.fori_loop(0, 4, body, 0)

    def slot(n):
        return roll_l(cut[8 * (n // 8) : 8 * (n // 8) + 8, :], (8 - 16 * (n % 8)) % 128)

    s = slot(54)
    sx[0, MINI, :] = s
    f = [slot(i) for i in range(27)]
    rho, u = moments(f)
    out = collide(f, s, rho, u)
    for i in range(27):
        tx[i, MINI, :] = out[i]
        ax[i, MINI, :] = slot(27 + i)
    for msg, e in zip((msg0, msg1), sides("gx")):
        pack_x(msg, e, 1, gz, tx, ax, sx)


def carry_over(pairs):
    def body(k, carry):
        here = tile(jnp.where(k == 8, 16, k + 4))
        for src, dst in pairs:
            for i in range(src.shape[0]):
                dst[i, here, :] = src[i, here, :]
        return carry

    lax.fori_loop(0, 9, body, 0)


def span_kernel(tx_in, ax_in, sx_in, got0, got1, tx, ax, sx, msg0, msg1):
    gz = lax.axis_index("gz")
    carry_over(((tx_in, tx), (ax_in, ax), (sx_in, sx)))
    for msg, s in zip((got0, got1), sides("gx")):
        unpack_x(msg, s, 1, tx, ax, sx)
    for msg, e in zip((msg0, msg1), sides("gy")):
        pack_y(msg, e, 1, gz, tx, ax, sx)


def span_kernel_2(tx_in, got0, got1, tx, msg0, msg1):
    gz = lax.axis_index("gz")
    carry_over(((tx_in, tx),))
    for msg, s in zip((got0, got1), sides("gx")):
        unpack_x(msg, s, -1, tx)
    for msg, e in zip((msg0, msg1), sides("gy")):
        pack_y(msg, e, -1, gz, tx)


def put_own(ref, i, x, half, value):
    ref[i, tile(2 * (x - 2) + half), :] = value


def middle_kernel(tx, ax, sx, got0, got1, a2, f1, u_own, u_yh, sy, q2, msg0, msg1, ty, ay, f_own, f_yh, c_own, c_yh, p_own):
    gz = lax.axis_index("gz")
    for msg, s in zip((got0, got1), sides("gy")):
        unpack_y(msg, s, 1, ty, ay, sy)
    stream_main(tx, ty, f_own, f_yh, 1, gz, 1, 7, put_tile)
    stream_mini(tx, ty, f_own, f_yh, 1, gz)

    def again(k, carry):
        n = jnp.where(k == 12, 16, k + 2)
        here = tile(n)
        for src, sol, dst, us in ((f_own, sx, c_own, u_own), (f_yh, sy, c_yh, u_yh)):
            f = [src[i, here, :] for i in range(27)]
            rho, u = moments(f)
            us[0, here, :] = rho
            for c in range(3):
                us[c + 1, here, :] = u[c]
            out = collide(f, sol[0, here, :], rho, u)
            for i in range(27):
                dst[i, here, :] = out[i]
        return carry

    lax.fori_loop(0, 13, again, 0)

    def keep(n, carry):
        for i in range(27):
            f1[i, tile(n), :] = f_own[i, tile(n + 4), :]
        return carry

    lax.fori_loop(0, 8, keep, 0)
    stream_main(c_own, c_yh, f_own, None, 1, gz, 2, 6, put_tile)
    stream_mini(c_own, c_yh, f_own, None, 1, gz)
    stream_main(ax, ay, p_own, None, -1, gz, 2, 6, put_tile)
    stream_mini(ax, ay, p_own, None, -1, gz)

    def back(k, carry):
        n = jnp.where(k == 8, 16, k + 4)
        here = tile(n)
        f = [f_own[i, here, :] for i in range(27)]
        p = [p_own[i, here, :] for i in range(27)]
        rho, u = moments(f)
        out, blame = pull_back(p, sx[0, here, :], u, f, rho)
        for i in range(27):
            a2[i, here, :] = out[i]
        q2[tile(k), :] = blame
        return carry

    lax.fori_loop(0, 9, back, 0)
    for msg, e in zip((msg0, msg1), sides("gx")):
        pack_x(msg, e, -1, gz, a2)


def last_kernel(a2, pops, block, mask, f1, u_own, u_yh, sx, sy, q2, got0, got1, adjoint, grad, ty, p_own, p_yh, c_own, c_yh):
    gz = lax.axis_index("gz")
    for msg, s in zip((got0, got1), sides("gy")):
        unpack_y(msg, s, -1, ty)
    stream_main(a2, ty, p_own, p_yh, -1, gz, 1, 7, put_tile)
    stream_mini(a2, ty, p_own, p_yh, -1, gz)

    def again(k, carry):
        n = jnp.where(k == 12, 16, k + 2)
        here = tile(n)
        for src, sol, dst, us in ((p_own, sx, c_own, u_own), (p_yh, sy, c_yh, u_yh)):
            out, _ = pull_back([src[i, here, :] for i in range(27)], sol[0, here, :], [us[c, here, :] for c in (1, 2, 3)])
            for i in range(27):
                dst[i, here, :] = out[i]
        return carry

    lax.fori_loop(0, 13, again, 0)

    def first_blame(x, carry):
        for half in (0, 1):
            here = tile(2 * x + 4 + half)
            there = tile(2 * x + half)
            u = [u_own[c, here, :] for c in (1, 2, 3)]
            _, blame = pull_back([p_own[i, here, :] for i in range(27)], sx[0, here, :], u, [f1[i, there, :] for i in range(27)], u_own[0, here, :])
            grad[x, :, pl.ds(128 * half, 128)] = blame + q2[there, :]
        return carry

    lax.fori_loop(0, 4, first_blame, 0)
    stream_main(c_own, c_yh, p_own, None, -1, gz, 2, 6, put_tile)

    def back(x, carry):
        for half in (0, 1):
            z = pl.ds(128 * half, 128)
            here = tile(2 * x + 4 + half)
            f = [pops[i, x, :, z] for i in range(27)]
            rho, u = moments(f)
            out, blame = pull_back([p_own[i, here, :] for i in range(27)], sx[0, here, :], u, f, rho)
            for i in range(27):
                adjoint[i, x, :, z] = out[i]
            grad[x, :, z] = (1.0 - mask[x, :, z].astype(F32)) * (grad[x, :, z] + blame)
        return carry

    lax.fori_loop(0, 4, back, 0)


def call(kernel, outs, scratch=(), name=None):
    return pl.pallas_call(
        kernel,
        out_shape=[jax.ShapeDtypeStruct(s, F32) for s in outs],
        scratch_shapes=[pltpu.VMEM(s, F32) for s in scratch],
        compiler_params=pltpu.CompilerParams(vmem_limit_bytes=48 * 1024 * 1024),
        name=name,
    )


def swap(x, axis, odd):
    n = lax.axis_size(axis)
    pairs = [(i, (i ^ 1) if not odd else ((i + 1) % n if i % 2 else (i - 1) % n)) for i in range(n)]
    return lax.ppermute(x, axis, pairs)


BIG = (27, ROWS, 128)
ONE = (1, ROWS, 128)
X1 = ((2 * 37 + 2) * 8, 128)
Y1 = (37 * 16 + 40, 128)
X2 = ((2 * 27 + 1) * 8, 128)
Y2 = (27 * 16 + 32, 128)


def body(populations, blockage, solid_mask, cotangent):
    (cut,) = call(cut_kernel, [(56, 128)], name="cut")(populations, blockage, solid_mask, cotangent)
    cut = lax.ppermute(cut, "gz", [(0, 1), (1, 0)])
    tx, ax, sx, m0, m1 = call(first_kernel, [BIG, BIG, ONE, X1, X1], name="first")(populations, blockage, solid_mask, cotangent, cut)
    m0, m1 = swap(m0, "gx", False), swap(m1, "gx", True)
    tx, ax, sx, m0, m1 = call(span_kernel, [BIG, BIG, ONE, Y1, Y1], name="span")(tx, ax, sx, m0, m1)
    m0, m1 = swap(m0, "gy", False), swap(m1, "gy", True)
    a2, f1, u_own, u_yh, sy, q2, m0, m1 = call(
        middle_kernel,
        [BIG, (27, 64, 128), (4, ROWS, 128), (4, ROWS, 128), ONE, (72, 128), X2, X2],
        scratch=[BIG] * 7,
        name="middle",
    )(tx, ax, sx, m0, m1)
    m0, m1 = swap(m0, "gx", False), swap(m1, "gx", True)
    a2, m0, m1 = call(span_kernel_2, [BIG, Y2, Y2], name="span2")(a2, m0, m1)
    m0, m1 = swap(m0, "gy", False), swap(m1, "gy", True)
    adjoint, grad = call(last_kernel, [(27, 4, 8, 256), (4, 8, 256)], scratch=[BIG] * 5, name="last")(
        a2, populations, blockage, solid_mask, f1, u_own, u_yh, sx, sy, q2, m0, m1
    )
    return adjoint, grad


def solution(mesh):
    placed = (P(None, "gx", "gy", "gz"), P("gx", "gy", "gz"), P("gx", "gy", "gz"), P(None, "gx", "gy", "gz"))
    return jax.shard_map(
        body, mesh=mesh, in_specs=placed, out_specs=(P(None, "gx", "gy", "gz"), P("gx", "gy", "gz")), check_vma=False
    )
```

```python
import functools
import jax
import jax.numpy as jnp
from jax import lax
from jax.experimental import pallas as pl
from jax.experimental.pallas import tpu as pltpu
from jax.sharding import PartitionSpec as P

DIRS = [(a, b, d) for a in (-1, 0, 1) for b in (-1, 0, 1) for d in (-1, 0, 1)]
WEIGHTS = [(8.0 / 27.0, 2.0 / 27.0, 1.0 / 54.0, 1.0 / 216.0)[abs(a) + abs(b) + abs(d)] for a, b, d in DIRS]
OMEGA = 1.25
NT = 17
ROWS = NT * 8
MINI = pl.ds(128, 8)
F32 = jnp.float32


def tile(n):
    return pl.ds(n * 8, 8) if isinstance(n, int) else pl.ds(pl.multiple_of(n * 8, 8), 8)


def lanes():
    return lax.broadcasted_iota(jnp.int32, (8, 128), 1)


def subs():
    return lax.broadcasted_iota(jnp.int32, (8, 128), 0)


def roll_l(v, k):
    return pltpu.roll(v, k, 1)


def roll_s(v, k):
    return pltpu.roll(v, k, 0)


def mod128(k):
    return lax.rem(k + 256, 128)


def sides(axis):
    parity = lax.rem(lax.axis_index(axis), 2)
    return (1 - 2 * parity, 2 * parity - 1)


def moments(f):
    rho = f[13]
    mom = [None, None, None]
    for i in range(13):
        plus, minus = f[i] + f[26 - i], f[26 - i] - f[i]
        rho = rho + plus
        for k in range(3):
            c = DIRS[26 - i][k]
            if c:
                term = minus if c > 0 else -minus
                mom[k] = term if mom[k] is None else (mom[k] + minus if c > 0 else mom[k] - minus)
    inv = 1.0 / rho
    return rho, [m * inv for m in mom]


def dot_c(vec, comps):
    out = None
    for c, v in zip(vec, comps):
        if c:
            if out is None:
                out = v if c > 0 else -v
            else:
                out = out + v if c > 0 else out - v
    return out


def collide(f, solid, rho, u):
    fluid = 1.0 - solid
    own = (1.0 - OMEGA) * fluid
    base = OMEGA * fluid * rho
    rest = base * (1.0 - 1.5 * (u[0] * u[0] + u[1] * u[1] + u[2] * u[2]))
    out = [None] * 27
    for i in range(13):
        j = 26 - i
        w = WEIGHTS[i]
        cu = dot_c(DIRS[j], u)
        bc = base * cu
        even = w * (rest + 4.5 * (bc * cu))
        odd = (3.0 * w) * bc
        out[j] = own * f[j] + solid * f[i] + (even + odd)
        out[i] = own * f[i] + solid * f[j] + (even - odd)
    out[13] = (own + solid) * f[13] + WEIGHTS[13] * rest
    return out


def pull_back(p, solid, u, f=None, rho=None):
    w0 = WEIGHTS[13] * p[13]
    w1 = [None] * 3
    w2 = {}
    add = lambda x, y: y if x is None else x + y
    by_class = {}
    for i in range(13):
        j = 26 - i
        plus, minus = WEIGHTS[i] * (p[j] + p[i]), WEIGHTS[i] * (p[j] - p[i])
        w0 = w0 + plus
        c = DIRS[j]
        for k in range(3):
            if c[k]:
                w1[k] = add(w1[k], minus if c[k] > 0 else -minus)
            for m in range(k, 3):
                cc = c[k] * c[m]
                if cc:
                    w2[(k, m)] = add(w2.get((k, m)), plus if cc > 0 else -plus)
    at = lambda k, m: w2[(min(k, m), max(k, m))]
    w2u = [at(k, 0) * u[0] + at(k, 1) * u[1] + at(k, 2) * u[2] for k in range(3)]
    uwu = u[0] * w2u[0] + u[1] * w2u[1] + u[2] * w2u[2]
    uu = u[0] * u[0] + u[1] * u[1] + u[2] * u[2]
    fluid = 1.0 - solid
    own = (1.0 - OMEGA) * fluid
    gain = OMEGA * fluid
    g_rho = gain * (w0 * (1.0 + 1.5 * uu) - 4.5 * uwu)
    g_mom = [gain * (3.0 * w1[k] + 9.0 * w2u[k] - 3.0 * (u[k] * w0)) for k in range(3)]
    out = [None] * 27
    for i in range(13):
        j = 26 - i
        odd = dot_c(DIRS[j], g_mom)
        out[j] = own * p[j] + solid * p[i] + (g_rho + odd)
        out[i] = own * p[i] + solid * p[j] + (g_rho - odd)
    out[13] = (own + solid) * p[13] + g_rho
    if f is None:
        return out, None
    blame = OMEGA * (p[13] * f[13])
    for i in range(13):
        j = 26 - i
        blame = blame + (p[i] * (f[j] - (1.0 - OMEGA) * f[i]) + p[j] * (f[i] - (1.0 - OMEGA) * f[j]))
    w1u = w1[0] * u[0] + w1[1] * u[1] + w1[2] * u[2]
    blame = blame - (OMEGA * rho) * (w0 * (1.0 - 1.5 * uu) + 3.0 * w1u + 4.5 * uwu)
    return out, blame


def stream_main(own, yh, out_own, out_yh, orient, gz, low, high, put):
    lane, sub = lanes(), subs()
    floor = (lane == 0) & (gz == 0)
    roof = (lane == 127) & (gz == 1)

    def body(x, carry):
        for a in (-1, 0, 1):
            for b in (-1, 0, 1):
                xs = x - orient * a
                bp = orient * b
                both = out_yh is not None
                need = both or bp != 0
                into = 9 * (a + 1) + 3 * (b + 1) + 1 + orient * (2 * gz - 1)
                shift = 127 - 2 * gz - 4 * xs
                ins_own = roll_l(own[into, MINI, :], shift)
                ins_yh = roll_l(yh[into, MINI, :], shift) if need else None
                for d in (-1, 0, 1):
                    i = 9 * (a + 1) + 3 * (b + 1) + d + 1
                    dp = orient * d

                    def shifted(ref, ins):
                        t0, t1 = ref[i, tile(2 * xs), :], ref[i, tile(2 * xs + 1), :]
                        if dp == 1:
                            return (jnp.where(lane == 0, ins, roll_l(t0, 1)), roll_l(jnp.where(lane == 127, t0, t1), 1))
                        if dp == -1:
                            return (roll_l(jnp.where(lane == 0, t1, t0), 127), jnp.where(lane == 127, ins, roll_l(t1, 127)))
                        return t0, t1

                    mine = shifted(own, ins_own)
                    halo = shifted(yh, ins_yh) if need else (None, None)
                    for half in (0, 1):
                        vo, vy = mine[half], halo[half]
                        ny = vy
                        if bp == 1:
                            no = roll_s(jnp.where(sub == 7, vy, vo), 1)
                            if both:
                                ny = roll_s(jnp.where(sub == 7, vo, vy), 1)
                        elif bp == -1:
                            no = roll_s(jnp.where(sub == 0, vy, vo), 7)
                            if both:
                                ny = roll_s(jnp.where(sub == 0, vo, vy), 7)
                        else:
                            no = vo
                        wall = floor if (dp == 1 and half == 0) else roof if (dp == -1 and half == 1) else None
                        here = tile(2 * x + half)
                        if wall is not None:
                            no = jnp.where(wall, own[26 - i, here, :], no)
                            if both:
                                ny = jnp.where(wall, yh[26 - i, here, :], ny)
                        put(out_own, i, x, half, no)
                        if both:
                            out_yh[i, here, :] = ny
        return carry

    lax.fori_loop(low, high, body, 0)


def put_tile(ref, i, x, half, value):
    ref[i, tile(2 * x + half), :] = value


def stream_mini(own, yh, out_own, out_yh, orient, gz):
    lane, sub = lanes(), subs()
    slot = lax.rem(lane, 4)
    edge = 1 - gz
    for a in (-1, 0, 1):
        for b in (-1, 0, 1):
            bp = orient * b
            both = out_yh is not None
            need = both or bp != 0
            outof = 9 * (a + 1) + 3 * (b + 1) + 1 + orient * (1 - 2 * gz)

            def rim(ref):
                acc = jnp.zeros((8, 128), F32)
                for xe in range(8):
                    src = ref[outof, tile(2 * xe + edge), :]
                    acc = jnp.where(lane == 4 * xe + 3 * gz, roll_l(src, 4 * xe + 1 + 2 * gz), acc)
                return acc

            rim_own = rim(own)
            rim_yh = rim(yh) if need else None
            for d in (-1, 0, 1):
                i = 9 * (a + 1) + 3 * (b + 1) + d + 1
                dp = orient * d
                ap = orient * a

                def shifted(ref, edge_values):
                    v = ref[i, MINI, :]
                    if dp == 1:
                        v = jnp.where(slot == 0, edge_values, roll_l(v, 1))
                    if dp == -1:
                        v = jnp.where(slot == 3, edge_values, roll_l(v, 127))
                    if ap:
                        v = roll_l(v, (4 * ap) % 128)
                    return v

                vo = shifted(own, rim_own)
                vy = shifted(yh, rim_yh) if need else None
                ny = vy
                if bp == 1:
                    no = roll_s(jnp.where(sub == 7, vy, vo), 1)
                    if both:
                        ny = roll_s(jnp.where(sub == 7, vo, vy), 1)
                elif bp == -1:
                    no = roll_s(jnp.where(sub == 0, vy, vo), 7)
                    if both:
                        ny = roll_s(jnp.where(sub == 0, vo, vy), 7)
                else:
                    no = vo
                out_own[i, MINI, :] = no
                if both:
                    out_yh[i, MINI, :] = ny


def entries(e, orient, stride):
    others = [(r // 3) * 3 + r % 3 if stride == 9 else (r // 3) * 9 + r % 3 for r in range(9)]
    inward, outward = stride * (orient * e + 1), stride * (1 - orient * e)
    out = [(inward + c, 1, None, 0) for c in others]
    out += [(stride + c, 1, None, 0) for c in others]
    out += [(inward + c, 2, outward + c, orient * (r % 3 - 1)) for r, c in enumerate(others)]
    return out


def wall_masks(gz, by_half):
    lane, half = lanes(), lax.rem(subs(), 2)
    floor, roof = (lane == 0) & (gz == 0), (lane == 127) & (gz == 1)
    if by_half:
        return {-1: floor & (half == 0), 1: roof & (half == 1)}
    return {-1: floor, 1: roof}


def pack_x(msg, e, orient, gz, pops, adj=None, solid=None):
    near = 2 + 3 * ((e + 1) // 2)
    walls = wall_masks(gz, False)
    lane = lanes()
    items = [(pops, i, near if layer == 1 else near - e, st, dp) for i, layer, st, dp in entries(e, orient, 9)]
    if adj is not None:
        items += [(adj, 9 * (1 - e) + c, near, None, 0) for c in range(9)]
        items += [(solid, 0, near, None, 0)]
    strip = [jnp.zeros((8, 128), F32) for _ in range((len(items) + 31) // 32)]
    for k, (ref, i, plane, stash, dp) in enumerate(items):
        for half in (0, 1):
            v = ref[i, tile(2 * plane + half), :]
            if stash is not None and ((dp == -1 and half == 0) or (dp == 1 and half == 1)):
                v = jnp.where(walls[dp], ref[stash, tile(2 * near + half), :], v)
            msg[(2 * k + half) * 8 : (2 * k + half) * 8 + 8, :] = v
        s = 4 * (k % 32)
        moved = roll_l(ref[i, MINI, :], mod128(s - 4 * plane))
        strip[k // 32] = jnp.where((lane >= s) & (lane < s + 4), moved, strip[k // 32])
    for n, v in enumerate(strip):
        r = (2 * len(items) + n) * 8
        msg[r : r + 8, :] = v


def unpack_x(msg, s, orient, pops, adj=None, solid=None):
    near = 2 + 3 * ((s + 1) // 2) + s
    e = -s
    lane = lanes()
    plane_of = lax.div(lane, 4)
    outward = 9 * (1 - orient * e)
    items = [(pops, i, near if layer == 1 else near + s, st) for i, layer, st, _ in entries(e, orient, 9)]
    if adj is not None:
        items += [(adj, 9 * (1 - e) + c, near, None) for c in range(9)]
        items += [(solid, 0, near, None)]
    for k, (ref, i, plane, stash) in enumerate(items):
        for half in (0, 1):
            v = msg[(2 * k + half) * 8 : (2 * k + half) * 8 + 8, :]
            ref[i, tile(2 * plane + half), :] = v
            if stash is not None:
                ref[stash, tile(2 * near + half), :] = v
        r = (2 * len(items) + k // 32) * 8
        moved = roll_l(msg[r : r + 8, :], mod128(4 * plane - 4 * (k % 32)))
        ref[i, MINI, :] = jnp.where(plane_of == plane, moved, ref[i, MINI, :])


def pack_y(msg, e, orient, gz, pops, adj=None, solid=None):
    near = 7 * ((e + 1) // 2)
    walls = wall_masks(gz, True)
    items = [(pops, i, near if layer == 1 else near - e, st, dp) for i, layer, st, dp in entries(e, orient, 3)]
    if adj is not None:
        items += [(adj, 3 * (1 - e) + c, near, None, 0) for c in Y_OTHERS]
        items += [(solid, 0, near, None, 0)]
    for k, (ref, i, row, stash, dp) in enumerate(items):
        for part in (0, 1):
            v = ref[i, pl.ds(64 * part + row, 8, stride=8), :]
            if dp:
                v = jnp.where(walls[dp], ref[stash, pl.ds(64 * part + near, 8, stride=8), :], v)
            msg[(2 * k + part) * 8 : (2 * k + part) * 8 + 8, :] = v
        msg[16 * len(items) + k : 16 * len(items) + k + 1, :] = ref[i, pl.ds(128 + row, 1), :]


Y_OTHERS = [(r // 3) * 9 + r % 3 for r in range(9)]


def unpack_y(msg, s, orient, pops, adj=None, solid=None):
    near = 7 * ((1 - s) // 2)
    e = -s
    items = [(pops, i, near if layer == 1 else near + s, st) for i, layer, st, _ in entries(e, orient, 3)]
    if adj is not None:
        items += [(adj, 3 * (1 - e) + c, near, None) for c in Y_OTHERS]
        items += [(solid, 0, near, None)]
    for k, (ref, i, row, stash) in enumerate(items):
        for part in (0, 1):
            v = msg[(2 * k + part) * 8 : (2 * k + part) * 8 + 8, :]
            ref[i, pl.ds(64 * part + row, 8, stride=8), :] = v
            if stash is not None:
                ref[stash, pl.ds(64 * part + near, 8, stride=8), :] = v
        ref[i, pl.ds(128 + row, 1), :] = msg[16 * len(items) + k : 16 * len(items) + k + 1, :]


def solid_of(blockage, mask):
    m = mask.astype(F32)
    return blockage * (1.0 - m) + m


def cut_kernel(pops_hbm, block_hbm, mask_hbm, cot_hbm, msg, pops, block, mask, cot, sems):
    gz = lax.axis_index("gz")
    lane = lanes()
    z = pl.ds(pl.multiple_of(128 * (1 - gz), 128), 128)
    copies = []
    for n, (src, dst) in enumerate(((pops_hbm, pops), (cot_hbm, cot))):
        copies.append(pltpu.make_async_copy(src.at[:, :, :, z], dst, sems.at[n]))
    for n, (src, dst) in enumerate(((block_hbm, block), (mask_hbm, mask))):
        copies.append(pltpu.make_async_copy(src.at[:, :, z], dst, sems.at[n + 2]))
    for copy in copies:
        copy.start()
    for copy in copies:
        copy.wait()
    for n in range(7):
        acc = jnp.zeros((8, 128), F32)
        for j in range(8):
            slot = 8 * n + j
            if slot > 54:
                break
            for x in range(4):
                if slot == 54:
                    edge = solid_of(block[x], mask[x])
                else:
                    ref, i = (pops, slot) if slot < 27 else (cot, slot - 27)
                    edge = ref[i, x]
                at = 16 * j + 4 * x
                moved = roll_l(edge, mod128(at + 4 - 4 * gz))
                acc = jnp.where((lane >= at) & (lane < at + 4), moved, acc)
        msg[8 * n : 8 * n + 8, :] = acc


def first_kernel(pops, block, mask, cot, cut, tx, ax, sx, msg0, msg1):
    gz = lax.axis_index("gz")

    def body(x, carry):
        for half in (0, 1):
            z = pl.ds(128 * half, 128)
            here = tile(2 * (x + 2) + half)
            s = solid_of(block[x, :, z], mask[x, :, z])
            sx[0, here, :] = s
            f = [pops[i, x, :, z] for i in range(27)]
            rho, u = moments(f)
            out = collide(f, s, rho, u)
            for i in range(27):
                tx[i, here, :] = out[i]
                ax[i, here, :] = cot[i, x, :, z]
        return carry

    lax.fori_loop(0, 4, body, 0)

    def slot(n):
        return roll_l(cut[8 * (n // 8) : 8 * (n // 8) + 8, :], (8 - 16 * (n % 8)) % 128)

    s = slot(54)
    sx[0, MINI, :] = s
    f = [slot(i) for i in range(27)]
    rho, u = moments(f)
    out = collide(f, s, rho, u)
    for i in range(27):
        tx[i, MINI, :] = out[i]
        ax[i, MINI, :] = slot(27 + i)
    for msg, e in zip((msg0, msg1), sides("gx")):
        pack_x(msg, e, 1, gz, tx, ax, sx)


def carry_over(pairs):
    def body(k, carry):
        here = tile(jnp.where(k == 8, 16, k + 4))
        for src, dst in pairs:
            for i in range(src.shape[0]):
                dst[i, here, :] = src[i, here, :]
        return carry

    lax.fori_loop(0, 9, body, 0)


def span_kernel(tx_in, ax_in, sx_in, got0, got1, tx, ax, sx, msg0, msg1):
    gz = lax.axis_index("gz")
    carry_over(((tx_in, tx), (ax_in, ax), (sx_in, sx)))
    for msg, s in zip((got0, got1), sides("gx")):
        unpack_x(msg, s, 1, tx, ax, sx)
    for msg, e in zip((msg0, msg1), sides("gy")):
        pack_y(msg, e, 1, gz, tx, ax, sx)


def span_kernel_2(tx_in, got0, got1, tx, msg0, msg1):
    gz = lax.axis_index("gz")
    carry_over(((tx_in, tx),))
    for msg, s in zip((got0, got1), sides("gx")):
        unpack_x(msg, s, -1, tx)
    for msg, e in zip((msg0, msg1), sides("gy")):
        pack_y(msg, e, -1, gz, tx)


def middle_kernel(tx, ax, sx, got0, got1, a2, f1, u_own, u_yh, sy, q2, msg0, msg1, ty, ay, f2, f_yh, c_own, c_yh, p_own):
    gz = lax.axis_index("gz")
    for msg, s in zip((got0, got1), sides("gy")):
        unpack_y(msg, s, 1, ty, ay, sy)
    stream_main(tx, ty, f1, f_yh, 1, gz, 1, 7, put_tile)
    stream_mini(tx, ty, f1, f_yh, 1, gz)

    def again(k, carry):
        n = jnp.where(k == 12, 16, k + 2)
        here = tile(n)
        for src, sol, dst, us in ((f1, sx, c_own, u_own), (f_yh, sy, c_yh, u_yh)):
            f = [src[i, here, :] for i in range(27)]
            rho, u = moments(f)
            us[0, here, :] = rho
            for c in range(3):
                us[c + 1, here, :] = u[c]
            out = collide(f, sol[0, here, :], rho, u)
            for i in range(27):
                dst[i, here, :] = out[i]
        return carry

    lax.fori_loop(0, 13, again, 0)

    stream_main(c_own, c_yh, f2, None, 1, gz, 2, 6, put_tile)
    stream_mini(c_own, c_yh, f2, None, 1, gz)
    stream_main(ax, ay, p_own, None, -1, gz, 2, 6, put_tile)
    stream_mini(ax, ay, p_own, None, -1, gz)

    def back(k, carry):
        n = jnp.where(k == 8, 16, k + 4)
        here = tile(n)
        f = [f2[i, here, :] for i in range(27)]
        p = [p_own[i, here, :] for i in range(27)]
        rho, u = moments(f)
        out, blame = pull_back(p, sx[0, here, :], u, f, rho)
        for i in range(27):
            a2[i, here, :] = out[i]
        q2[tile(k), :] = blame
        return carry

    lax.fori_loop(0, 9, back, 0)
    for msg, e in zip((msg0, msg1), sides("gx")):
        pack_x(msg, e, -1, gz, a2)


def last_kernel(a2, pops, block, mask, f1, u_own, u_yh, sx, sy, q2, got0, got1, adjoint, grad, ty, p_own, p_yh, c_own, c_yh, q1):
    gz = lax.axis_index("gz")
    for msg, s in zip((got0, got1), sides("gy")):
        unpack_y(msg, s, -1, ty)
    stream_main(a2, ty, p_own, p_yh, -1, gz, 1, 7, put_tile)
    stream_mini(a2, ty, p_own, p_yh, -1, gz)

    def again(k, carry):
        n = jnp.where(k == 12, 16, k + 2)
        here = tile(n)
        for src, sol, dst, us in ((p_own, sx, c_own, u_own), (p_yh, sy, c_yh, u_yh)):
            p = [src[i, here, :] for i in range(27)]
            u = [us[c, here, :] for c in (1, 2, 3)]
            f = None if src is p_yh else [f1[i, here, :] for i in range(27)]
            out, blame = pull_back(p, sol[0, here, :], u, f, us[0, here, :])
            for i in range(27):
                dst[i, here, :] = out[i]
            if f is not None:
                q1[here, :] = blame
        return carry

    lax.fori_loop(0, 13, again, 0)
    stream_main(c_own, c_yh, p_own, None, -1, gz, 2, 6, put_tile)

    def back(x, carry):
        for half in (0, 1):
            z = pl.ds(128 * half, 128)
            here = tile(2 * x + 4 + half)
            f = [pops[i, x, :, z] for i in range(27)]
            rho, u = moments(f)
            out, blame = pull_back([p_own[i, here, :] for i in range(27)], sx[0, here, :], u, f, rho)
            for i in range(27):
                adjoint[i, x, :, z] = out[i]
            grad[x, :, z] = (1.0 - mask[x, :, z].astype(F32)) * (q1[here, :] + q2[tile(2 * x + half), :] + blame)
        return carry

    lax.fori_loop(0, 4, back, 0)


def call(kernel, outs, scratch=(), name=None, mib=8, in_specs=None):
    return pl.pallas_call(
        kernel,
        out_shape=[jax.ShapeDtypeStruct(s, F32) for s in outs],
        scratch_shapes=[pltpu.VMEM(s, F32) if isinstance(s, tuple) else s for s in scratch],
        **({} if in_specs is None else {"in_specs": in_specs}),
        compiler_params=pltpu.CompilerParams(vmem_limit_bytes=mib * 1024 * 1024),
        name=name,
    )


def swap(x, axis, odd):
    n = lax.axis_size(axis)
    pairs = [(i, (i ^ 1) if not odd else ((i + 1) % n if i % 2 else (i - 1) % n)) for i in range(n)]
    return lax.ppermute(x, axis, pairs)


BIG = (27, ROWS, 128)
ONE = (1, ROWS, 128)
X1 = ((2 * 37 + 2) * 8, 128)
Y1 = (37 * 16 + 40, 128)
X2 = ((2 * 27 + 1) * 8, 128)
Y2 = (27 * 16 + 32, 128)


def body(populations, blockage, solid_mask, cotangent):
    halves = [pltpu.VMEM((27, 4, 8, 128), F32), pltpu.VMEM((4, 8, 128), F32), pltpu.VMEM((4, 8, 128), jnp.int32), pltpu.VMEM((27, 4, 8, 128), F32)]
    anywhere = [pl.BlockSpec(memory_space=pltpu.HBM)] * 4
    (cut,) = call(cut_kernel, [(56, 128)], scratch=halves + [pltpu.SemaphoreType.DMA((4,))], name="cut", mib=60, in_specs=anywhere)(populations, blockage, solid_mask, cotangent)
    cut = lax.ppermute(cut, "gz", [(0, 1), (1, 0)])
    tx, ax, sx, m0, m1 = call(first_kernel, [BIG, BIG, ONE, X1, X1], name="first")(populations, blockage, solid_mask, cotangent, cut)
    m0, m1 = swap(m0, "gx", False), swap(m1, "gx", True)
    tx, ax, sx, m0, m1 = call(span_kernel, [BIG, BIG, ONE, Y1, Y1], name="span")(tx, ax, sx, m0, m1)
    m0, m1 = swap(m0, "gy", False), swap(m1, "gy", True)
    a2, f1, u_own, u_yh, sy, q2, m0, m1 = call(
        middle_kernel,
        [BIG, BIG, (4, ROWS, 128), (4, ROWS, 128), ONE, (72, 128), X2, X2],
        scratch=[BIG] * 7,
        name="middle",
        mib=24,
    )(tx, ax, sx, m0, m1)
    m0, m1 = swap(m0, "gx", False), swap(m1, "gx", True)
    a2, m0, m1 = call(span_kernel_2, [BIG, Y2, Y2], name="span2")(a2, m0, m1)
    m0, m1 = swap(m0, "gy", False), swap(m1, "gy", True)
    adjoint, grad = call(last_kernel, [(27, 4, 8, 256), (4, 8, 256)], scratch=[BIG] * 5 + [(ROWS, 128)], name="last", mib=20)(
        a2, populations, blockage, solid_mask, f1, u_own, u_yh, sx, sy, q2, m0, m1
    )
    return adjoint, grad


def solution(mesh):
    placed = (P(None, "gx", "gy", "gz"), P("gx", "gy", "gz"), P("gx", "gy", "gz"), P(None, "gx", "gy", "gz"))
    return jax.shard_map(
        body, mesh=mesh, in_specs=placed, out_specs=(P(None, "gx", "gy", "gz"), P("gx", "gy", "gz")), check_vma=False
    )
```

```python
import functools
import jax
import jax.numpy as jnp
from jax import lax
from jax.experimental import pallas as pl
from jax.experimental.pallas import tpu as pltpu
from jax.sharding import PartitionSpec as P

DIRS = [(a, b, d) for a in (-1, 0, 1) for b in (-1, 0, 1) for d in (-1, 0, 1)]
WEIGHTS = [(8.0 / 27.0, 2.0 / 27.0, 1.0 / 54.0, 1.0 / 216.0)[abs(a) + abs(b) + abs(d)] for a, b, d in DIRS]
OMEGA = 1.25
NT = 17
ROWS = NT * 8
MINI = pl.ds(128, 8)
F32 = jnp.float32


def tile(n):
    return pl.ds(n * 8, 8) if isinstance(n, int) else pl.ds(pl.multiple_of(n * 8, 8), 8)


def lanes():
    return lax.broadcasted_iota(jnp.int32, (8, 128), 1)


def subs():
    return lax.broadcasted_iota(jnp.int32, (8, 128), 0)


def roll_l(v, k):
    return pltpu.roll(v, k, 1)


def roll_s(v, k):
    return pltpu.roll(v, k, 0)


def mod128(k):
    return lax.rem(k + 256, 128)


def sides(axis):
    parity = lax.rem(lax.axis_index(axis), 2)
    return (1 - 2 * parity, 2 * parity - 1)


def moments(f):
    rho = f[13]
    mom = [None, None, None]
    for i in range(13):
        plus, minus = f[i] + f[26 - i], f[26 - i] - f[i]
        rho = rho + plus
        for k in range(3):
            c = DIRS[26 - i][k]
            if c:
                term = minus if c > 0 else -minus
                mom[k] = term if mom[k] is None else (mom[k] + minus if c > 0 else mom[k] - minus)
    inv = 1.0 / rho
    return rho, [m * inv for m in mom]


def dot_c(vec, comps):
    out = None
    for c, v in zip(vec, comps):
        if c:
            if out is None:
                out = v if c > 0 else -v
            else:
                out = out + v if c > 0 else out - v
    return out


def collide(f, solid, rho, u):
    fluid = 1.0 - solid
    own = (1.0 - OMEGA) * fluid
    base = OMEGA * fluid * rho
    rest = base * (1.0 - 1.5 * (u[0] * u[0] + u[1] * u[1] + u[2] * u[2]))
    out = [None] * 27
    for i in range(13):
        j = 26 - i
        w = WEIGHTS[i]
        cu = dot_c(DIRS[j], u)
        bc = base * cu
        even = w * (rest + 4.5 * (bc * cu))
        odd = (3.0 * w) * bc
        out[j] = own * f[j] + solid * f[i] + (even + odd)
        out[i] = own * f[i] + solid * f[j] + (even - odd)
    out[13] = (own + solid) * f[13] + WEIGHTS[13] * rest
    return out


def pull_back(p, solid, u, f=None, rho=None):
    w0 = WEIGHTS[13] * p[13]
    w1 = [None] * 3
    w2 = {}
    add = lambda x, y: y if x is None else x + y
    by_class = {}
    for i in range(13):
        j = 26 - i
        plus, minus = WEIGHTS[i] * (p[j] + p[i]), WEIGHTS[i] * (p[j] - p[i])
        w0 = w0 + plus
        c = DIRS[j]
        for k in range(3):
            if c[k]:
                w1[k] = add(w1[k], minus if c[k] > 0 else -minus)
            for m in range(k, 3):
                cc = c[k] * c[m]
                if cc:
                    w2[(k, m)] = add(w2.get((k, m)), plus if cc > 0 else -plus)
    at = lambda k, m: w2[(min(k, m), max(k, m))]
    w2u = [at(k, 0) * u[0] + at(k, 1) * u[1] + at(k, 2) * u[2] for k in range(3)]
    uwu = u[0] * w2u[0] + u[1] * w2u[1] + u[2] * w2u[2]
    uu = u[0] * u[0] + u[1] * u[1] + u[2] * u[2]
    fluid = 1.0 - solid
    own = (1.0 - OMEGA) * fluid
    gain = OMEGA * fluid
    g_rho = gain * (w0 * (1.0 + 1.5 * uu) - 4.5 * uwu)
    g_mom = [gain * (3.0 * w1[k] + 9.0 * w2u[k] - 3.0 * (u[k] * w0)) for k in range(3)]
    out = [None] * 27
    for i in range(13):
        j = 26 - i
        odd = dot_c(DIRS[j], g_mom)
        out[j] = own * p[j] + solid * p[i] + (g_rho + odd)
        out[i] = own * p[i] + solid * p[j] + (g_rho - odd)
    out[13] = (own + solid) * p[13] + g_rho
    if f is None:
        return out, None
    blame = OMEGA * (p[13] * f[13])
    for i in range(13):
        j = 26 - i
        blame = blame + (p[i] * (f[j] - (1.0 - OMEGA) * f[i]) + p[j] * (f[i] - (1.0 - OMEGA) * f[j]))
    w1u = w1[0] * u[0] + w1[1] * u[1] + w1[2] * u[2]
    blame = blame - (OMEGA * rho) * (w0 * (1.0 - 1.5 * uu) + 3.0 * w1u + 4.5 * uwu)
    return out, blame


STRIP_ROW = (7, 6, 0, 1)


def sources(bp, ext):
    if bp == 0:
        return [(0, None, 0, None), (2, None, 2, None)] if ext else []
    if bp == 1:
        return [(0, None, None, 0)] + ([(1, None, 0, None), (None, 7, 2, None)] if ext else [])
    return [(2, None, None, 7)] + ([(3, None, 2, None), (None, 0, 0, None)] if ext else [])


def shift_z(t0, t1, dp, ins, lane):
    if dp == 1:
        return jnp.where(lane == 0, ins, roll_l(t0, 1)), roll_l(jnp.where(lane == 127, t0, t1), 1)
    if dp == -1:
        return roll_l(jnp.where(lane == 0, t1, t0), 127), jnp.where(lane == 127, ins, roll_l(t1, 127))
    return t0, t1


def direction(a, b, d):
    return 9 * (a + 1) + 3 * (b + 1) + d + 1


def stream(own, rows, strip_rows, out, out_rows, out_strip_rows, orient, gz, low, high):
    lane, sub = lanes(), subs()
    ext = out_rows is not None

    def body(x, carry):
        for a in (-1, 0, 1):
            for b in (-1, 0, 1):
                xs = x - orient * a
                bp = orient * b
                into = direction(a, b, 0) + orient * (2 * gz - 1)
                ins = roll_l(own[into, MINI, :], 127 - 2 * gz - 4 * xs)
                for d in (-1, 0, 1):
                    i = direction(a, b, d)
                    pair = shift_z(own[i, tile(2 * xs), :], own[i, tile(2 * xs + 1), :], orient * d, ins, lane)
                    for half in (0, 1):
                        v = pair[half]
                        if bp:
                            v = roll_s(v, bp % 8)
                        out[i, tile(2 * x + half), :] = v
        return carry

    lax.fori_loop(low, high, body, 0)

    for a in (-1, 0, 1):
        for b in (-1, 0, 1):
            bp, ap = orient * b, orient * a
            into = direction(a, b, 0) + orient * (2 * gz - 1)
            for k_in, row_in, k_out, row_out in sources(bp, ext):
                if k_in is None:
                    line = own[into, pl.ds(128 + row_in, 1), :]
                else:
                    line = strip_rows[into, pl.ds(STRIP_ROW[k_in], 1), :]
                ins = jnp.sum(jnp.where(lane == 4 * sub + 3 * gz, jnp.broadcast_to(line, (8, 128)), 0.0), axis=1, keepdims=True)
                for d in (-1, 0, 1):
                    i = direction(a, b, d)
                    if k_in is None:
                        t0, t1 = (own[i, pl.ds(8 * half + row_in, 8, stride=16), :] for half in (0, 1))
                    else:
                        t0, t1 = rows[i, k_in, 0:8, :], rows[i, k_in, 8:16, :]
                    pair = shift_z(t0, t1, orient * d, ins, lane)
                    for half in (0, 1):
                        v = pair[half]
                        if ap:
                            v = roll_s(v, ap % 8)
                        if k_out is None:
                            out[i, pl.ds(8 * half + row_out, 8, stride=16), :] = v
                        else:
                            out_rows[i, k_out, 8 * half : 8 * half + 8, :] = v

    wall = lane == 127 * gz
    for a in (-1, 0, 1):
        for b in (-1, 0, 1):
            i = direction(a, b, 0) + orient * (1 - 2 * gz)
            for x in range(low, high):
                here = tile(2 * x + gz)
                out[i, here, :] = jnp.where(wall, own[26 - i, here, :], out[i, here, :])
            if ext:
                for k in (0, 2):
                    here = tile(gz)
                    out_rows[i, k, here, :] = jnp.where(wall, rows[26 - i, k, here, :], out_rows[i, k, here, :])

    slot = lax.rem(lane, 4)
    edge = 1 - gz
    for a in (-1, 0, 1):
        for b in (-1, 0, 1):
            bp, ap = orient * b, orient * a
            outof = direction(a, b, 0) + orient * (1 - 2 * gz)
            need = [k for k, _, _, _ in sources(bp, ext) if k is not None]
            rim = jnp.zeros((8, 128), F32)
            for xe in range(8):
                src = own[outof, tile(2 * xe + edge), :]
                rim = jnp.where(lane == 4 * xe + 3 * gz, roll_l(src, 4 * xe + 1 + 2 * gz), rim)
            rim_rows = jnp.zeros((8, 128), F32)
            for k in need:
                src = pltpu.roll(roll_l(rows[outof, k, tile(edge), :], 1 + 2 * gz), 0, 1, stride=4, stride_axis=0)
                line = jnp.sum(jnp.where(lane == 4 * sub + 3 * gz, src, 0.0), axis=0, keepdims=True)
                rim_rows = jnp.where(sub == STRIP_ROW[k], line, rim_rows)
            for d in (-1, 0, 1):
                i = direction(a, b, d)
                dp = orient * d

                def shifted(v, edge_values):
                    if dp == 1:
                        v = jnp.where(slot == 0, edge_values, roll_l(v, 1))
                    if dp == -1:
                        v = jnp.where(slot == 3, edge_values, roll_l(v, 127))
                    return roll_l(v, (4 * ap) % 128) if ap else v

                vo = shifted(own[i, MINI, :], rim)
                vy = shifted(strip_rows[i], rim_rows) if need else None
                if bp == 0:
                    out[i, MINI, :] = vo
                    if ext:
                        out_strip_rows[i] = vy
                else:
                    last = 7 if bp == 1 else 0
                    out[i, MINI, :] = roll_s(jnp.where(sub == last, vy, vo), bp % 8)
                    if ext:
                        out_strip_rows[i] = roll_s(jnp.where(sub == last, vo, vy), bp % 8)


def entries(e, orient, stride, extra):
    others = [(r // 3, r % 3) for r in range(9)]
    number = lambda across, d: 3 * across + d if stride == 9 else 9 * across + d
    inward, outward = stride * (orient * e + 1), stride * (1 - orient * e)
    out = [(0, inward + number(c, d), 1, None, orient * (c - 1), 0) for c, d in others]
    out += [(0, stride + number(c, d), 1, None, orient * (c - 1), 0) for c, d in others]
    out += [(0, inward + number(c, d), 2, outward + number(c, d) if d != 1 else None, orient * (c - 1), orient * (d - 1)) for c, d in others]
    if extra:
        out += [(1, stride * (1 - e) + number(c, d), 1, None, 1 - c, 0) for c, d in others]
        out += [(2, 0, 1, None, 0, 0)]
    return out


def row_kinds(which, bp):
    if which == 1:
        return {1: (0,), 0: (), -1: (2,)}[bp]
    return {1: (0, 1), 0: (0, 2), -1: (2, 3)}[bp]


def near_plane(e):
    return 2 + 3 * ((e + 1) // 2)


def pack_faces(msg, e, orient, gz, arrays):
    near = near_plane(e)
    walls = {-1: (lanes() == 0) & (gz == 0), 1: (lanes() == 127) & (gz == 1)}
    for n, (which, i, layer, stash, _, dp) in enumerate(entries(e, orient, 9, len(arrays) > 1)):
        ref, plane = arrays[which], near if layer == 1 else near - e
        for half in (0, 1):
            v = ref[i, tile(2 * plane + half), :]
            if stash is not None and half == (dp + 1) // 2:
                v = jnp.where(walls[dp], ref[stash, tile(2 * near + half), :], v)
            msg[(2 * n + half) * 8 : (2 * n + half) * 8 + 8, :] = v


def unpack_faces(msg, s, orient, arrays):
    near = near_plane(s) + s
    for n, (which, i, layer, stash, _, dp) in enumerate(entries(-s, orient, 9, len(arrays) > 1)):
        ref, plane = arrays[which], near if layer == 1 else near + s
        for half in (0, 1):
            v = msg[(2 * n + half) * 8 : (2 * n + half) * 8 + 8, :]
            ref[i, tile(2 * plane + half), :] = v
            if stash is not None and half == (dp + 1) // 2:
                ref[stash, tile(2 * near + half), :] = v


def pack_sides(msg, e, orient, gz, arrays, strips):
    near = 7 * ((e + 1) // 2)
    lane = lax.broadcasted_iota(jnp.int32, (4, 128), 1)
    walls = {-1: (lane == 0) & (gz == 0), 1: (lane == 127) & (gz == 1)}
    items = entries(e, orient, 3, len(arrays) > 1)
    for n, (which, i, layer, stash, _, dp) in enumerate(items):
        ref, row = arrays[which], near if layer == 1 else near - e
        for half in (0, 1):
            v = ref[i, pl.ds(32 + 8 * half + row, 4, stride=16), :]
            if stash is not None and half == (dp + 1) // 2:
                v = jnp.where(walls[dp], ref[stash, pl.ds(32 + 8 * half + near, 4, stride=16), :], v)
            msg[8 * n + 4 * half : 8 * n + 4 * half + 4, :] = v
        msg[8 * len(items) + n : 8 * len(items) + n + 1, :] = strips[which][i, pl.ds(row, 1), :]


def unpack_sides(msg, s, orient, rows, strip_rows):
    k = s + 1
    near = 7 * ((1 - s) // 2)
    items = entries(-s, orient, 3, len(rows) > 1)
    for n, (which, i, layer, _, _, _) in enumerate(items):
        for half in (0, 1):
            rows[which][i, k + layer - 1, 8 * half + 2 : 8 * half + 6, :] = msg[8 * n + 4 * half : 8 * n + 4 * half + 4, :]
        row = near if layer == 1 else near + s
        strip_rows[which][i, pl.ds(row, 1), :] = msg[8 * len(items) + n : 8 * len(items) + n + 1, :]


def edge_rows(e, orient, extra):
    return 2 * sum(len(row_kinds(item[0], item[4])) for item in entries(e, orient, 9, extra))


def pack_edges(msg, e, orient, gz, rows, strips, strip_rows):
    near = near_plane(e)
    lane = lanes()
    lane2 = lax.broadcasted_iota(jnp.int32, (2, 128), 1)
    half2 = lax.broadcasted_iota(jnp.int32, (2, 128), 0)
    walls = {-1: (lane2 == 0) & (half2 == 0) & (gz == 0), 1: (lane2 == 127) & (half2 == 1) & (gz == 1)}
    items = entries(e, orient, 9, len(rows) > 1)
    at = 0
    tiles = (len(items) + 31) // 32
    packed = [[jnp.zeros((8, 128), F32) for _ in range(tiles)] for _ in range(2)]
    for n, (which, i, layer, stash, bp, dp) in enumerate(items):
        plane = near if layer == 1 else near - e
        for k in row_kinds(which, bp):
            v = rows[which][i, k, pl.ds(plane, 2, stride=8), :]
            if stash is not None:
                v = jnp.where(walls[dp], rows[which][stash, k, pl.ds(near, 2, stride=8), :], v)
            msg[at : at + 2, :] = v
            at += 2
        s = 4 * (n % 32)
        for kind, v in enumerate((strips[which][i], strip_rows[which][i])):
            moved = roll_l(v, mod128(s - 4 * plane))
            packed[kind][n // 32] = jnp.where((lane >= s) & (lane < s + 4), moved, packed[kind][n // 32])
    at = -(-at // 8) * 8
    for v in packed[0] + packed[1]:
        msg[at : at + 8, :] = v
        at += 8


def unpack_edges(msg, s, orient, rows, owns, strip_rows):
    near = near_plane(s) + s
    plane_of = lax.div(lanes(), 4)
    items = entries(-s, orient, 9, len(rows) > 1)
    at = 0
    base = -(-edge_rows(1, orient, len(rows) > 1) // 8) * 8
    tiles = (len(items) + 31) // 32
    for n, (which, i, layer, stash, bp, _) in enumerate(items):
        plane = near if layer == 1 else near + s
        for k in row_kinds(which, bp):
            v = msg[at : at + 2, :]
            at += 2
            rows[which][i, k, pl.ds(plane, 2, stride=8), :] = v
            if stash is not None:
                rows[which][stash, k, pl.ds(near, 2, stride=8), :] = v
        for kind in (0, 1):
            r = base + 8 * (tiles * kind + n // 32)
            moved = roll_l(msg[r : r + 8, :], mod128(4 * plane - 4 * (n % 32)))
            if kind:
                strip_rows[which][i] = jnp.where(plane_of == plane, moved, strip_rows[which][i])
            else:
                owns[which][i, MINI, :] = jnp.where(plane_of == plane, moved, owns[which][i, MINI, :])


def reflect_rows(rows, orient):
    for a in range(3):
        for d in (0, 2):
            for k, b in ((0, 1 + orient), (2, 1 - orient)):
                rows[9 * a + 3 * (2 - b) + d, k] = rows[9 * a + 3 * b + d, k + 1]


def solid_of(blockage, mask):
    m = mask.astype(F32)
    return blockage * (1.0 - m) + m


def cut_kernel(pops_hbm, block_hbm, mask_hbm, cot_hbm, msg, pops, block, mask, cot, sems):
    gz = lax.axis_index("gz")
    lane = lanes()
    z = pl.ds(pl.multiple_of(128 * (1 - gz), 128), 128)
    copies = []
    for n, (src, dst) in enumerate(((pops_hbm, pops), (cot_hbm, cot))):
        copies.append(pltpu.make_async_copy(src.at[:, :, :, z], dst, sems.at[n]))
    for n, (src, dst) in enumerate(((block_hbm, block), (mask_hbm, mask))):
        copies.append(pltpu.make_async_copy(src.at[:, :, z], dst, sems.at[n + 2]))
    for copy in copies:
        copy.start()
    for copy in copies:
        copy.wait()
    for n in range(7):
        acc = jnp.zeros((8, 128), F32)
        for j in range(8):
            slot = 8 * n + j
            if slot > 54:
                break
            for x in range(4):
                if slot == 54:
                    edge = solid_of(block[x], mask[x])
                else:
                    ref, i = (pops, slot) if slot < 27 else (cot, slot - 27)
                    edge = ref[i, x]
                at = 16 * j + 4 * x
                moved = roll_l(edge, mod128(at + 4 - 4 * gz))
                acc = jnp.where((lane >= at) & (lane < at + 4), moved, acc)
        msg[8 * n : 8 * n + 8, :] = acc


def first_kernel(pops, block, mask, cot, after, tx, ax, sx, msg0, msg1):
    gz = lax.axis_index("gz")

    def body(x, carry):
        for half in (0, 1):
            z = pl.ds(128 * half, 128)
            here = tile(2 * (x + 2) + half)
            s = solid_of(block[x, :, z], mask[x, :, z])
            sx[0, here, :] = s
            f = [pops[i, x, :, z] for i in range(27)]
            rho, u = moments(f)
            out = collide(f, s, rho, u)
            for i in range(27):
                tx[i, here, :] = out[i]
                ax[i, here, :] = cot[i, x, :, z]
        return carry

    lax.fori_loop(0, 4, body, 0)
    for msg, e in zip((msg0, msg1), sides("gx")):
        pack_faces(msg, e, 1, gz, (tx, ax, sx))


def strip_kernel(cut, tx, ax, sx, tm, am, sm, msg0, msg1):
    gz = lax.axis_index("gz")

    def slot(n):
        return roll_l(cut[8 * (n // 8) : 8 * (n // 8) + 8, :], (8 - 16 * (n % 8)) % 128)

    s = slot(54)
    sm[0] = s
    f = [slot(i) for i in range(27)]
    rho, u = moments(f)
    out = collide(f, s, rho, u)
    for i in range(27):
        tm[i] = out[i]
        am[i] = slot(27 + i)
    for msg, e in zip((msg0, msg1), sides("gy")):
        pack_sides(msg, e, 1, gz, (tx, ax, sx), (tm, am, sm))


def edge_kernel(tm, am, sm, got0, got1, msg0, msg1, tr, ar, sr, tmr, amr, smr):
    gz = lax.axis_index("gz")
    rows, strip_rows = (tr, ar, sr), (tmr, amr, smr)
    for msg, s in zip((got0, got1), sides("gy")):
        unpack_sides(msg, s, 1, rows, strip_rows)
    for msg, e in zip((msg0, msg1), sides("gx")):
        pack_edges(msg, e, 1, gz, rows, (tm, am, sm), strip_rows)


def edge_kernel_2(tm, got0, got1, msg0, msg1, tr, tmr):
    gz = lax.axis_index("gz")
    for msg, s in zip((got0, got1), sides("gy")):
        unpack_sides(msg, s, -1, (tr,), (tmr,))
    for msg, e in zip((msg0, msg1), sides("gx")):
        pack_edges(msg, e, -1, gz, (tr,), (tm,), (tmr,))


def gather_in(pairs, strips):
    def body(n, carry):
        for src, dst in pairs:
            for i in range(src.shape[0]):
                dst[i, tile(n), :] = src[i, tile(n), :]
        return carry

    lax.fori_loop(4, 12, body, 0)
    for (_, dst), strip in zip(pairs, strips):
        for i in range(strip.shape[0]):
            dst[i, MINI, :] = strip[i]


def receive(orient, owns, rows, strip_rows, by_y, faces, edges):
    for msg, s in zip(by_y, sides("gy")):
        unpack_sides(msg, s, orient, rows, strip_rows)
    for face, edge, s in zip(faces, edges, sides("gx")):
        unpack_faces(face, s, orient, owns)
        unpack_edges(edge, s, orient, rows, owns, strip_rows)
    reflect_rows(rows[0], orient)


def middle_kernel(
    tx, ax, sx, tm, am, sm, y0, y1, x0, x1, e0, e1,
    a2, a2m, f1, u_own, u_rows, u_strip, s_own, s_rows, s_strip, q2, ym0, ym1, xm0, xm1,
    t, a, tr, ar, tmr, amr, fr, fmr, c, cr, cmr, f2, p,
):
    gz = lax.axis_index("gz")
    gather_in(((tx, t), (ax, a), (sx, s_own)), (tm, am, sm))
    receive(1, (t, a, s_own), (tr, ar, s_rows), (tmr, amr, s_strip), (y0, y1), (x0, x1), (e0, e1))
    stream(t, tr, tmr, f1, fr, fmr, 1, gz, 1, 7)

    def collide_at(load, solid, store, store_u):
        f = [load(i) for i in range(27)]
        rho, u = moments(f)
        for n, v in enumerate([rho] + u):
            store_u(n, v)
        out = collide(f, solid, rho, u)
        for i in range(27):
            store(i, out[i])

    def again(k, carry):
        here = tile(jnp.where(k == 12, 16, k + 2))

        def put(i, v):
            c[i, here, :] = v

        def put_u(n, v):
            u_own[n, here, :] = v

        collide_at(lambda i: f1[i, here, :], s_own[0, here, :], put, put_u)
        return carry

    lax.fori_loop(0, 13, again, 0)

    def again_rows(k, carry):
        for half in (0, 1):
            here = tile(half)

            def put(i, v):
                cr[i, 2 * k, here, :] = v

            def put_u(n, v):
                u_rows[n, 2 * k, here, :] = v

            collide_at(lambda i: fr[i, 2 * k, here, :], s_rows[0, 2 * k, here, :], put, put_u)
        return carry

    lax.fori_loop(0, 2, again_rows, 0)

    def put_strip(i, v):
        cmr[i] = v

    def put_strip_u(n, v):
        u_strip[n] = v

    collide_at(lambda i: fmr[i], s_strip[0], put_strip, put_strip_u)
    stream(c, cr, cmr, f2, None, None, 1, gz, 2, 6)
    stream(a, ar, amr, p, None, None, -1, gz, 2, 6)

    def back(here):
        f = [f2[i, here, :] for i in range(27)]
        rho, u = moments(f)
        return pull_back([p[i, here, :] for i in range(27)], s_own[0, here, :], u, f, rho)

    def back_own(k, carry):
        here = tile(k + 4)
        out, blame = back(here)
        for i in range(27):
            a2[i, here, :] = out[i]
        q2[tile(k), :] = blame
        return carry

    lax.fori_loop(0, 8, back_own, 0)
    out, _ = back(MINI)
    for i in range(27):
        a2m[i] = out[i]
    for msg, e in zip((ym0, ym1), sides("gy")):
        pack_sides(msg, e, -1, gz, (a2,), (a2m,))
    for msg, e in zip((xm0, xm1), sides("gx")):
        pack_faces(msg, e, -1, gz, (a2,))


def last_kernel(
    a2, a2m, pops, mask, f1, u_own, u_rows, u_strip, s_own, s_rows, s_strip, q2, y0, y1, x0, x1, e0, e1,
    adjoint, grad,
    t, tr, tmr, p, pr, pmr, c, cr, cmr, q1,
):
    gz = lax.axis_index("gz")
    gather_in(((a2, t),), (a2m,))
    receive(-1, (t,), (tr,), (tmr,), (y0, y1), (x0, x1), (e0, e1))
    stream(t, tr, tmr, p, pr, pmr, -1, gz, 1, 7)

    def again(k, carry):
        here = tile(jnp.where(k == 12, 16, k + 2))
        u = [u_own[n, here, :] for n in (1, 2, 3)]
        out, blame = pull_back([p[i, here, :] for i in range(27)], s_own[0, here, :], u, [f1[i, here, :] for i in range(27)], u_own[0, here, :])
        for i in range(27):
            c[i, here, :] = out[i]
        q1[here, :] = blame
        return carry

    lax.fori_loop(0, 13, again, 0)

    def again_rows(k, carry):
        for half in (0, 1):
            here = tile(half)
            u = [u_rows[n, 2 * k, here, :] for n in (1, 2, 3)]
            out, _ = pull_back([pr[i, 2 * k, here, :] for i in range(27)], s_rows[0, 2 * k, here, :], u)
            for i in range(27):
                cr[i, 2 * k, here, :] = out[i]
        return carry

    lax.fori_loop(0, 2, again_rows, 0)
    out, _ = pull_back([pmr[i] for i in range(27)], s_strip[0], [u_strip[n] for n in (1, 2, 3)])
    for i in range(27):
        cmr[i] = out[i]
    stream(c, cr, cmr, p, None, None, -1, gz, 2, 6)

    def back(x, carry):
        for half in (0, 1):
            z = pl.ds(128 * half, 128)
            here = tile(2 * x + 4 + half)
            f = [pops[i, x, :, z] for i in range(27)]
            rho, u = moments(f)
            out, blame = pull_back([p[i, here, :] for i in range(27)], s_own[0, here, :], u, f, rho)
            for i in range(27):
                adjoint[i, x, :, z] = out[i]
            grad[x, :, z] = (1.0 - mask[x, :, z].astype(F32)) * (q1[here, :] + q2[tile(2 * x + half), :] + blame)
        return carry

    lax.fori_loop(0, 4, back, 0)


def call(kernel, outs, scratch=(), name=None, mib=8, in_specs=None):
    return pl.pallas_call(
        kernel,
        out_shape=[jax.ShapeDtypeStruct(s, F32) for s in outs],
        scratch_shapes=[pltpu.VMEM(s, F32) if isinstance(s, tuple) else s for s in scratch],
        **({} if in_specs is None else {"in_specs": in_specs}),
        compiler_params=pltpu.CompilerParams(vmem_limit_bytes=mib * 1024 * 1024),
        name=name,
    )


def swap(x, axis, odd):
    n = lax.axis_size(axis)
    pairs = [(i, (i ^ 1) if not odd else ((i + 1) % n if i % 2 else (i - 1) % n)) for i in range(n)]
    return lax.ppermute(x, axis, pairs)


BIG = (27, ROWS, 128)
ONE = (1, ROWS, 128)
STRIP = (27, 8, 128)
STRIP1 = (1, 8, 128)
HALO = (27, 4, 16, 128)
HALO1 = (1, 4, 16, 128)


def face_shape(n):
    return (16 * n, 128)


def side_shape(n):
    return (8 * n + -(-n // 8) * 8, 128)


def edge_shape(extra):
    n = 37 if extra else 27
    return (-(-edge_rows(1, 1, extra) // 8) * 8 + 16 * (-(-n // 32)), 128)


def swaps(pair, axis):
    return [swap(pair[0], axis, False), swap(pair[1], axis, True)]


def body(populations, blockage, solid_mask, cotangent):
    halves = [pltpu.VMEM((27, 4, 8, 128), F32), pltpu.VMEM((4, 8, 128), F32), pltpu.VMEM((4, 8, 128), jnp.int32), pltpu.VMEM((27, 4, 8, 128), F32)]
    anywhere = [pl.BlockSpec(memory_space=pltpu.HBM)] * 4
    (cut,) = call(cut_kernel, [(56, 128)], scratch=halves + [pltpu.SemaphoreType.DMA((4,))], name="cut", mib=60, in_specs=anywhere)(
        populations, blockage, solid_mask, cotangent
    )
    tx, ax, sx, *faces = call(first_kernel, [BIG, BIG, ONE, face_shape(37), face_shape(37)], name="first")(
        populations, blockage, solid_mask, cotangent, cut
    )
    cut = lax.ppermute(cut, "gz", [(0, 1), (1, 0)])
    tm, am, sm, *by_y = call(strip_kernel, [STRIP, STRIP, STRIP1, side_shape(37), side_shape(37)], name="strip")(cut, tx, ax, sx)
    by_y = swaps(by_y, "gy")
    faces, _ = lax.optimization_barrier((faces, tm))
    faces = swaps(faces, "gx")
    edges = call(
        edge_kernel, [edge_shape(True)] * 2, scratch=[HALO, HALO, HALO1, STRIP, STRIP, STRIP1], name="edge", mib=12
    )(tm, am, sm, *by_y)
    edges = swaps(edges, "gx")
    a2, a2m, f1, u_own, u_rows, u_strip, s_own, s_rows, s_strip, q2, *out = call(
        middle_kernel,
        [BIG, STRIP, BIG, (4, ROWS, 128), (4, 4, 16, 128), (4, 8, 128), ONE, HALO1, STRIP1, (64, 128)]
        + [side_shape(27)] * 2
        + [face_shape(27)] * 2,
        scratch=[BIG, BIG, HALO, HALO, STRIP, STRIP, HALO, STRIP, BIG, HALO, STRIP, BIG, BIG],
        name="middle",
        mib=24,
    )(tx, ax, sx, tm, am, sm, *by_y, *faces, *edges)
    by_y = swaps(out[:2], "gy")
    faces = swaps(out[2:], "gx")
    edges = call(edge_kernel_2, [edge_shape(False)] * 2, scratch=[HALO, STRIP], name="edge2", mib=8)(a2m, *by_y)
    edges = swaps(edges, "gx")
    adjoint, grad = call(
        last_kernel,
        [populations.shape, blockage.shape],
        scratch=[BIG, HALO, STRIP, BIG, HALO, STRIP, BIG, HALO, STRIP, (ROWS, 128)],
        name="last",
        mib=20,
    )(a2, a2m, populations, solid_mask, f1, u_own, u_rows, u_strip, s_own, s_rows, s_strip, q2, *by_y, *faces, *edges)
    return adjoint, grad


def solution(mesh):
    placed = (P(None, "gx", "gy", "gz"), P("gx", "gy", "gz"), P("gx", "gy", "gz"), P(None, "gx", "gy", "gz"))
    return jax.shard_map(
        body, mesh=mesh, in_specs=placed, out_specs=(P(None, "gx", "gy", "gz"), P("gx", "gy", "gz")), check_vma=False
    )
```

```python
import functools
import jax
import jax.numpy as jnp
from jax import lax
from jax.experimental import pallas as pl
from jax.experimental.pallas import tpu as pltpu
from jax.sharding import PartitionSpec as P

DIRS = [(a, b, d) for a in (-1, 0, 1) for b in (-1, 0, 1) for d in (-1, 0, 1)]
WEIGHTS = [(8.0 / 27.0, 2.0 / 27.0, 1.0 / 54.0, 1.0 / 216.0)[abs(a) + abs(b) + abs(d)] for a, b, d in DIRS]
OMEGA = 1.25
ROWS = 144
MINI = pl.ds(0, 8)
F32 = jnp.float32


def octet(n):
    return pl.ds(n * 8, 8) if isinstance(n, int) else pl.ds(pl.multiple_of(n * 8, 8), 8)


def tile(n):
    return octet(n + 1)


def lanes():
    return lax.broadcasted_iota(jnp.int32, (8, 128), 1)


def subs():
    return lax.broadcasted_iota(jnp.int32, (8, 128), 0)


def roll_l(v, k):
    return pltpu.roll(v, k, 1)


def roll_s(v, k):
    return pltpu.roll(v, k, 0)


def mod128(k):
    return lax.rem(k + 256, 128)


def sides(axis):
    parity = lax.rem(lax.axis_index(axis), 2)
    return (1 - 2 * parity, 2 * parity - 1)


class Later:
    def __init__(self, group):
        self.group, self.held = group, []

    def put(self, ref, at, value):
        self.held.append((ref, at, value))
        if len(self.held) >= self.group:
            self.flush()

    def flush(self):
        for ref, at, value in self.held:
            ref[at] = value
        self.held = []


ALL = slice(None)
OWN_GROUP, ROW_GROUP, STRIP_GROUP, PACK_GROUP = 18, 12, 12, 16


def moments(f):
    rho = f[13]
    mom = [None, None, None]
    for i in range(13):
        plus, minus = f[i] + f[26 - i], f[26 - i] - f[i]
        rho = rho + plus
        for k in range(3):
            c = DIRS[26 - i][k]
            if c:
                term = minus if c > 0 else -minus
                mom[k] = term if mom[k] is None else (mom[k] + minus if c > 0 else mom[k] - minus)
    inv = 1.0 / rho
    return rho, [m * inv for m in mom]


def dot_c(vec, comps):
    out = None
    for c, v in zip(vec, comps):
        if c:
            if out is None:
                out = v if c > 0 else -v
            else:
                out = out + v if c > 0 else out - v
    return out


def collide(f, solid, rho, u):
    fluid = 1.0 - solid
    own = (1.0 - OMEGA) * fluid
    base = OMEGA * fluid * rho
    rest = base * (1.0 - 1.5 * (u[0] * u[0] + u[1] * u[1] + u[2] * u[2]))
    out = [None] * 27
    for i in range(13):
        j = 26 - i
        w = WEIGHTS[i]
        cu = dot_c(DIRS[j], u)
        bc = base * cu
        even = w * (rest + 4.5 * (bc * cu))
        odd = (3.0 * w) * bc
        out[j] = own * f[j] + solid * f[i] + (even + odd)
        out[i] = own * f[i] + solid * f[j] + (even - odd)
    out[13] = (own + solid) * f[13] + WEIGHTS[13] * rest
    return out


def pull_back(p, solid, u, f=None, rho=None):
    w0 = WEIGHTS[13] * p[13]
    w1 = [None] * 3
    w2 = {}
    add = lambda x, y: y if x is None else x + y
    by_class = {}
    for i in range(13):
        j = 26 - i
        plus, minus = WEIGHTS[i] * (p[j] + p[i]), WEIGHTS[i] * (p[j] - p[i])
        w0 = w0 + plus
        c = DIRS[j]
        for k in range(3):
            if c[k]:
                w1[k] = add(w1[k], minus if c[k] > 0 else -minus)
            for m in range(k, 3):
                cc = c[k] * c[m]
                if cc:
                    w2[(k, m)] = add(w2.get((k, m)), plus if cc > 0 else -plus)
    at = lambda k, m: w2[(min(k, m), max(k, m))]
    w2u = [at(k, 0) * u[0] + at(k, 1) * u[1] + at(k, 2) * u[2] for k in range(3)]
    uwu = u[0] * w2u[0] + u[1] * w2u[1] + u[2] * w2u[2]
    uu = u[0] * u[0] + u[1] * u[1] + u[2] * u[2]
    fluid = 1.0 - solid
    own = (1.0 - OMEGA) * fluid
    gain = OMEGA * fluid
    g_rho = gain * (w0 * (1.0 + 1.5 * uu) - 4.5 * uwu)
    g_mom = [gain * (3.0 * w1[k] + 9.0 * w2u[k] - 3.0 * (u[k] * w0)) for k in range(3)]
    out = [None] * 27
    for i in range(13):
        j = 26 - i
        odd = dot_c(DIRS[j], g_mom)
        out[j] = own * p[j] + solid * p[i] + (g_rho + odd)
        out[i] = own * p[i] + solid * p[j] + (g_rho - odd)
    out[13] = (own + solid) * p[13] + g_rho
    if f is None:
        return out, None
    blame = OMEGA * (p[13] * f[13])
    for i in range(13):
        j = 26 - i
        blame = blame + (p[i] * (f[j] - (1.0 - OMEGA) * f[i]) + p[j] * (f[i] - (1.0 - OMEGA) * f[j]))
    w1u = w1[0] * u[0] + w1[1] * u[1] + w1[2] * u[2]
    blame = blame - (OMEGA * rho) * (w0 * (1.0 - 1.5 * uu) + 3.0 * w1u + 4.5 * uwu)
    return out, blame


STRIP_ROW = (7, 6, 0, 1)


def sources(bp, ext):
    if bp == 0:
        return [(0, None, 0, None), (2, None, 2, None)] if ext else []
    if bp == 1:
        return [(0, None, None, 0)] + ([(1, None, 0, None), (None, 7, 2, None)] if ext else [])
    return [(2, None, None, 7)] + ([(3, None, 2, None), (None, 0, 0, None)] if ext else [])


def shift_z(t0, t1, dp, ins, lane):
    if dp == 1:
        return jnp.where(lane == 0, ins, roll_l(t0, 1)), roll_l(jnp.where(lane == 127, t0, t1), 1)
    if dp == -1:
        return roll_l(jnp.where(lane == 0, t1, t0), 127), jnp.where(lane == 127, ins, roll_l(t1, 127))
    return t0, t1


def fan_out(line, sub, gz):
    v = roll_l(jnp.broadcast_to(line, (8, 128)), 127 - 2 * gz)
    for bit in (1, 2, 4):
        v = jnp.where((sub & bit) != 0, roll_l(v, 128 - 4 * bit), v)
    return v


def direction(a, b, d):
    return 9 * (a + 1) + 3 * (b + 1) + d + 1


def stream(own, rows, strip_rows, out, out_rows, out_strip_rows, orient, gz, low, high):
    lane, sub = lanes(), subs()
    ext = out_rows is not None

    def body(x, carry):
        later = Later(OWN_GROUP)
        for a in (-1, 0, 1):
            for b in (-1, 0, 1):
                xs = x - orient * a
                bp = orient * b
                into = direction(a, b, 0) + orient * (2 * gz - 1)
                ins = roll_l(own[into, MINI, :], 127 - 2 * gz - 4 * xs)
                if bp:
                    ins = roll_s(ins, bp % 8)
                for d in (-1, 0, 1):
                    i = direction(a, b, d)
                    t0, t1 = (own[i, pl.ds(16 * xs + 8 * half + 8 - bp, 8), :] for half in (0, 1))
                    pair = shift_z(t0, t1, orient * d, ins, lane)
                    for half in (0, 1):
                        later.put(out, (i, tile(2 * x + half), ALL), pair[half])
        later.flush()
        return carry

    lax.fori_loop(low, high, body, 0)

    jobs = []
    for a in (-1, 0, 1):
        for b in (-1, 0, 1):
            bp, ap = orient * b, orient * a
            into = direction(a, b, 0) + orient * (2 * gz - 1)
            for k_in, row_in, k_out, row_out in sources(bp, ext):
                if k_in is None:
                    line = own[into, pl.ds(row_in, 1), :]
                else:
                    line = strip_rows[into, pl.ds(STRIP_ROW[k_in], 1), :]
                jobs.append((a, b, ap, k_in, row_in, k_out, row_out, jnp.sum(jnp.where(lane == 4 * sub + 3 * gz, jnp.broadcast_to(line, (8, 128)), 0.0), axis=1, keepdims=True)))
    later = Later(ROW_GROUP)
    for a, b, ap, k_in, row_in, k_out, row_out, ins in jobs:
        for d in (-1, 0, 1):
            i = direction(a, b, d)
            if k_in is None:
                t0, t1 = (own[i, pl.ds(8 + 8 * half + row_in, 8, stride=16), :] for half in (0, 1))
            else:
                t0, t1 = rows[i, k_in, 0:8, :], rows[i, k_in, 8:16, :]
            pair = shift_z(t0, t1, orient * d, ins, lane)
            for half in (0, 1):
                v = pair[half]
                if ap:
                    v = roll_s(v, ap % 8)
                if k_out is None:
                    later.put(out, (i, pl.ds(8 + 8 * half + row_out, 8, stride=16), ALL), v)
                else:
                    later.put(out_rows, (i, k_out, octet(half), ALL), v)
    later.flush()

    wall = lane == 127 * gz
    later = Later(ROW_GROUP)
    for a in (-1, 0, 1):
        for b in (-1, 0, 1):
            i = direction(a, b, 0) + orient * (1 - 2 * gz)
            for x in range(low, high):
                here = tile(2 * x + gz)
                later.put(out, (i, here, ALL), jnp.where(wall, own[26 - i, here, :], out[i, here, :]))
            if ext:
                for k in (0, 2):
                    here = octet(gz)
                    later.put(out_rows, (i, k, here, ALL), jnp.where(wall, rows[26 - i, k, here, :], out_rows[i, k, here, :]))
    later.flush()

    slot = lax.rem(lane, 4)
    edge = 1 - gz
    later = Later(STRIP_GROUP)
    rims = []
    for a in (-1, 0, 1):
        for b in (-1, 0, 1):
            bp, ap = orient * b, orient * a
            outof = direction(a, b, 0) + orient * (1 - 2 * gz)
            need = [k for k, _, _, _ in sources(bp, ext) if k is not None]
            rim = jnp.zeros((8, 128), F32)
            for xe in range(low - ap, high - ap):
                src = own[outof, tile(2 * xe + edge), :]
                rim = jnp.where(lane == 4 * xe + 3 * gz, roll_l(src, 4 * xe + 1 + 2 * gz), rim)
            rim_rows = jnp.zeros((8, 128), F32)
            for k in need:
                src = pltpu.roll(roll_l(rows[outof, k, octet(edge), :], 1 + 2 * gz), 0, 1, stride=4, stride_axis=0)
                line = jnp.sum(jnp.where(lane == 4 * sub + 3 * gz, src, 0.0), axis=0, keepdims=True)
                rim_rows = jnp.where(sub == STRIP_ROW[k], line, rim_rows)
            rims.append((a, b, bp, ap, need, rim, rim_rows))
    for a, b, bp, ap, need, rim, rim_rows in rims:
        for d in (-1, 0, 1):
            i = direction(a, b, d)
            dp = orient * d

            def shifted(v, edge_values):
                if dp == 1:
                    v = jnp.where(slot == 0, edge_values, roll_l(v, 1))
                if dp == -1:
                    v = jnp.where(slot == 3, edge_values, roll_l(v, 127))
                return roll_l(v, (4 * ap) % 128) if ap else v

            vo = shifted(own[i, MINI, :], rim)
            vy = shifted(strip_rows[i], rim_rows) if need else None
            if bp == 0:
                later.put(out, (i, MINI, ALL), vo)
                if ext:
                    later.put(out_strip_rows, i, vy)
            else:
                last = 7 if bp == 1 else 0
                later.put(out, (i, MINI, ALL), roll_s(jnp.where(sub == last, vy, vo), bp % 8))
                if ext:
                    later.put(out_strip_rows, i, roll_s(jnp.where(sub == last, vo, vy), bp % 8))
    later.flush()


def entries(e, orient, stride, extra):
    others = [(r // 3, r % 3) for r in range(9)]
    number = lambda across, d: 3 * across + d if stride == 9 else 9 * across + d
    inward, outward = stride * (orient * e + 1), stride * (1 - orient * e)
    out = [(0, inward + number(c, d), 1, None, orient * (c - 1), 0) for c, d in others]
    out += [(0, stride + number(c, d), 1, None, orient * (c - 1), 0) for c, d in others]
    out += [(0, inward + number(c, d), 2, outward + number(c, d) if d != 1 else None, orient * (c - 1), orient * (d - 1)) for c, d in others]
    if extra:
        out += [(1, stride * (1 - e) + number(c, d), 1, None, 1 - c, 0) for c, d in others]
        out += [(2, 0, 1, None, 0, 0)]
    return out


def row_kinds(which, bp):
    if which == 1:
        return {1: (0,), 0: (), -1: (2,)}[bp]
    return {1: (0, 1), 0: (0, 2), -1: (2, 3)}[bp]


def near_plane(e):
    return 2 + 3 * ((e + 1) // 2)


def pack_faces(msg, e, orient, gz, arrays):
    later = Later(PACK_GROUP)
    near = near_plane(e)
    walls = {-1: (lanes() == 0) & (gz == 0), 1: (lanes() == 127) & (gz == 1)}
    for n, (which, i, layer, stash, _, dp) in enumerate(entries(e, orient, 9, len(arrays) > 1)):
        ref, plane = arrays[which], near if layer == 1 else near - e
        for half in (0, 1):
            v = ref[i, tile(2 * plane + half), :]
            if stash is not None and half == (dp + 1) // 2:
                v = jnp.where(walls[dp], ref[stash, tile(2 * near + half), :], v)
            later.put(msg, (slice((2 * n + half) * 8, (2 * n + half) * 8 + 8), ALL), v)
    later.flush()


def unpack_faces(msg, s, orient, arrays):
    later = Later(PACK_GROUP)
    near = near_plane(s) + s
    for n, (which, i, layer, stash, _, dp) in enumerate(entries(-s, orient, 9, len(arrays) > 1)):
        ref, plane = arrays[which], near if layer == 1 else near + s
        for half in (0, 1):
            v = msg[(2 * n + half) * 8 : (2 * n + half) * 8 + 8, :]
            later.put(ref, (i, tile(2 * plane + half), ALL), v)
            if stash is not None and half == (dp + 1) // 2:
                later.put(ref, (stash, tile(2 * near + half), ALL), v)
    later.flush()


def pack_sides(msg, e, orient, gz, arrays, strips):
    later = Later(PACK_GROUP)
    near = 7 * ((e + 1) // 2)
    lane = lax.broadcasted_iota(jnp.int32, (4, 128), 1)
    walls = {-1: (lane == 0) & (gz == 0), 1: (lane == 127) & (gz == 1)}
    items = entries(e, orient, 3, len(arrays) > 1)
    for n, (which, i, layer, stash, _, dp) in enumerate(items):
        ref, row = arrays[which], near if layer == 1 else near - e
        for half in (0, 1):
            v = ref[i, pl.ds(40 + 8 * half + row, 4, stride=16), :]
            if stash is not None and half == (dp + 1) // 2:
                v = jnp.where(walls[dp], ref[stash, pl.ds(40 + 8 * half + near, 4, stride=16), :], v)
            later.put(msg, (slice(8 * n + 4 * half, 8 * n + 4 * half + 4), ALL), v)
        later.put(msg, (slice(8 * len(items) + n, 8 * len(items) + n + 1), ALL), strips[which][i, pl.ds(row, 1), :])
    later.flush()


def unpack_sides(msg, s, orient, rows, strip_rows):
    k = s + 1
    later = Later(PACK_GROUP)
    near = 7 * ((1 - s) // 2)
    items = entries(-s, orient, 3, len(rows) > 1)
    for n, (which, i, layer, _, _, _) in enumerate(items):
        for half in (0, 1):
            later.put(rows[which], (i, k + layer - 1, slice(8 * half + 2, 8 * half + 6), ALL), msg[8 * n + 4 * half : 8 * n + 4 * half + 4, :])
        row = near if layer == 1 else near + s
        later.put(strip_rows[which], (i, pl.ds(row, 1), ALL), msg[8 * len(items) + n : 8 * len(items) + n + 1, :])
    later.flush()


def edge_rows(e, orient, extra):
    return 2 * sum(len(row_kinds(item[0], item[4])) for item in entries(e, orient, 9, extra))


def pack_edges(msg, e, orient, gz, rows, strips, strip_rows):
    later = Later(PACK_GROUP)
    near = near_plane(e)
    lane = lanes()
    lane2 = lax.broadcasted_iota(jnp.int32, (2, 128), 1)
    half2 = lax.broadcasted_iota(jnp.int32, (2, 128), 0)
    walls = {-1: (lane2 == 0) & (half2 == 0) & (gz == 0), 1: (lane2 == 127) & (half2 == 1) & (gz == 1)}
    items = entries(e, orient, 9, len(rows) > 1)
    at = 0
    tiles = (len(items) + 31) // 32
    packed = [[jnp.zeros((8, 128), F32) for _ in range(tiles)] for _ in range(2)]
    for n, (which, i, layer, stash, bp, dp) in enumerate(items):
        plane = near if layer == 1 else near - e
        for k in row_kinds(which, bp):
            v = rows[which][i, k, pl.ds(plane, 2, stride=8), :]
            if stash is not None:
                v = jnp.where(walls[dp], rows[which][stash, k, pl.ds(near, 2, stride=8), :], v)
            later.put(msg, (slice(at, at + 2), ALL), v)
            at += 2
        s = 4 * (n % 32)
        for kind, v in enumerate((strips[which][i], strip_rows[which][i])):
            moved = roll_l(v, mod128(s - 4 * plane))
            packed[kind][n // 32] = jnp.where((lane >= s) & (lane < s + 4), moved, packed[kind][n // 32])
    at = -(-at // 8) * 8
    for v in packed[0] + packed[1]:
        later.put(msg, (slice(at, at + 8), ALL), v)
        at += 8
    later.flush()


def unpack_edges(msg, s, orient, rows, owns, strip_rows):
    near = near_plane(s) + s
    plane_of = lax.div(lanes(), 4)
    items = entries(-s, orient, 9, len(rows) > 1)
    at = 0
    base = -(-edge_rows(1, orient, len(rows) > 1) // 8) * 8
    tiles = (len(items) + 31) // 32
    for n, (which, i, layer, stash, bp, _) in enumerate(items):
        plane = near if layer == 1 else near + s
        for k in row_kinds(which, bp):
            v = msg[at : at + 2, :]
            at += 2
            rows[which][i, k, pl.ds(plane, 2, stride=8), :] = v
            if stash is not None:
                rows[which][stash, k, pl.ds(near, 2, stride=8), :] = v
        for kind in (0, 1):
            r = base + 8 * (tiles * kind + n // 32)
            moved = roll_l(msg[r : r + 8, :], mod128(4 * plane - 4 * (n % 32)))
            if kind:
                strip_rows[which][i] = jnp.where(plane_of == plane, moved, strip_rows[which][i])
            else:
                owns[which][i, MINI, :] = jnp.where(plane_of == plane, moved, owns[which][i, MINI, :])


def reflect_rows(rows, orient):
    for a in range(3):
        for d in (0, 2):
            for k, b in ((0, 1 + orient), (2, 1 - orient)):
                rows[9 * a + 3 * (2 - b) + d, k] = rows[9 * a + 3 * b + d, k + 1]


def solid_of(blockage, mask):
    m = mask.astype(F32)
    return blockage * (1.0 - m) + m


def cut_kernel(pops_hbm, block_hbm, mask_hbm, cot_hbm, msg, pops, block, mask, cot, sems):
    gz = lax.axis_index("gz")
    lane = lanes()
    z = pl.ds(pl.multiple_of(128 * (1 - gz), 128), 128)
    copies = []
    for n, (src, dst) in enumerate(((pops_hbm, pops), (cot_hbm, cot))):
        copies.append(pltpu.make_async_copy(src.at[:, :, :, z], dst, sems.at[n]))
    for n, (src, dst) in enumerate(((block_hbm, block), (mask_hbm, mask))):
        copies.append(pltpu.make_async_copy(src.at[:, :, z], dst, sems.at[n + 2]))
    for copy in copies:
        copy.start()
    for copy in copies:
        copy.wait()
    for n in range(7):
        acc = jnp.zeros((8, 128), F32)
        for j in range(8):
            slot = 8 * n + j
            if slot > 54:
                break
            for x in range(4):
                if slot == 54:
                    edge = solid_of(block[x], mask[x])
                else:
                    ref, i = (pops, slot) if slot < 27 else (cot, slot - 27)
                    edge = ref[i, x]
                at = 16 * j + 4 * x
                moved = roll_l(edge, mod128(at + 4 - 4 * gz))
                acc = jnp.where((lane >= at) & (lane < at + 4), moved, acc)
        msg[8 * n : 8 * n + 8, :] = acc


def first_kernel(pops, block, mask, cot, after, tx, ax, sx, msg0, msg1):
    gz = lax.axis_index("gz")

    def body(x, carry):
        for half in (0, 1):
            z = pl.ds(128 * half, 128)
            here = tile(2 * (x + 2) + half)
            s = solid_of(block[x, :, z], mask[x, :, z])
            sx[0, here, :] = s
            f = [pops[i, x, :, z] for i in range(27)]
            rho, u = moments(f)
            out = collide(f, s, rho, u)
            for i in range(27):
                tx[i, here, :] = out[i]
                ax[i, here, :] = cot[i, x, :, z]
        return carry

    lax.fori_loop(0, 4, body, 0)
    for msg, e in zip((msg0, msg1), sides("gx")):
        pack_faces(msg, e, 1, gz, (tx, ax, sx))


def strip_kernel(cut, tx, ax, sx, tm, am, sm, msg0, msg1):
    gz = lax.axis_index("gz")

    def slot(n):
        return roll_l(cut[8 * (n // 8) : 8 * (n // 8) + 8, :], (8 - 16 * (n % 8)) % 128)

    s = slot(54)
    sm[0] = s
    f = [slot(i) for i in range(27)]
    rho, u = moments(f)
    out = collide(f, s, rho, u)
    for i in range(27):
        tm[i] = out[i]
        am[i] = slot(27 + i)
    for msg, e in zip((msg0, msg1), sides("gy")):
        pack_sides(msg, e, 1, gz, (tx, ax, sx), (tm, am, sm))


def edge_kernel(tm, am, sm, got0, got1, msg0, msg1, tr, ar, sr, tmr, amr, smr):
    gz = lax.axis_index("gz")
    rows, strip_rows = (tr, ar, sr), (tmr, amr, smr)
    for msg, s in zip((got0, got1), sides("gy")):
        unpack_sides(msg, s, 1, rows, strip_rows)
    for msg, e in zip((msg0, msg1), sides("gx")):
        pack_edges(msg, e, 1, gz, rows, (tm, am, sm), strip_rows)


def edge_kernel_2(tm, got0, got1, msg0, msg1, tr, tmr):
    gz = lax.axis_index("gz")
    for msg, s in zip((got0, got1), sides("gy")):
        unpack_sides(msg, s, -1, (tr,), (tmr,))
    for msg, e in zip((msg0, msg1), sides("gx")):
        pack_edges(msg, e, -1, gz, (tr,), (tm,), (tmr,))


def gather_in(pairs, strips):
    def body(n, carry):
        later = Later(PACK_GROUP)
        for src, dst in pairs:
            for i in range(src.shape[0]):
                later.put(dst, (i, tile(n), ALL), src[i, tile(n), :])
        later.flush()
        return carry

    lax.fori_loop(4, 12, body, 0)
    for (_, dst), strip in zip(pairs, strips):
        for i in range(strip.shape[0]):
            dst[i, MINI, :] = strip[i]


def receive(orient, owns, rows, strip_rows, by_y, faces, edges):
    for msg, s in zip(by_y, sides("gy")):
        unpack_sides(msg, s, orient, rows, strip_rows)
    for face, edge, s in zip(faces, edges, sides("gx")):
        unpack_faces(face, s, orient, owns)
        unpack_edges(edge, s, orient, rows, owns, strip_rows)
    reflect_rows(rows[0], orient)


def middle_kernel(
    tx, ax, sx, tm, am, sm, y0, y1, x0, x1, e0, e1,
    a2, a2m, f1, u_own, u_rows, u_strip, s_own, s_rows, s_strip, q2, ym0, ym1, xm0, xm1,
    t, a, tr, ar, tmr, amr, fr, fmr, c, cr, cmr, f2, p,
):
    gz = lax.axis_index("gz")
    gather_in(((tx, t), (ax, a), (sx, s_own)), (tm, am, sm))
    receive(1, (t, a, s_own), (tr, ar, s_rows), (tmr, amr, s_strip), (y0, y1), (x0, x1), (e0, e1))
    stream(t, tr, tmr, f1, fr, fmr, 1, gz, 1, 7)

    def collide_at(load, solid, store, store_u):
        f = [load(i) for i in range(27)]
        rho, u = moments(f)
        for n, v in enumerate([rho] + u):
            store_u(n, v)
        out = collide(f, solid, rho, u)
        for i in range(27):
            store(i, out[i])

    def again(k, carry):
        here = tile(jnp.where(k == 12, -1, k + 2))

        def put(i, v):
            c[i, here, :] = v

        def put_u(n, v):
            u_own[n, here, :] = v

        collide_at(lambda i: f1[i, here, :], s_own[0, here, :], put, put_u)
        return carry

    lax.fori_loop(0, 13, again, 0)

    def again_rows(k, carry):
        for half in (0, 1):
            here = octet(half)

            def put(i, v):
                cr[i, 2 * k, here, :] = v

            def put_u(n, v):
                u_rows[n, 2 * k, here, :] = v

            collide_at(lambda i: fr[i, 2 * k, here, :], s_rows[0, 2 * k, here, :], put, put_u)
        return carry

    lax.fori_loop(0, 2, again_rows, 0)

    def put_strip(i, v):
        cmr[i] = v

    def put_strip_u(n, v):
        u_strip[n] = v

    collide_at(lambda i: fmr[i], s_strip[0], put_strip, put_strip_u)
    stream(c, cr, cmr, f2, None, None, 1, gz, 2, 6)
    stream(a, ar, amr, p, None, None, -1, gz, 2, 6)

    def back(here):
        f = [f2[i, here, :] for i in range(27)]
        rho, u = moments(f)
        return pull_back([p[i, here, :] for i in range(27)], s_own[0, here, :], u, f, rho)

    def back_own(k, carry):
        here = tile(k + 4)
        out, blame = back(here)
        for i in range(27):
            a2[i, here, :] = out[i]
        q2[octet(k), :] = blame
        return carry

    lax.fori_loop(0, 8, back_own, 0)
    out, _ = back(MINI)
    for i in range(27):
        a2m[i] = out[i]
    for msg, e in zip((ym0, ym1), sides("gy")):
        pack_sides(msg, e, -1, gz, (a2,), (a2m,))
    for msg, e in zip((xm0, xm1), sides("gx")):
        pack_faces(msg, e, -1, gz, (a2,))


def last_kernel(
    a2, a2m, pops, mask, f1, u_own, u_rows, u_strip, s_own, s_rows, s_strip, q2, y0, y1, x0, x1, e0, e1,
    adjoint, grad,
    t, tr, tmr, p, pr, pmr, c, cr, cmr, q1,
):
    gz = lax.axis_index("gz")
    gather_in(((a2, t),), (a2m,))
    receive(-1, (t,), (tr,), (tmr,), (y0, y1), (x0, x1), (e0, e1))
    stream(t, tr, tmr, p, pr, pmr, -1, gz, 1, 7)

    def again(k, carry):
        here = tile(jnp.where(k == 12, -1, k + 2))
        u = [u_own[n, here, :] for n in (1, 2, 3)]
        out, blame = pull_back([p[i, here, :] for i in range(27)], s_own[0, here, :], u, [f1[i, here, :] for i in range(27)], u_own[0, here, :])
        for i in range(27):
            c[i, here, :] = out[i]
        q1[here, :] = blame
        return carry

    lax.fori_loop(0, 13, again, 0)

    def again_rows(k, carry):
        for half in (0, 1):
            here = octet(half)
            u = [u_rows[n, 2 * k, here, :] for n in (1, 2, 3)]
            out, _ = pull_back([pr[i, 2 * k, here, :] for i in range(27)], s_rows[0, 2 * k, here, :], u)
            for i in range(27):
                cr[i, 2 * k, here, :] = out[i]
        return carry

    lax.fori_loop(0, 2, again_rows, 0)
    out, _ = pull_back([pmr[i] for i in range(27)], s_strip[0], [u_strip[n] for n in (1, 2, 3)])
    for i in range(27):
        cmr[i] = out[i]
    stream(c, cr, cmr, p, None, None, -1, gz, 2, 6)

    def back(x, carry):
        for half in (0, 1):
            z = pl.ds(128 * half, 128)
            here = tile(2 * x + 4 + half)
            f = [pops[i, x, :, z] for i in range(27)]
            rho, u = moments(f)
            out, blame = pull_back([p[i, here, :] for i in range(27)], s_own[0, here, :], u, f, rho)
            for i in range(27):
                adjoint[i, x, :, z] = out[i]
            grad[x, :, z] = (1.0 - mask[x, :, z].astype(F32)) * (q1[here, :] + q2[octet(2 * x + half), :] + blame)
        return carry

    lax.fori_loop(0, 4, back, 0)


def call(kernel, outs, scratch=(), name=None, mib=8, in_specs=None):
    return pl.pallas_call(
        kernel,
        out_shape=[jax.ShapeDtypeStruct(s, F32) for s in outs],
        scratch_shapes=[pltpu.VMEM(s, F32) if isinstance(s, tuple) else s for s in scratch],
        **({} if in_specs is None else {"in_specs": in_specs}),
        compiler_params=pltpu.CompilerParams(vmem_limit_bytes=mib * 1024 * 1024),
        name=name,
    )


def swap(x, axis, odd):
    n = lax.axis_size(axis)
    pairs = [(i, (i ^ 1) if not odd else ((i + 1) % n if i % 2 else (i - 1) % n)) for i in range(n)]
    return lax.ppermute(x, axis, pairs)


BIG = (27, ROWS, 128)
ONE = (1, ROWS, 128)
STRIP = (27, 8, 128)
STRIP1 = (1, 8, 128)
HALO = (27, 4, 16, 128)
HALO1 = (1, 4, 16, 128)


def face_shape(n):
    return (16 * n, 128)


def side_shape(n):
    return (8 * n + -(-n // 8) * 8, 128)


def edge_shape(extra):
    n = 37 if extra else 27
    return (-(-edge_rows(1, 1, extra) // 8) * 8 + 16 * (-(-n // 32)), 128)


def swaps(pair, axis):
    return [swap(pair[0], axis, False), swap(pair[1], axis, True)]


def body(populations, blockage, solid_mask, cotangent):
    halves = [pltpu.VMEM((27, 4, 8, 128), F32), pltpu.VMEM((4, 8, 128), F32), pltpu.VMEM((4, 8, 128), jnp.int32), pltpu.VMEM((27, 4, 8, 128), F32)]
    anywhere = [pl.BlockSpec(memory_space=pltpu.HBM)] * 4
    (cut,) = call(cut_kernel, [(56, 128)], scratch=halves + [pltpu.SemaphoreType.DMA((4,))], name="cut", mib=60, in_specs=anywhere)(
        populations, blockage, solid_mask, cotangent
    )
    tx, ax, sx, *faces = call(first_kernel, [BIG, BIG, ONE, face_shape(37), face_shape(37)], name="first")(
        populations, blockage, solid_mask, cotangent, cut
    )
    cut = lax.ppermute(cut, "gz", [(0, 1), (1, 0)])
    tm, am, sm, *by_y = call(strip_kernel, [STRIP, STRIP, STRIP1, side_shape(37), side_shape(37)], name="strip")(cut, tx, ax, sx)
    by_y = swaps(by_y, "gy")
    faces, _ = lax.optimization_barrier((faces, tm))
    faces = swaps(faces, "gx")
    edges = call(
        edge_kernel, [edge_shape(True)] * 2, scratch=[HALO, HALO, HALO1, STRIP, STRIP, STRIP1], name="edge", mib=12
    )(tm, am, sm, *by_y)
    edges = swaps(edges, "gx")
    a2, a2m, f1, u_own, u_rows, u_strip, s_own, s_rows, s_strip, q2, *out = call(
        middle_kernel,
        [BIG, STRIP, BIG, (4, ROWS, 128), (4, 4, 16, 128), (4, 8, 128), ONE, HALO1, STRIP1, (64, 128)]
        + [(440, 128)] * 2
        + [face_shape(27)] * 2,
        scratch=[BIG, BIG, HALO, HALO, STRIP, STRIP, HALO, STRIP, BIG, HALO, STRIP, BIG, BIG],
        name="middle",
        mib=24,
    )(tx, ax, sx, tm, am, sm, *by_y, *faces, *edges)
    by_y = swaps(out[:2], "gy")
    faces = swaps(out[2:], "gx")
    edges = call(edge_kernel_2, [edge_shape(False)] * 2, scratch=[HALO, STRIP], name="edge2", mib=8)(a2m, *by_y)
    edges = swaps(edges, "gx")
    adjoint, grad = call(
        last_kernel,
        [populations.shape, blockage.shape],
        scratch=[BIG, HALO, STRIP, BIG, HALO, STRIP, BIG, HALO, STRIP, (ROWS, 128)],
        name="last",
        mib=20,
    )(a2, a2m, populations, solid_mask, f1, u_own, u_rows, u_strip, s_own, s_rows, s_strip, q2, *by_y, *faces, *edges)
    return adjoint, grad


def solution(mesh):
    placed = (P(None, "gx", "gy", "gz"), P("gx", "gy", "gz"), P("gx", "gy", "gz"), P(None, "gx", "gy", "gz"))
    return jax.shard_map(
        body, mesh=mesh, in_specs=placed, out_specs=(P(None, "gx", "gy", "gz"), P("gx", "gy", "gz")), check_vma=False
    )
```

```python
import functools
import jax
import jax.numpy as jnp
from jax import lax
from jax.experimental import pallas as pl
from jax.experimental.pallas import tpu as pltpu
from jax.sharding import PartitionSpec as P

DIRS = [(a, b, d) for a in (-1, 0, 1) for b in (-1, 0, 1) for d in (-1, 0, 1)]
WEIGHTS = [(8.0 / 27.0, 2.0 / 27.0, 1.0 / 54.0, 1.0 / 216.0)[abs(a) + abs(b) + abs(d)] for a, b, d in DIRS]
OMEGA = 1.25
ROWS = 144
MINI = pl.ds(0, 8)
F32 = jnp.float32


def octet(n):
    return pl.ds(n * 8, 8) if isinstance(n, int) else pl.ds(pl.multiple_of(n * 8, 8), 8)


def tile(n):
    return octet(n + 1)


def lanes():
    return lax.broadcasted_iota(jnp.int32, (8, 128), 1)


def subs():
    return lax.broadcasted_iota(jnp.int32, (8, 128), 0)


def roll_l(v, k):
    return pltpu.roll(v, k, 1)


def roll_s(v, k):
    return pltpu.roll(v, k, 0)


def mod128(k):
    return lax.rem(k + 256, 128)


def sides(axis):
    parity = lax.rem(lax.axis_index(axis), 2)
    return (1 - 2 * parity, 2 * parity - 1)


class Later:
    def __init__(self, group):
        self.group, self.held = group, []

    def put(self, ref, at, value):
        self.held.append((ref, at, value))
        if len(self.held) >= self.group:
            self.flush()

    def flush(self):
        for ref, at, value in self.held:
            ref[at] = value
        self.held = []


ALL = slice(None)
OWN_GROUP, ROW_GROUP, STRIP_GROUP, PACK_GROUP = 18, 12, 12, 16


def moments(f):
    rho = f[13]
    mom = [None, None, None]
    for i in range(13):
        plus, minus = f[i] + f[26 - i], f[26 - i] - f[i]
        rho = rho + plus
        for k in range(3):
            c = DIRS[26 - i][k]
            if c:
                term = minus if c > 0 else -minus
                mom[k] = term if mom[k] is None else (mom[k] + minus if c > 0 else mom[k] - minus)
    inv = 1.0 / rho
    return rho, [m * inv for m in mom]


def dot_c(vec, comps):
    out = None
    for c, v in zip(vec, comps):
        if c:
            if out is None:
                out = v if c > 0 else -v
            else:
                out = out + v if c > 0 else out - v
    return out


def collide(f, solid, rho, u):
    fluid = 1.0 - solid
    own = (1.0 - OMEGA) * fluid
    base = OMEGA * fluid * rho
    rest = base * (1.0 - 1.5 * (u[0] * u[0] + u[1] * u[1] + u[2] * u[2]))
    out = [None] * 27
    for i in range(13):
        j = 26 - i
        w = WEIGHTS[i]
        cu = dot_c(DIRS[j], u)
        bc = base * cu
        even = w * (rest + 4.5 * (bc * cu))
        odd = (3.0 * w) * bc
        out[j] = own * f[j] + solid * f[i] + (even + odd)
        out[i] = own * f[i] + solid * f[j] + (even - odd)
    out[13] = (own + solid) * f[13] + WEIGHTS[13] * rest
    return out


def pull_back(p, solid, u, f=None, rho=None):
    w0 = WEIGHTS[13] * p[13]
    w1 = [None] * 3
    w2 = {}
    add = lambda x, y: y if x is None else x + y
    by_class = {}
    for i in range(13):
        j = 26 - i
        plus, minus = WEIGHTS[i] * (p[j] + p[i]), WEIGHTS[i] * (p[j] - p[i])
        w0 = w0 + plus
        c = DIRS[j]
        for k in range(3):
            if c[k]:
                w1[k] = add(w1[k], minus if c[k] > 0 else -minus)
            for m in range(k, 3):
                cc = c[k] * c[m]
                if cc:
                    w2[(k, m)] = add(w2.get((k, m)), plus if cc > 0 else -plus)
    at = lambda k, m: w2[(min(k, m), max(k, m))]
    w2u = [at(k, 0) * u[0] + at(k, 1) * u[1] + at(k, 2) * u[2] for k in range(3)]
    uwu = u[0] * w2u[0] + u[1] * w2u[1] + u[2] * w2u[2]
    uu = u[0] * u[0] + u[1] * u[1] + u[2] * u[2]
    fluid = 1.0 - solid
    own = (1.0 - OMEGA) * fluid
    gain = OMEGA * fluid
    g_rho = gain * (w0 * (1.0 + 1.5 * uu) - 4.5 * uwu)
    g_mom = [gain * (3.0 * w1[k] + 9.0 * w2u[k] - 3.0 * (u[k] * w0)) for k in range(3)]
    out = [None] * 27
    for i in range(13):
        j = 26 - i
        odd = dot_c(DIRS[j], g_mom)
        out[j] = own * p[j] + solid * p[i] + (g_rho + odd)
        out[i] = own * p[i] + solid * p[j] + (g_rho - odd)
    out[13] = (own + solid) * p[13] + g_rho
    if f is None:
        return out, None
    blame = OMEGA * (p[13] * f[13])
    for i in range(13):
        j = 26 - i
        blame = blame + (p[i] * (f[j] - (1.0 - OMEGA) * f[i]) + p[j] * (f[i] - (1.0 - OMEGA) * f[j]))
    w1u = w1[0] * u[0] + w1[1] * u[1] + w1[2] * u[2]
    blame = blame - (OMEGA * rho) * (w0 * (1.0 - 1.5 * uu) + 3.0 * w1u + 4.5 * uwu)
    return out, blame


STRIP_ROW = (7, 6, 0, 1)


def sources(bp, ext):
    if bp == 0:
        return [(0, None, 0, None), (2, None, 2, None)] if ext else []
    if bp == 1:
        return [(0, None, None, 0)] + ([(1, None, 0, None), (None, 7, 2, None)] if ext else [])
    return [(2, None, None, 7)] + ([(3, None, 2, None), (None, 0, 0, None)] if ext else [])


def shift_z(t0, t1, dp, ins, lane):
    if dp == 1:
        return jnp.where(lane == 0, ins, roll_l(t0, 1)), roll_l(jnp.where(lane == 127, t0, t1), 1)
    if dp == -1:
        return roll_l(jnp.where(lane == 0, t1, t0), 127), jnp.where(lane == 127, ins, roll_l(t1, 127))
    return t0, t1


def fan_out(line, sub, gz):
    v = roll_l(jnp.broadcast_to(line, (8, 128)), 127 - 2 * gz)
    for bit in (1, 2, 4):
        v = jnp.where((sub & bit) != 0, roll_l(v, 128 - 4 * bit), v)
    return v


def direction(a, b, d):
    return 9 * (a + 1) + 3 * (b + 1) + d + 1


def stream(own, rows, strip_rows, out, out_rows, out_strip_rows, orient, gz, low, high, inner=True, strip=True):
    lane, sub = lanes(), subs()
    ext = out_rows is not None

    def body(n, carry):
        x = n if inner else jnp.where(n < 3, n, n + 2)
        later = Later(OWN_GROUP)
        for a in (-1, 0, 1):
            for b in (-1, 0, 1):
                xs = x - orient * a
                bp = orient * b
                into = direction(a, b, 0) + orient * (2 * gz - 1)
                ins = roll_l(own[into, MINI, :], 127 - 2 * gz - 4 * xs)
                if bp:
                    ins = roll_s(ins, bp % 8)
                for d in (-1, 0, 1):
                    i = direction(a, b, d)
                    t0, t1 = (own[i, pl.ds(16 * xs + 8 * half + 8 - bp, 8), :] for half in (0, 1))
                    pair = shift_z(t0, t1, orient * d, ins, lane)
                    for half in (0, 1):
                        later.put(out, (i, tile(2 * x + half), ALL), pair[half])
        later.flush()
        return carry

    lax.fori_loop(low, high if inner else high - 2, body, 0)

    jobs = []
    for a in (-1, 0, 1):
        for b in (-1, 0, 1):
            bp, ap = orient * b, orient * a
            into = direction(a, b, 0) + orient * (2 * gz - 1)
            for k_in, row_in, k_out, row_out in sources(bp, ext):
                if k_in is None:
                    line = own[into, pl.ds(row_in, 1), :]
                else:
                    line = strip_rows[into, pl.ds(STRIP_ROW[k_in], 1), :]
                jobs.append((a, b, ap, k_in, row_in, k_out, row_out, jnp.sum(jnp.where(lane == 4 * sub + 3 * gz, jnp.broadcast_to(line, (8, 128)), 0.0), axis=1, keepdims=True)))
    later = Later(ROW_GROUP)
    for a, b, ap, k_in, row_in, k_out, row_out, ins in jobs:
        for d in (-1, 0, 1):
            i = direction(a, b, d)
            if k_in is None:
                t0, t1 = (own[i, pl.ds(8 + 8 * half + row_in, 8, stride=16), :] for half in (0, 1))
            else:
                t0, t1 = rows[i, k_in, 0:8, :], rows[i, k_in, 8:16, :]
            pair = shift_z(t0, t1, orient * d, ins, lane)
            for half in (0, 1):
                v = pair[half]
                if ap:
                    v = roll_s(v, ap % 8)
                if k_out is None:
                    later.put(out, (i, pl.ds(8 + 8 * half + row_out, 8, stride=16), ALL), v)
                else:
                    later.put(out_rows, (i, k_out, octet(half), ALL), v)
    later.flush()

    wall = lane == 127 * gz
    later = Later(ROW_GROUP)
    for a in (-1, 0, 1):
        for b in (-1, 0, 1):
            i = direction(a, b, 0) + orient * (1 - 2 * gz)
            for x in range(low, high):
                if not inner and x in (3, 4):
                    continue
                here = tile(2 * x + gz)
                later.put(out, (i, here, ALL), jnp.where(wall, own[26 - i, here, :], out[i, here, :]))
            if ext:
                for k in (0, 2):
                    here = octet(gz)
                    later.put(out_rows, (i, k, here, ALL), jnp.where(wall, rows[26 - i, k, here, :], out_rows[i, k, here, :]))
    later.flush()

    if not strip:
        return
    slot = lax.rem(lane, 4)
    edge = 1 - gz
    later = Later(STRIP_GROUP)
    rims = []
    for a in (-1, 0, 1):
        for b in (-1, 0, 1):
            bp, ap = orient * b, orient * a
            outof = direction(a, b, 0) + orient * (1 - 2 * gz)
            need = [k for k, _, _, _ in sources(bp, ext) if k is not None]
            rim = jnp.zeros((8, 128), F32)
            for xe in range(low - ap, high - ap):
                src = own[outof, tile(2 * xe + edge), :]
                rim = jnp.where(lane == 4 * xe + 3 * gz, roll_l(src, 4 * xe + 1 + 2 * gz), rim)
            rim_rows = jnp.zeros((8, 128), F32)
            for k in need:
                src = pltpu.roll(roll_l(rows[outof, k, octet(edge), :], 1 + 2 * gz), 0, 1, stride=4, stride_axis=0)
                line = jnp.sum(jnp.where(lane == 4 * sub + 3 * gz, src, 0.0), axis=0, keepdims=True)
                rim_rows = jnp.where(sub == STRIP_ROW[k], line, rim_rows)
            rims.append((a, b, bp, ap, need, rim, rim_rows))
    for a, b, bp, ap, need, rim, rim_rows in rims:
        for d in (-1, 0, 1):
            i = direction(a, b, d)
            dp = orient * d

            def shifted(v, edge_values):
                if dp == 1:
                    v = jnp.where(slot == 0, edge_values, roll_l(v, 1))
                if dp == -1:
                    v = jnp.where(slot == 3, edge_values, roll_l(v, 127))
                return roll_l(v, (4 * ap) % 128) if ap else v

            vo = shifted(own[i, MINI, :], rim)
            vy = shifted(strip_rows[i], rim_rows) if need else None
            if bp == 0:
                later.put(out, (i, MINI, ALL), vo)
                if ext:
                    later.put(out_strip_rows, i, vy)
            else:
                last = 7 if bp == 1 else 0
                later.put(out, (i, MINI, ALL), roll_s(jnp.where(sub == last, vy, vo), bp % 8))
                if ext:
                    later.put(out_strip_rows, i, roll_s(jnp.where(sub == last, vo, vy), bp % 8))
    later.flush()


def entries(e, orient, stride, extra):
    others = [(r // 3, r % 3) for r in range(9)]
    number = lambda across, d: 3 * across + d if stride == 9 else 9 * across + d
    inward, outward = stride * (orient * e + 1), stride * (1 - orient * e)
    out = [(0, inward + number(c, d), 1, None, orient * (c - 1), 0) for c, d in others]
    out += [(0, stride + number(c, d), 1, None, orient * (c - 1), 0) for c, d in others]
    out += [(0, inward + number(c, d), 2, outward + number(c, d) if d != 1 else None, orient * (c - 1), orient * (d - 1)) for c, d in others]
    if extra:
        out += [(1, stride * (1 - e) + number(c, d), 1, None, 1 - c, 0) for c, d in others]
        out += [(2, 0, 1, None, 0, 0)]
    return out


def row_kinds(which, bp):
    if which == 1:
        return {1: (0,), 0: (), -1: (2,)}[bp]
    return {1: (0, 1), 0: (0, 2), -1: (2, 3)}[bp]


def near_plane(e):
    return 2 + 3 * ((e + 1) // 2)


def pack_faces(msg, e, orient, gz, arrays):
    later = Later(PACK_GROUP)
    near = near_plane(e)
    walls = {-1: (lanes() == 0) & (gz == 0), 1: (lanes() == 127) & (gz == 1)}
    for n, (which, i, layer, stash, _, dp) in enumerate(entries(e, orient, 9, len(arrays) > 1)):
        ref, plane = arrays[which], near if layer == 1 else near - e
        for half in (0, 1):
            v = ref[i, tile(2 * plane + half), :]
            if stash is not None and half == (dp + 1) // 2:
                v = jnp.where(walls[dp], ref[stash, tile(2 * near + half), :], v)
            later.put(msg, (slice((2 * n + half) * 8, (2 * n + half) * 8 + 8), ALL), v)
    later.flush()


def unpack_faces(msg, s, orient, arrays):
    later = Later(PACK_GROUP)
    near = near_plane(s) + s
    for n, (which, i, layer, stash, _, dp) in enumerate(entries(-s, orient, 9, len(arrays) > 1)):
        ref, plane = arrays[which], near if layer == 1 else near + s
        for half in (0, 1):
            v = msg[(2 * n + half) * 8 : (2 * n + half) * 8 + 8, :]
            later.put(ref, (i, tile(2 * plane + half), ALL), v)
            if stash is not None and half == (dp + 1) // 2:
                later.put(ref, (stash, tile(2 * near + half), ALL), v)
    later.flush()


def pack_sides(msg, e, orient, gz, arrays, strips):
    later = Later(PACK_GROUP)
    near = 7 * ((e + 1) // 2)
    lane = lax.broadcasted_iota(jnp.int32, (4, 128), 1)
    walls = {-1: (lane == 0) & (gz == 0), 1: (lane == 127) & (gz == 1)}
    items = entries(e, orient, 3, len(arrays) > 1)
    for n, (which, i, layer, stash, _, dp) in enumerate(items):
        ref, row = arrays[which], near if layer == 1 else near - e
        for half in (0, 1):
            v = ref[i, pl.ds(40 + 8 * half + row, 4, stride=16), :]
            if stash is not None and half == (dp + 1) // 2:
                v = jnp.where(walls[dp], ref[stash, pl.ds(40 + 8 * half + near, 4, stride=16), :], v)
            later.put(msg, (slice(8 * n + 4 * half, 8 * n + 4 * half + 4), ALL), v)
        later.put(msg, (slice(8 * len(items) + n, 8 * len(items) + n + 1), ALL), strips[which][i, pl.ds(row, 1), :])
    later.flush()


def unpack_sides(msg, s, orient, rows, strip_rows):
    k = s + 1
    later = Later(PACK_GROUP)
    near = 7 * ((1 - s) // 2)
    items = entries(-s, orient, 3, len(rows) > 1)
    for n, (which, i, layer, _, _, _) in enumerate(items):
        for half in (0, 1):
            later.put(rows[which], (i, k + layer - 1, slice(8 * half + 2, 8 * half + 6), ALL), msg[8 * n + 4 * half : 8 * n + 4 * half + 4, :])
        row = near if layer == 1 else near + s
        later.put(strip_rows[which], (i, pl.ds(row, 1), ALL), msg[8 * len(items) + n : 8 * len(items) + n + 1, :])
    later.flush()


def edge_rows(e, orient, extra):
    return 2 * sum(len(row_kinds(item[0], item[4])) for item in entries(e, orient, 9, extra))


def pack_edges(msg, e, orient, gz, rows, strips, strip_rows):
    later = Later(PACK_GROUP)
    near = near_plane(e)
    lane = lanes()
    lane2 = lax.broadcasted_iota(jnp.int32, (2, 128), 1)
    half2 = lax.broadcasted_iota(jnp.int32, (2, 128), 0)
    walls = {-1: (lane2 == 0) & (half2 == 0) & (gz == 0), 1: (lane2 == 127) & (half2 == 1) & (gz == 1)}
    items = entries(e, orient, 9, len(rows) > 1)
    at = 0
    tiles = (len(items) + 31) // 32
    packed = [[jnp.zeros((8, 128), F32) for _ in range(tiles)] for _ in range(2)]
    for n, (which, i, layer, stash, bp, dp) in enumerate(items):
        plane = near if layer == 1 else near - e
        for k in row_kinds(which, bp):
            v = rows[which][i, k, pl.ds(plane, 2, stride=8), :]
            if stash is not None:
                v = jnp.where(walls[dp], rows[which][stash, k, pl.ds(near, 2, stride=8), :], v)
            later.put(msg, (slice(at, at + 2), ALL), v)
            at += 2
        s = 4 * (n % 32)
        for kind, v in enumerate((strips[which][i], strip_rows[which][i])):
            moved = roll_l(v, mod128(s - 4 * plane))
            packed[kind][n // 32] = jnp.where((lane >= s) & (lane < s + 4), moved, packed[kind][n // 32])
    at = -(-at // 8) * 8
    for v in packed[0] + packed[1]:
        later.put(msg, (slice(at, at + 8), ALL), v)
        at += 8
    later.flush()


def unpack_edges(msg, s, orient, rows, owns, strip_rows):
    near = near_plane(s) + s
    plane_of = lax.div(lanes(), 4)
    items = entries(-s, orient, 9, len(rows) > 1)
    at = 0
    base = -(-edge_rows(1, orient, len(rows) > 1) // 8) * 8
    tiles = (len(items) + 31) // 32
    for n, (which, i, layer, stash, bp, _) in enumerate(items):
        plane = near if layer == 1 else near + s
        for k in row_kinds(which, bp):
            v = msg[at : at + 2, :]
            at += 2
            rows[which][i, k, pl.ds(plane, 2, stride=8), :] = v
            if stash is not None:
                rows[which][stash, k, pl.ds(near, 2, stride=8), :] = v
        for kind in (0, 1):
            r = base + 8 * (tiles * kind + n // 32)
            moved = roll_l(msg[r : r + 8, :], mod128(4 * plane - 4 * (n % 32)))
            if kind:
                strip_rows[which][i] = jnp.where(plane_of == plane, moved, strip_rows[which][i])
            else:
                owns[which][i, MINI, :] = jnp.where(plane_of == plane, moved, owns[which][i, MINI, :])


def reflect_rows(rows, orient):
    for a in range(3):
        for d in (0, 2):
            for k, b in ((0, 1 + orient), (2, 1 - orient)):
                rows[9 * a + 3 * (2 - b) + d, k] = rows[9 * a + 3 * b + d, k + 1]


def solid_of(blockage, mask):
    m = mask.astype(F32)
    return blockage * (1.0 - m) + m


def cut_kernel(pops_hbm, block_hbm, mask_hbm, cot_hbm, msg, pops, block, mask, cot, sems):
    gz = lax.axis_index("gz")
    lane = lanes()
    z = pl.ds(pl.multiple_of(128 * (1 - gz), 128), 128)
    copies = []
    for n, (src, dst) in enumerate(((pops_hbm, pops), (cot_hbm, cot))):
        copies.append(pltpu.make_async_copy(src.at[:, :, :, z], dst, sems.at[n]))
    for n, (src, dst) in enumerate(((block_hbm, block), (mask_hbm, mask))):
        copies.append(pltpu.make_async_copy(src.at[:, :, z], dst, sems.at[n + 2]))
    for copy in copies:
        copy.start()
    for copy in copies:
        copy.wait()
    for n in range(7):
        acc = jnp.zeros((8, 128), F32)
        for j in range(8):
            slot = 8 * n + j
            if slot > 54:
                break
            for x in range(4):
                if slot == 54:
                    edge = solid_of(block[x], mask[x])
                else:
                    ref, i = (pops, slot) if slot < 27 else (cot, slot - 27)
                    edge = ref[i, x]
                at = 16 * j + 4 * x
                moved = roll_l(edge, mod128(at + 4 - 4 * gz))
                acc = jnp.where((lane >= at) & (lane < at + 4), moved, acc)
        msg[8 * n : 8 * n + 8, :] = acc


def first_kernel(pops, block, mask, cot, after, tx, ax, sx, msg0, msg1):
    gz = lax.axis_index("gz")

    def body(x, carry):
        for half in (0, 1):
            z = pl.ds(128 * half, 128)
            here = tile(2 * (x + 2) + half)
            s = solid_of(block[x, :, z], mask[x, :, z])
            sx[0, here, :] = s
            f = [pops[i, x, :, z] for i in range(27)]
            rho, u = moments(f)
            out = collide(f, s, rho, u)
            for i in range(27):
                tx[i, here, :] = out[i]
                ax[i, here, :] = cot[i, x, :, z]
        return carry

    lax.fori_loop(0, 4, body, 0)
    for msg, e in zip((msg0, msg1), sides("gx")):
        pack_faces(msg, e, 1, gz, (tx, ax, sx))


def strip_kernel(cut, tx, ax, sx, tm, am, sm, msg0, msg1):
    gz = lax.axis_index("gz")

    def slot(n):
        return roll_l(cut[8 * (n // 8) : 8 * (n // 8) + 8, :], (8 - 16 * (n % 8)) % 128)

    s = slot(54)
    sm[0] = s
    f = [slot(i) for i in range(27)]
    rho, u = moments(f)
    out = collide(f, s, rho, u)
    for i in range(27):
        tm[i] = out[i]
        am[i] = slot(27 + i)
    for msg, e in zip((msg0, msg1), sides("gy")):
        pack_sides(msg, e, 1, gz, (tx, ax, sx), (tm, am, sm))


def edge_kernel(tm, am, sm, got0, got1, msg0, msg1, tr, ar, sr, tmr, amr, smr):
    gz = lax.axis_index("gz")
    rows, strip_rows = (tr, ar, sr), (tmr, amr, smr)
    for msg, s in zip((got0, got1), sides("gy")):
        unpack_sides(msg, s, 1, rows, strip_rows)
    for msg, e in zip((msg0, msg1), sides("gx")):
        pack_edges(msg, e, 1, gz, rows, (tm, am, sm), strip_rows)


def edge_kernel_2(tm, got0, got1, msg0, msg1, tr, tmr):
    gz = lax.axis_index("gz")
    for msg, s in zip((got0, got1), sides("gy")):
        unpack_sides(msg, s, -1, (tr,), (tmr,))
    for msg, e in zip((msg0, msg1), sides("gx")):
        pack_edges(msg, e, -1, gz, (tr,), (tm,), (tmr,))


def gather_in(pairs, strips):
    def body(n, carry):
        later = Later(PACK_GROUP)
        for src, dst in pairs:
            for i in range(src.shape[0]):
                later.put(dst, (i, tile(n), ALL), src[i, tile(n), :])
        later.flush()
        return carry

    lax.fori_loop(4, 12, body, 0)
    for (_, dst), strip in zip(pairs, strips):
        for i in range(strip.shape[0]):
            dst[i, MINI, :] = strip[i]


def receive(orient, owns, rows, strip_rows, by_y, faces, edges):
    for msg, s in zip(by_y, sides("gy")):
        unpack_sides(msg, s, orient, rows, strip_rows)
    for face, edge, s in zip(faces, edges, sides("gx")):
        unpack_faces(face, s, orient, owns)
        unpack_edges(edge, s, orient, rows, owns, strip_rows)
    reflect_rows(rows[0], orient)


def insert(pairs):
    def body(k, carry):
        later = Later(PACK_GROUP)
        for src, dst in pairs:
            for i in range(src.shape[0]):
                later.put(dst, (i, tile(k + 6), ALL), src[i, octet(k), :])
        later.flush()
        return carry

    lax.fori_loop(0, 4, body, 0)


def inner_kernel(tx, ax, sx, tm, am, sm, y0, y1, f_in, c_in, u_in, p_in, t, a, tr, ar, sr, tmr, amr, smr, f, p):
    gz = lax.axis_index("gz")
    gather_in(((tx, t), (ax, a)), (tm, am))
    for msg, s in zip((y0, y1), sides("gy")):
        unpack_sides(msg, s, 1, (tr, ar, sr), (tmr, amr, smr))
    stream(t, tr, tmr, f, None, None, 1, gz, 3, 5, strip=False)
    stream(a, ar, amr, p, None, None, -1, gz, 3, 5, strip=False)

    def body(k, carry):
        here, there = tile(k + 6), octet(k)
        pops = [f[i, here, :] for i in range(27)]
        rho, u = moments(pops)
        for n, v in enumerate([rho] + u):
            u_in[n, there, :] = v
        out = collide(pops, sx[0, here, :], rho, u)
        for i in range(27):
            f_in[i, there, :] = pops[i]
            c_in[i, there, :] = out[i]
            p_in[i, there, :] = p[i, here, :]
        return carry

    lax.fori_loop(0, 4, body, 0)


def inner_kernel_2(a2, a2m, f1, u_own, s_own, y0, y1, c_in, q_in, t, tr, tmr, p):
    gz = lax.axis_index("gz")
    gather_in(((a2, t),), (a2m,))
    for msg, s in zip((y0, y1), sides("gy")):
        unpack_sides(msg, s, -1, (tr,), (tmr,))
    stream(t, tr, tmr, p, None, None, -1, gz, 3, 5, strip=False)

    def body(k, carry):
        here, there = tile(k + 6), octet(k)
        u = [u_own[n, here, :] for n in (1, 2, 3)]
        out, blame = pull_back([p[i, here, :] for i in range(27)], s_own[0, here, :], u, [f1[i, here, :] for i in range(27)], u_own[0, here, :])
        for i in range(27):
            c_in[i, there, :] = out[i]
        q_in[0, there, :] = blame
        return carry

    lax.fori_loop(0, 4, body, 0)


def outer_tile(k):
    return tile(jnp.where(k == 8, -1, jnp.where(k < 4, k + 2, k + 6)))


def middle_kernel(
    tx, ax, sx, tm, am, sm, y0, y1, x0, x1, e0, e1, f_in, c_in, u_in, p_in,
    a2, a2m, f1, u_own, u_rows, u_strip, s_own, s_rows, s_strip, q2, ym0, ym1, xm0, xm1,
    t, a, tr, ar, tmr, amr, fr, fmr, c, cr, cmr, f2, p,
):
    gz = lax.axis_index("gz")
    gather_in(((tx, t), (ax, a), (sx, s_own)), (tm, am, sm))
    receive(1, (t, a, s_own), (tr, ar, s_rows), (tmr, amr, s_strip), (y0, y1), (x0, x1), (e0, e1))
    stream(t, tr, tmr, f1, fr, fmr, 1, gz, 1, 7, inner=False)
    insert(((f_in, f1), (c_in, c), (u_in, u_own)))

    def collide_at(load, solid, store, store_u):
        f = [load(i) for i in range(27)]
        rho, u = moments(f)
        for n, v in enumerate([rho] + u):
            store_u(n, v)
        out = collide(f, solid, rho, u)
        for i in range(27):
            store(i, out[i])

    def again(k, carry):
        here = outer_tile(k)

        def put(i, v):
            c[i, here, :] = v

        def put_u(n, v):
            u_own[n, here, :] = v

        collide_at(lambda i: f1[i, here, :], s_own[0, here, :], put, put_u)
        return carry

    lax.fori_loop(0, 9, again, 0)

    def again_rows(k, carry):
        for half in (0, 1):
            here = octet(half)

            def put(i, v):
                cr[i, 2 * k, here, :] = v

            def put_u(n, v):
                u_rows[n, 2 * k, here, :] = v

            collide_at(lambda i: fr[i, 2 * k, here, :], s_rows[0, 2 * k, here, :], put, put_u)
        return carry

    lax.fori_loop(0, 2, again_rows, 0)

    def put_strip(i, v):
        cmr[i] = v

    def put_strip_u(n, v):
        u_strip[n] = v

    collide_at(lambda i: fmr[i], s_strip[0], put_strip, put_strip_u)
    stream(c, cr, cmr, f2, None, None, 1, gz, 2, 6)
    stream(a, ar, amr, p, None, None, -1, gz, 2, 6, inner=False)
    insert(((p_in, p),))

    def back(here):
        f = [f2[i, here, :] for i in range(27)]
        rho, u = moments(f)
        return pull_back([p[i, here, :] for i in range(27)], s_own[0, here, :], u, f, rho)

    def back_own(k, carry):
        here = tile(k + 4)
        out, blame = back(here)
        for i in range(27):
            a2[i, here, :] = out[i]
        q2[octet(k), :] = blame
        return carry

    lax.fori_loop(0, 8, back_own, 0)
    out, _ = back(MINI)
    for i in range(27):
        a2m[i] = out[i]
    for msg, e in zip((ym0, ym1), sides("gy")):
        pack_sides(msg, e, -1, gz, (a2,), (a2m,))
    for msg, e in zip((xm0, xm1), sides("gx")):
        pack_faces(msg, e, -1, gz, (a2,))


def last_kernel(
    a2, a2m, pops, mask, f1, u_own, u_rows, u_strip, s_own, s_rows, s_strip, q2, y0, y1, x0, x1, e0, e1, c_in, q_in,
    adjoint, grad,
    t, tr, tmr, p, pr, pmr, c, cr, cmr, q1,
):
    gz = lax.axis_index("gz")
    gather_in(((a2, t),), (a2m,))
    receive(-1, (t,), (tr,), (tmr,), (y0, y1), (x0, x1), (e0, e1))
    stream(t, tr, tmr, p, pr, pmr, -1, gz, 1, 7, inner=False)
    insert(((c_in, c), (q_in, q1)))

    def again(k, carry):
        here = outer_tile(k)
        u = [u_own[n, here, :] for n in (1, 2, 3)]
        out, blame = pull_back([p[i, here, :] for i in range(27)], s_own[0, here, :], u, [f1[i, here, :] for i in range(27)], u_own[0, here, :])
        for i in range(27):
            c[i, here, :] = out[i]
        q1[0, here, :] = blame
        return carry

    lax.fori_loop(0, 9, again, 0)

    def again_rows(k, carry):
        for half in (0, 1):
            here = octet(half)
            u = [u_rows[n, 2 * k, here, :] for n in (1, 2, 3)]
            out, _ = pull_back([pr[i, 2 * k, here, :] for i in range(27)], s_rows[0, 2 * k, here, :], u)
            for i in range(27):
                cr[i, 2 * k, here, :] = out[i]
        return carry

    lax.fori_loop(0, 2, again_rows, 0)
    out, _ = pull_back([pmr[i] for i in range(27)], s_strip[0], [u_strip[n] for n in (1, 2, 3)])
    for i in range(27):
        cmr[i] = out[i]
    stream(c, cr, cmr, p, None, None, -1, gz, 2, 6)

    def back(x, carry):
        for half in (0, 1):
            z = pl.ds(128 * half, 128)
            here = tile(2 * x + 4 + half)
            f = [pops[i, x, :, z] for i in range(27)]
            rho, u = moments(f)
            out, blame = pull_back([p[i, here, :] for i in range(27)], s_own[0, here, :], u, f, rho)
            for i in range(27):
                adjoint[i, x, :, z] = out[i]
            grad[x, :, z] = (1.0 - mask[x, :, z].astype(F32)) * (q1[0, here, :] + q2[octet(2 * x + half), :] + blame)
        return carry

    lax.fori_loop(0, 4, back, 0)


def call(kernel, outs, scratch=(), name=None, mib=8, in_specs=None, cost=None):
    return pl.pallas_call(
        kernel,
        out_shape=[jax.ShapeDtypeStruct(s, F32) for s in outs],
        scratch_shapes=[pltpu.VMEM(s, F32) if isinstance(s, tuple) else s for s in scratch],
        **({} if in_specs is None else {"in_specs": in_specs}),
        compiler_params=pltpu.CompilerParams(vmem_limit_bytes=mib * 1024 * 1024),
        name=name,
        cost_estimate=None if cost is None else pl.CostEstimate(flops=0, bytes_accessed=cost, transcendentals=0),
    )


def swap(x, axis, odd):
    n = lax.axis_size(axis)
    pairs = [(i, (i ^ 1) if not odd else ((i + 1) % n if i % 2 else (i - 1) % n)) for i in range(n)]
    return lax.ppermute(x, axis, pairs)


BIG = (27, ROWS, 128)
ONE = (1, ROWS, 128)
QUAD = (27, 32, 128)
STRIP = (27, 8, 128)
STRIP1 = (1, 8, 128)
HALO = (27, 4, 16, 128)
HALO1 = (1, 4, 16, 128)


def face_shape(n):
    return (16 * n, 128)


def side_shape(n):
    return (8 * n + -(-n // 8) * 8, 128)


def edge_shape(extra):
    n = 37 if extra else 27
    return (-(-edge_rows(1, 1, extra) // 8) * 8 + 16 * (-(-n // 32)), 128)


def swaps(pair, axis):
    return [swap(pair[0], axis, False), swap(pair[1], axis, True)]


def body(populations, blockage, solid_mask, cotangent):
    halves = [pltpu.VMEM((27, 4, 8, 128), F32), pltpu.VMEM((4, 8, 128), F32), pltpu.VMEM((4, 8, 128), jnp.int32), pltpu.VMEM((27, 4, 8, 128), F32)]
    anywhere = [pl.BlockSpec(memory_space=pltpu.HBM)] * 4
    (cut,) = call(cut_kernel, [(56, 128)], scratch=halves + [pltpu.SemaphoreType.DMA((4,))], name="cut", mib=60, in_specs=anywhere)(
        populations, blockage, solid_mask, cotangent
    )
    tx, ax, sx, *faces = call(first_kernel, [BIG, BIG, ONE, face_shape(37), face_shape(37)], name="first")(
        populations, blockage, solid_mask, cotangent, cut
    )
    cut = lax.ppermute(cut, "gz", [(0, 1), (1, 0)])
    tm, am, sm, *by_y = call(strip_kernel, [STRIP, STRIP, STRIP1, side_shape(37), side_shape(37)], name="strip")(cut, tx, ax, sx)
    by_y = swaps(by_y, "gy")
    faces, _ = lax.optimization_barrier((faces, tm))
    faces = swaps(faces, "gx")
    edges = call(
        edge_kernel, [edge_shape(True)] * 2, scratch=[HALO, HALO, HALO1, STRIP, STRIP, STRIP1], name="edge", mib=12
    )(tm, am, sm, *by_y)
    edges = swaps(edges, "gx")
    inner = call(
        inner_kernel,
        [QUAD, QUAD, (4, 32, 128), QUAD],
        scratch=[BIG, BIG, HALO, HALO, HALO1, STRIP, STRIP, STRIP1, BIG, BIG],
        name="inner",
        mib=20,
        cost=6_000_000,
    )(tx, ax, sx, tm, am, sm, *by_y)
    a2, a2m, f1, u_own, u_rows, u_strip, s_own, s_rows, s_strip, q2, *out = call(
        middle_kernel,
        [BIG, STRIP, BIG, (4, ROWS, 128), (4, 4, 16, 128), (4, 8, 128), ONE, HALO1, STRIP1, (64, 128)]
        + [(440, 128)] * 2
        + [face_shape(27)] * 2,
        scratch=[BIG, BIG, HALO, HALO, STRIP, STRIP, HALO, STRIP, BIG, HALO, STRIP, BIG, BIG],
        name="middle",
        mib=24,
    )(tx, ax, sx, tm, am, sm, *by_y, *faces, *edges, *inner)
    by_y = swaps(out[:2], "gy")
    faces = swaps(out[2:], "gx")
    edges = call(edge_kernel_2, [edge_shape(False)] * 2, scratch=[HALO, STRIP], name="edge2", mib=8)(a2m, *by_y)
    edges = swaps(edges, "gx")
    inner = call(
        inner_kernel_2, [QUAD, (1, 32, 128)], scratch=[BIG, HALO, STRIP, BIG], name="inner2", mib=14, cost=6_000_000
    )(a2, a2m, f1, u_own, s_own, *by_y)
    adjoint, grad = call(
        last_kernel,
        [populations.shape, blockage.shape],
        scratch=[BIG, HALO, STRIP, BIG, HALO, STRIP, BIG, HALO, STRIP, ONE],
        name="last",
        mib=20,
    )(a2, a2m, populations, solid_mask, f1, u_own, u_rows, u_strip, s_own, s_rows, s_strip, q2, *by_y, *faces, *edges, *inner)
    return adjoint, grad


def solution(mesh):
    placed = (P(None, "gx", "gy", "gz"), P("gx", "gy", "gz"), P("gx", "gy", "gz"), P(None, "gx", "gy", "gz"))
    return jax.shard_map(
        body, mesh=mesh, in_specs=placed, out_specs=(P(None, "gx", "gy", "gz"), P("gx", "gy", "gz")), check_vma=False
    )
```

```python
import functools
import jax
import jax.numpy as jnp
from jax import lax
from jax.experimental import pallas as pl
from jax.experimental.pallas import tpu as pltpu
from jax.sharding import PartitionSpec as P

DIRS = [(a, b, d) for a in (-1, 0, 1) for b in (-1, 0, 1) for d in (-1, 0, 1)]
WEIGHTS = [(8.0 / 27.0, 2.0 / 27.0, 1.0 / 54.0, 1.0 / 216.0)[abs(a) + abs(b) + abs(d)] for a, b, d in DIRS]
OMEGA = 1.25
ROWS = 144
MINI = pl.ds(0, 8)
F32 = jnp.float32


def octet(n):
    return pl.ds(n * 8, 8) if isinstance(n, int) else pl.ds(pl.multiple_of(n * 8, 8), 8)


def tile(n):
    return octet(n + 1)


def lanes():
    return lax.broadcasted_iota(jnp.int32, (8, 128), 1)


def subs():
    return lax.broadcasted_iota(jnp.int32, (8, 128), 0)


def roll_l(v, k):
    return pltpu.roll(v, k, 1)


def roll_s(v, k):
    return pltpu.roll(v, k, 0)


def mod128(k):
    return lax.rem(k + 256, 128)


def sides(axis):
    parity = lax.rem(lax.axis_index(axis), 2)
    return (1 - 2 * parity, 2 * parity - 1)


class Later:
    def __init__(self, group):
        self.group, self.held = group, []

    def put(self, ref, at, value):
        self.held.append((ref, at, value))
        if len(self.held) >= self.group:
            self.flush()

    def flush(self):
        for ref, at, value in self.held:
            ref[at] = value
        self.held = []


ALL = slice(None)
OWN_GROUP, ROW_GROUP, STRIP_GROUP, PACK_GROUP = 18, 12, 12, 16


def moments(f):
    rho = f[13]
    mom = [None, None, None]
    for i in range(13):
        plus, minus = f[i] + f[26 - i], f[26 - i] - f[i]
        rho = rho + plus
        for k in range(3):
            c = DIRS[26 - i][k]
            if c:
                term = minus if c > 0 else -minus
                mom[k] = term if mom[k] is None else (mom[k] + minus if c > 0 else mom[k] - minus)
    inv = 1.0 / rho
    return rho, [m * inv for m in mom]


def dot_c(vec, comps):
    out = None
    for c, v in zip(vec, comps):
        if c:
            if out is None:
                out = v if c > 0 else -v
            else:
                out = out + v if c > 0 else out - v
    return out


def collide(f, solid, rho, u):
    fluid = 1.0 - solid
    own = (1.0 - OMEGA) * fluid
    base = OMEGA * fluid * rho
    rest = base * (1.0 - 1.5 * (u[0] * u[0] + u[1] * u[1] + u[2] * u[2]))
    out = [None] * 27
    for i in range(13):
        j = 26 - i
        w = WEIGHTS[i]
        cu = dot_c(DIRS[j], u)
        bc = base * cu
        even = w * (rest + 4.5 * (bc * cu))
        odd = (3.0 * w) * bc
        out[j] = own * f[j] + solid * f[i] + (even + odd)
        out[i] = own * f[i] + solid * f[j] + (even - odd)
    out[13] = (own + solid) * f[13] + WEIGHTS[13] * rest
    return out


def pull_back(p, solid, u, f=None, rho=None):
    w0 = WEIGHTS[13] * p[13]
    w1 = [None] * 3
    w2 = {}
    add = lambda x, y: y if x is None else x + y
    by_class = {}
    for i in range(13):
        j = 26 - i
        plus, minus = WEIGHTS[i] * (p[j] + p[i]), WEIGHTS[i] * (p[j] - p[i])
        w0 = w0 + plus
        c = DIRS[j]
        for k in range(3):
            if c[k]:
                w1[k] = add(w1[k], minus if c[k] > 0 else -minus)
            for m in range(k, 3):
                cc = c[k] * c[m]
                if cc:
                    w2[(k, m)] = add(w2.get((k, m)), plus if cc > 0 else -plus)
    at = lambda k, m: w2[(min(k, m), max(k, m))]
    w2u = [at(k, 0) * u[0] + at(k, 1) * u[1] + at(k, 2) * u[2] for k in range(3)]
    uwu = u[0] * w2u[0] + u[1] * w2u[1] + u[2] * w2u[2]
    uu = u[0] * u[0] + u[1] * u[1] + u[2] * u[2]
    fluid = 1.0 - solid
    own = (1.0 - OMEGA) * fluid
    gain = OMEGA * fluid
    g_rho = gain * (w0 * (1.0 + 1.5 * uu) - 4.5 * uwu)
    g_mom = [gain * (3.0 * w1[k] + 9.0 * w2u[k] - 3.0 * (u[k] * w0)) for k in range(3)]
    out = [None] * 27
    for i in range(13):
        j = 26 - i
        odd = dot_c(DIRS[j], g_mom)
        out[j] = own * p[j] + solid * p[i] + (g_rho + odd)
        out[i] = own * p[i] + solid * p[j] + (g_rho - odd)
    out[13] = (own + solid) * p[13] + g_rho
    if f is None:
        return out, None
    blame = OMEGA * (p[13] * f[13])
    for i in range(13):
        j = 26 - i
        blame = blame + (p[i] * (f[j] - (1.0 - OMEGA) * f[i]) + p[j] * (f[i] - (1.0 - OMEGA) * f[j]))
    w1u = w1[0] * u[0] + w1[1] * u[1] + w1[2] * u[2]
    blame = blame - (OMEGA * rho) * (w0 * (1.0 - 1.5 * uu) + 3.0 * w1u + 4.5 * uwu)
    return out, blame


STRIP_ROW = (7, 6, 0, 1)


def sources(bp, ext):
    if bp == 0:
        return [(0, None, 0, None), (2, None, 2, None)] if ext else []
    if bp == 1:
        return [(0, None, None, 0)] + ([(1, None, 0, None), (None, 7, 2, None)] if ext else [])
    return [(2, None, None, 7)] + ([(3, None, 2, None), (None, 0, 0, None)] if ext else [])


def shift_z(t0, t1, dp, ins, lane):
    if dp == 1:
        return jnp.where(lane == 0, ins, roll_l(t0, 1)), roll_l(jnp.where(lane == 127, t0, t1), 1)
    if dp == -1:
        return roll_l(jnp.where(lane == 0, t1, t0), 127), jnp.where(lane == 127, ins, roll_l(t1, 127))
    return t0, t1


def fan_out(line, sub, gz):
    v = roll_l(jnp.broadcast_to(line, (8, 128)), 127 - 2 * gz)
    for bit in (1, 2, 4):
        v = jnp.where((sub & bit) != 0, roll_l(v, 128 - 4 * bit), v)
    return v


def direction(a, b, d):
    return 9 * (a + 1) + 3 * (b + 1) + d + 1


def stream(own, rows, strip_rows, out, out_rows, out_strip_rows, orient, gz, low, high, inner=True, strip=True):
    lane, sub = lanes(), subs()
    ext = out_rows is not None

    def body(n, carry):
        x = n if inner else jnp.where(n < 3, n, n + 2)
        later = Later(OWN_GROUP)
        for a in (-1, 0, 1):
            for b in (-1, 0, 1):
                xs = x - orient * a
                bp = orient * b
                into = direction(a, b, 0) + orient * (2 * gz - 1)
                ins = roll_l(own[into, MINI, :], 127 - 2 * gz - 4 * xs)
                if bp:
                    ins = roll_s(ins, bp % 8)
                for d in (-1, 0, 1):
                    i = direction(a, b, d)
                    t0, t1 = (own[i, pl.ds(16 * xs + 8 * half + 8 - bp, 8), :] for half in (0, 1))
                    pair = shift_z(t0, t1, orient * d, ins, lane)
                    for half in (0, 1):
                        later.put(out, (i, tile(2 * x + half), ALL), pair[half])
        later.flush()
        return carry

    lax.fori_loop(low, high if inner else high - 2, body, 0)

    jobs = []
    for a in (-1, 0, 1):
        for b in (-1, 0, 1):
            bp, ap = orient * b, orient * a
            into = direction(a, b, 0) + orient * (2 * gz - 1)
            for k_in, row_in, k_out, row_out in sources(bp, ext):
                if k_in is None:
                    line = own[into, pl.ds(row_in, 1), :]
                else:
                    line = strip_rows[into, pl.ds(STRIP_ROW[k_in], 1), :]
                jobs.append((a, b, ap, k_in, row_in, k_out, row_out, jnp.sum(jnp.where(lane == 4 * sub + 3 * gz, jnp.broadcast_to(line, (8, 128)), 0.0), axis=1, keepdims=True)))
    later = Later(ROW_GROUP)
    for a, b, ap, k_in, row_in, k_out, row_out, ins in jobs:
        for d in (-1, 0, 1):
            i = direction(a, b, d)
            if k_in is None:
                t0, t1 = (own[i, pl.ds(8 + 8 * half + row_in, 8, stride=16), :] for half in (0, 1))
            else:
                t0, t1 = rows[i, k_in, 0:8, :], rows[i, k_in, 8:16, :]
            pair = shift_z(t0, t1, orient * d, ins, lane)
            for half in (0, 1):
                v = pair[half]
                if ap:
                    v = roll_s(v, ap % 8)
                if k_out is None:
                    later.put(out, (i, pl.ds(8 + 8 * half + row_out, 8, stride=16), ALL), v)
                else:
                    later.put(out_rows, (i, k_out, octet(half), ALL), v)
    later.flush()

    wall = lane == 127 * gz
    later = Later(ROW_GROUP)
    for a in (-1, 0, 1):
        for b in (-1, 0, 1):
            i = direction(a, b, 0) + orient * (1 - 2 * gz)
            for x in range(low, high):
                if not inner and x in (3, 4):
                    continue
                here = tile(2 * x + gz)
                later.put(out, (i, here, ALL), jnp.where(wall, own[26 - i, here, :], out[i, here, :]))
            if ext:
                for k in (0, 2):
                    here = octet(gz)
                    later.put(out_rows, (i, k, here, ALL), jnp.where(wall, rows[26 - i, k, here, :], out_rows[i, k, here, :]))
    later.flush()

    if not strip:
        return
    slot = lax.rem(lane, 4)
    edge = 1 - gz
    later = Later(STRIP_GROUP)
    rims = []
    for a in (-1, 0, 1):
        for b in (-1, 0, 1):
            bp, ap = orient * b, orient * a
            outof = direction(a, b, 0) + orient * (1 - 2 * gz)
            need = [k for k, _, _, _ in sources(bp, ext) if k is not None]
            rim = jnp.zeros((8, 128), F32)
            for xe in range(low - ap, high - ap):
                src = own[outof, tile(2 * xe + edge), :]
                rim = jnp.where(lane == 4 * xe + 3 * gz, roll_l(src, 4 * xe + 1 + 2 * gz), rim)
            rim_rows = jnp.zeros((8, 128), F32)
            for k in need:
                src = pltpu.roll(roll_l(rows[outof, k, octet(edge), :], 1 + 2 * gz), 0, 1, stride=4, stride_axis=0)
                line = jnp.sum(jnp.where(lane == 4 * sub + 3 * gz, src, 0.0), axis=0, keepdims=True)
                rim_rows = jnp.where(sub == STRIP_ROW[k], line, rim_rows)
            rims.append((a, b, bp, ap, need, rim, rim_rows))
    for a, b, bp, ap, need, rim, rim_rows in rims:
        for d in (-1, 0, 1):
            i = direction(a, b, d)
            dp = orient * d

            def shifted(v, edge_values):
                if dp == 1:
                    v = jnp.where(slot == 0, edge_values, roll_l(v, 1))
                if dp == -1:
                    v = jnp.where(slot == 3, edge_values, roll_l(v, 127))
                return roll_l(v, (4 * ap) % 128) if ap else v

            vo = shifted(own[i, MINI, :], rim)
            vy = shifted(strip_rows[i], rim_rows) if need else None
            if bp == 0:
                later.put(out, (i, MINI, ALL), vo)
                if ext:
                    later.put(out_strip_rows, i, vy)
            else:
                last = 7 if bp == 1 else 0
                later.put(out, (i, MINI, ALL), roll_s(jnp.where(sub == last, vy, vo), bp % 8))
                if ext:
                    later.put(out_strip_rows, i, roll_s(jnp.where(sub == last, vo, vy), bp % 8))
    later.flush()


def entries(e, orient, stride, extra):
    others = [(r // 3, r % 3) for r in range(9)]
    number = lambda across, d: 3 * across + d if stride == 9 else 9 * across + d
    inward, outward = stride * (orient * e + 1), stride * (1 - orient * e)
    out = [(0, inward + number(c, d), 1, None, orient * (c - 1), 0) for c, d in others]
    out += [(0, stride + number(c, d), 1, None, orient * (c - 1), 0) for c, d in others]
    out += [(0, inward + number(c, d), 2, outward + number(c, d) if d != 1 else None, orient * (c - 1), orient * (d - 1)) for c, d in others]
    if extra:
        out += [(1, stride * (1 - e) + number(c, d), 1, None, 1 - c, 0) for c, d in others]
        out += [(2, 0, 1, None, 0, 0)]
    return out


def row_kinds(which, bp):
    if which == 1:
        return {1: (0,), 0: (), -1: (2,)}[bp]
    return {1: (0, 1), 0: (0, 2), -1: (2, 3)}[bp]


def near_plane(e):
    return 2 + 3 * ((e + 1) // 2)


def pack_faces(msg, e, orient, gz, arrays):
    later = Later(PACK_GROUP)
    near = near_plane(e)
    walls = {-1: (lanes() == 0) & (gz == 0), 1: (lanes() == 127) & (gz == 1)}
    for n, (which, i, layer, stash, _, dp) in enumerate(entries(e, orient, 9, len(arrays) > 1)):
        ref, plane = arrays[which], near if layer == 1 else near - e
        for half in (0, 1):
            v = ref[i, tile(2 * plane + half), :]
            if stash is not None and half == (dp + 1) // 2:
                v = jnp.where(walls[dp], ref[stash, tile(2 * near + half), :], v)
            later.put(msg, (slice((2 * n + half) * 8, (2 * n + half) * 8 + 8), ALL), v)
    later.flush()


def unpack_faces(msg, s, orient, arrays):
    later = Later(PACK_GROUP)
    near = near_plane(s) + s
    for n, (which, i, layer, stash, _, dp) in enumerate(entries(-s, orient, 9, len(arrays) > 1)):
        ref, plane = arrays[which], near if layer == 1 else near + s
        for half in (0, 1):
            v = msg[(2 * n + half) * 8 : (2 * n + half) * 8 + 8, :]
            later.put(ref, (i, tile(2 * plane + half), ALL), v)
            if stash is not None and half == (dp + 1) // 2:
                later.put(ref, (stash, tile(2 * near + half), ALL), v)
    later.flush()


def pack_sides(msg, e, orient, gz, arrays, strips):
    later = Later(PACK_GROUP)
    near = 7 * ((e + 1) // 2)
    lane = lax.broadcasted_iota(jnp.int32, (4, 128), 1)
    walls = {-1: (lane == 0) & (gz == 0), 1: (lane == 127) & (gz == 1)}
    items = entries(e, orient, 3, len(arrays) > 1)
    for n, (which, i, layer, stash, _, dp) in enumerate(items):
        ref, row = arrays[which], near if layer == 1 else near - e
        for half in (0, 1):
            v = ref[i, pl.ds(40 + 8 * half + row, 4, stride=16), :]
            if stash is not None and half == (dp + 1) // 2:
                v = jnp.where(walls[dp], ref[stash, pl.ds(40 + 8 * half + near, 4, stride=16), :], v)
            later.put(msg, (slice(8 * n + 4 * half, 8 * n + 4 * half + 4), ALL), v)
        later.put(msg, (slice(8 * len(items) + n, 8 * len(items) + n + 1), ALL), strips[which][i, pl.ds(row, 1), :])
    later.flush()


def unpack_sides(msg, s, orient, rows, strip_rows):
    k = s + 1
    later = Later(PACK_GROUP)
    near = 7 * ((1 - s) // 2)
    items = entries(-s, orient, 3, len(rows) > 1)
    for n, (which, i, layer, _, _, _) in enumerate(items):
        for half in (0, 1):
            later.put(rows[which], (i, k + layer - 1, slice(8 * half + 2, 8 * half + 6), ALL), msg[8 * n + 4 * half : 8 * n + 4 * half + 4, :])
        row = near if layer == 1 else near + s
        later.put(strip_rows[which], (i, pl.ds(row, 1), ALL), msg[8 * len(items) + n : 8 * len(items) + n + 1, :])
    later.flush()


def edge_rows(e, orient, extra):
    return 2 * sum(len(row_kinds(item[0], item[4])) for item in entries(e, orient, 9, extra))


def pack_edges(msg, e, orient, gz, rows, strips, strip_rows):
    later = Later(PACK_GROUP)
    near = near_plane(e)
    lane = lanes()
    lane2 = lax.broadcasted_iota(jnp.int32, (2, 128), 1)
    half2 = lax.broadcasted_iota(jnp.int32, (2, 128), 0)
    walls = {-1: (lane2 == 0) & (half2 == 0) & (gz == 0), 1: (lane2 == 127) & (half2 == 1) & (gz == 1)}
    items = entries(e, orient, 9, len(rows) > 1)
    at = 0
    tiles = (len(items) + 31) // 32
    packed = [[jnp.zeros((8, 128), F32) for _ in range(tiles)] for _ in range(2)]
    for n, (which, i, layer, stash, bp, dp) in enumerate(items):
        plane = near if layer == 1 else near - e
        for k in row_kinds(which, bp):
            v = rows[which][i, k, pl.ds(plane, 2, stride=8), :]
            if stash is not None:
                v = jnp.where(walls[dp], rows[which][stash, k, pl.ds(near, 2, stride=8), :], v)
            later.put(msg, (slice(at, at + 2), ALL), v)
            at += 2
        s = 4 * (n % 32)
        for kind, v in enumerate((strips[which][i], strip_rows[which][i])):
            moved = roll_l(v, mod128(s - 4 * plane))
            packed[kind][n // 32] = jnp.where((lane >= s) & (lane < s + 4), moved, packed[kind][n // 32])
    at = -(-at // 8) * 8
    for v in packed[0] + packed[1]:
        later.put(msg, (slice(at, at + 8), ALL), v)
        at += 8
    later.flush()


def unpack_edges(msg, s, orient, rows, owns, strip_rows):
    near = near_plane(s) + s
    plane_of = lax.div(lanes(), 4)
    items = entries(-s, orient, 9, len(rows) > 1)
    at = 0
    base = -(-edge_rows(1, orient, len(rows) > 1) // 8) * 8
    tiles = (len(items) + 31) // 32
    for n, (which, i, layer, stash, bp, _) in enumerate(items):
        plane = near if layer == 1 else near + s
        for k in row_kinds(which, bp):
            v = msg[at : at + 2, :]
            at += 2
            rows[which][i, k, pl.ds(plane, 2, stride=8), :] = v
            if stash is not None:
                rows[which][stash, k, pl.ds(near, 2, stride=8), :] = v
        for kind in (0, 1):
            r = base + 8 * (tiles * kind + n // 32)
            moved = roll_l(msg[r : r + 8, :], mod128(4 * plane - 4 * (n % 32)))
            if kind:
                strip_rows[which][i] = jnp.where(plane_of == plane, moved, strip_rows[which][i])
            else:
                owns[which][i, MINI, :] = jnp.where(plane_of == plane, moved, owns[which][i, MINI, :])


def reflect_rows(rows, orient):
    for a in range(3):
        for d in (0, 2):
            for k, b in ((0, 1 + orient), (2, 1 - orient)):
                rows[9 * a + 3 * (2 - b) + d, k] = rows[9 * a + 3 * b + d, k + 1]


def solid_of(blockage, mask):
    m = mask.astype(F32)
    return blockage * (1.0 - m) + m


def lead_kernel(out):
    out[...] = jnp.zeros((8, 128), F32)


def cut_kernel(pops, block, mask, cot, after, msg):
    gz = lax.axis_index("gz")
    lane = lanes()
    top = gz == 0
    for n in range(7):
        acc = jnp.zeros((8, 128), F32)
        for j in range(8):
            slot = 8 * n + j
            if slot > 54:
                break
            for x in range(4):
                if slot == 54:
                    hi = solid_of(block[x, :, 128:256], mask[x, :, 128:256])
                    lo = solid_of(block[x, :, 0:128], mask[x, :, 0:128])
                else:
                    ref, i = (pops, slot) if slot < 27 else (cot, slot - 27)
                    hi, lo = ref[i, x, :, 128:256], ref[i, x, :, 0:128]
                at = 16 * j + 4 * x
                moved = roll_l(jnp.where(top, hi, lo), mod128(at + 4 - 4 * gz))
                acc = jnp.where((lane >= at) & (lane < at + 4), moved, acc)
        msg[8 * n : 8 * n + 8, :] = acc


def first_kernel(pops, block, mask, cot, after, tx, ax, sx, msg0, msg1):
    gz = lax.axis_index("gz")

    def body(x, carry):
        for half in (0, 1):
            z = pl.ds(128 * half, 128)
            here = tile(2 * (x + 2) + half)
            s = solid_of(block[x, :, z], mask[x, :, z])
            sx[0, here, :] = s
            f = [pops[i, x, :, z] for i in range(27)]
            rho, u = moments(f)
            out = collide(f, s, rho, u)
            for i in range(27):
                tx[i, here, :] = out[i]
                ax[i, here, :] = cot[i, x, :, z]
        return carry

    lax.fori_loop(0, 4, body, 0)
    for msg, e in zip((msg0, msg1), sides("gx")):
        pack_faces(msg, e, 1, gz, (tx, ax, sx))


def strip_kernel(cut, tx, ax, sx, tm, am, sm, msg0, msg1):
    gz = lax.axis_index("gz")

    def slot(n):
        return roll_l(cut[8 * (n // 8) : 8 * (n // 8) + 8, :], (8 - 16 * (n % 8)) % 128)

    s = slot(54)
    sm[0] = s
    f = [slot(i) for i in range(27)]
    rho, u = moments(f)
    out = collide(f, s, rho, u)
    for i in range(27):
        tm[i] = out[i]
        am[i] = slot(27 + i)
    for msg, e in zip((msg0, msg1), sides("gy")):
        pack_sides(msg, e, 1, gz, (tx, ax, sx), (tm, am, sm))


def edge_kernel(tm, am, sm, got0, got1, msg0, msg1, tr, ar, sr, tmr, amr, smr):
    gz = lax.axis_index("gz")
    rows, strip_rows = (tr, ar, sr), (tmr, amr, smr)
    for msg, s in zip((got0, got1), sides("gy")):
        unpack_sides(msg, s, 1, rows, strip_rows)
    for msg, e in zip((msg0, msg1), sides("gx")):
        pack_edges(msg, e, 1, gz, rows, (tm, am, sm), strip_rows)


def edge_kernel_2(tm, got0, got1, msg0, msg1, tr, tmr):
    gz = lax.axis_index("gz")
    for msg, s in zip((got0, got1), sides("gy")):
        unpack_sides(msg, s, -1, (tr,), (tmr,))
    for msg, e in zip((msg0, msg1), sides("gx")):
        pack_edges(msg, e, -1, gz, (tr,), (tm,), (tmr,))


def gather_in(pairs, strips):
    def body(n, carry):
        later = Later(PACK_GROUP)
        for src, dst in pairs:
            for i in range(src.shape[0]):
                later.put(dst, (i, tile(n), ALL), src[i, tile(n), :])
        later.flush()
        return carry

    lax.fori_loop(4, 12, body, 0)
    for (_, dst), strip in zip(pairs, strips):
        for i in range(strip.shape[0]):
            dst[i, MINI, :] = strip[i]


def receive(orient, owns, rows, strip_rows, by_y, faces, edges):
    for msg, s in zip(by_y, sides("gy")):
        unpack_sides(msg, s, orient, rows, strip_rows)
    for face, edge, s in zip(faces, edges, sides("gx")):
        unpack_faces(face, s, orient, owns)
        unpack_edges(edge, s, orient, rows, owns, strip_rows)
    reflect_rows(rows[0], orient)


def insert(pairs):
    def body(k, carry):
        later = Later(PACK_GROUP)
        for src, dst in pairs:
            for i in range(src.shape[0]):
                later.put(dst, (i, tile(k + 6), ALL), src[i, octet(k), :])
        later.flush()
        return carry

    lax.fori_loop(0, 4, body, 0)


def inner_kernel(tx, ax, sx, tm, am, sm, y0, y1, f_in, c_in, u_in, p_in, t, a, tr, ar, sr, tmr, amr, smr, f, p):
    gz = lax.axis_index("gz")
    gather_in(((tx, t), (ax, a)), (tm, am))
    for msg, s in zip((y0, y1), sides("gy")):
        unpack_sides(msg, s, 1, (tr, ar, sr), (tmr, amr, smr))
    stream(t, tr, tmr, f, None, None, 1, gz, 3, 5, strip=False)
    stream(a, ar, amr, p, None, None, -1, gz, 3, 5, strip=False)

    def body(k, carry):
        here, there = tile(k + 6), octet(k)
        pops = [f[i, here, :] for i in range(27)]
        rho, u = moments(pops)
        for n, v in enumerate([rho] + u):
            u_in[n, there, :] = v
        out = collide(pops, sx[0, here, :], rho, u)
        for i in range(27):
            f_in[i, there, :] = pops[i]
            c_in[i, there, :] = out[i]
            p_in[i, there, :] = p[i, here, :]
        return carry

    lax.fori_loop(0, 4, body, 0)


def inner_kernel_2(a2, a2m, f1, u_own, s_own, y0, y1, c_in, q_in, t, tr, tmr, p):
    gz = lax.axis_index("gz")
    gather_in(((a2, t),), (a2m,))
    for msg, s in zip((y0, y1), sides("gy")):
        unpack_sides(msg, s, -1, (tr,), (tmr,))
    stream(t, tr, tmr, p, None, None, -1, gz, 3, 5, strip=False)

    def body(k, carry):
        here, there = tile(k + 6), octet(k)
        u = [u_own[n, here, :] for n in (1, 2, 3)]
        out, blame = pull_back([p[i, here, :] for i in range(27)], s_own[0, here, :], u, [f1[i, here, :] for i in range(27)], u_own[0, here, :])
        for i in range(27):
            c_in[i, there, :] = out[i]
        q_in[0, there, :] = blame
        return carry

    lax.fori_loop(0, 4, body, 0)


def outer_tile(k):
    return tile(jnp.where(k == 8, -1, jnp.where(k < 4, k + 2, k + 6)))


def middle_kernel(
    tx, ax, sx, tm, am, sm, y0, y1, x0, x1, e0, e1, f_in, c_in, u_in, p_in,
    a2, a2m, f1, u_own, u_rows, u_strip, s_own, s_rows, s_strip, q2, ym0, ym1, xm0, xm1,
    t, a, tr, ar, tmr, amr, fr, fmr, c, cr, cmr, f2, p,
):
    gz = lax.axis_index("gz")
    gather_in(((tx, t), (ax, a), (sx, s_own)), (tm, am, sm))
    receive(1, (t, a, s_own), (tr, ar, s_rows), (tmr, amr, s_strip), (y0, y1), (x0, x1), (e0, e1))
    stream(t, tr, tmr, f1, fr, fmr, 1, gz, 1, 7, inner=False)
    insert(((f_in, f1), (c_in, c), (u_in, u_own)))

    def collide_at(load, solid, store, store_u):
        f = [load(i) for i in range(27)]
        rho, u = moments(f)
        for n, v in enumerate([rho] + u):
            store_u(n, v)
        out = collide(f, solid, rho, u)
        for i in range(27):
            store(i, out[i])

    def again(k, carry):
        here = outer_tile(k)

        def put(i, v):
            c[i, here, :] = v

        def put_u(n, v):
            u_own[n, here, :] = v

        collide_at(lambda i: f1[i, here, :], s_own[0, here, :], put, put_u)
        return carry

    lax.fori_loop(0, 9, again, 0)

    def again_rows(k, carry):
        for half in (0, 1):
            here = octet(half)

            def put(i, v):
                cr[i, 2 * k, here, :] = v

            def put_u(n, v):
                u_rows[n, 2 * k, here, :] = v

            collide_at(lambda i: fr[i, 2 * k, here, :], s_rows[0, 2 * k, here, :], put, put_u)
        return carry

    lax.fori_loop(0, 2, again_rows, 0)

    def put_strip(i, v):
        cmr[i] = v

    def put_strip_u(n, v):
        u_strip[n] = v

    collide_at(lambda i: fmr[i], s_strip[0], put_strip, put_strip_u)
    stream(c, cr, cmr, f2, None, None, 1, gz, 2, 6)
    stream(a, ar, amr, p, None, None, -1, gz, 2, 6, inner=False)
    insert(((p_in, p),))

    def back(here):
        f = [f2[i, here, :] for i in range(27)]
        rho, u = moments(f)
        return pull_back([p[i, here, :] for i in range(27)], s_own[0, here, :], u, f, rho)

    def back_own(k, carry):
        here = tile(k + 4)
        out, blame = back(here)
        for i in range(27):
            a2[i, here, :] = out[i]
        q2[octet(k), :] = blame
        return carry

    lax.fori_loop(0, 8, back_own, 0)
    out, _ = back(MINI)
    for i in range(27):
        a2m[i] = out[i]
    for msg, e in zip((ym0, ym1), sides("gy")):
        pack_sides(msg, e, -1, gz, (a2,), (a2m,))
    for msg, e in zip((xm0, xm1), sides("gx")):
        pack_faces(msg, e, -1, gz, (a2,))


def last_kernel(
    a2, a2m, pops, mask, f1, u_own, u_rows, u_strip, s_own, s_rows, s_strip, q2, y0, y1, x0, x1, e0, e1, c_in, q_in,
    adjoint, grad,
    t, tr, tmr, p, pr, pmr, c, cr, cmr, q1,
):
    gz = lax.axis_index("gz")
    gather_in(((a2, t),), (a2m,))
    receive(-1, (t,), (tr,), (tmr,), (y0, y1), (x0, x1), (e0, e1))
    stream(t, tr, tmr, p, pr, pmr, -1, gz, 1, 7, inner=False)
    insert(((c_in, c), (q_in, q1)))

    def again(k, carry):
        here = outer_tile(k)
        u = [u_own[n, here, :] for n in (1, 2, 3)]
        out, blame = pull_back([p[i, here, :] for i in range(27)], s_own[0, here, :], u, [f1[i, here, :] for i in range(27)], u_own[0, here, :])
        for i in range(27):
            c[i, here, :] = out[i]
        q1[0, here, :] = blame
        return carry

    lax.fori_loop(0, 9, again, 0)

    def again_rows(k, carry):
        for half in (0, 1):
            here = octet(half)
            u = [u_rows[n, 2 * k, here, :] for n in (1, 2, 3)]
            out, _ = pull_back([pr[i, 2 * k, here, :] for i in range(27)], s_rows[0, 2 * k, here, :], u)
            for i in range(27):
                cr[i, 2 * k, here, :] = out[i]
        return carry

    lax.fori_loop(0, 2, again_rows, 0)
    out, _ = pull_back([pmr[i] for i in range(27)], s_strip[0], [u_strip[n] for n in (1, 2, 3)])
    for i in range(27):
        cmr[i] = out[i]
    stream(c, cr, cmr, p, None, None, -1, gz, 2, 6)

    def back(x, carry):
        for half in (0, 1):
            z = pl.ds(128 * half, 128)
            here = tile(2 * x + 4 + half)
            f = [pops[i, x, :, z] for i in range(27)]
            rho, u = moments(f)
            out, blame = pull_back([p[i, here, :] for i in range(27)], s_own[0, here, :], u, f, rho)
            for i in range(27):
                adjoint[i, x, :, z] = out[i]
            grad[x, :, z] = (1.0 - mask[x, :, z].astype(F32)) * (q1[0, here, :] + q2[octet(2 * x + half), :] + blame)
        return carry

    lax.fori_loop(0, 4, back, 0)


def call(kernel, outs, scratch=(), name=None, mib=8, in_specs=None, cost=None):
    return pl.pallas_call(
        kernel,
        out_shape=[jax.ShapeDtypeStruct(s, F32) for s in outs],
        scratch_shapes=[pltpu.VMEM(s, F32) if isinstance(s, tuple) else s for s in scratch],
        **({} if in_specs is None else {"in_specs": in_specs}),
        compiler_params=pltpu.CompilerParams(vmem_limit_bytes=mib * 1024 * 1024),
        name=name,
        cost_estimate=None if cost is None else pl.CostEstimate(flops=2000 * cost if name == "lead" else 0, bytes_accessed=cost, transcendentals=0),
    )


def swap(x, axis, odd):
    n = lax.axis_size(axis)
    pairs = [(i, (i ^ 1) if not odd else ((i + 1) % n if i % 2 else (i - 1) % n)) for i in range(n)]
    return lax.ppermute(x, axis, pairs)


BIG = (27, ROWS, 128)
ONE = (1, ROWS, 128)
QUAD = (27, 32, 128)
STRIP = (27, 8, 128)
STRIP1 = (1, 8, 128)
HALO = (27, 4, 16, 128)
HALO1 = (1, 4, 16, 128)


def face_shape(n):
    return (16 * n, 128)


def side_shape(n):
    return (8 * n + -(-n // 8) * 8, 128)


def edge_shape(extra):
    n = 37 if extra else 27
    return (-(-edge_rows(1, 1, extra) // 8) * 8 + 16 * (-(-n // 32)), 128)


def swaps(pair, axis):
    return [swap(pair[0], axis, False), swap(pair[1], axis, True)]


def body(populations, blockage, solid_mask, cotangent):
    (lead,) = call(lead_kernel, [(8, 128)], name="lead", cost=12_000_000)()
    (cut,) = call(cut_kernel, [(56, 128)], name="cut")(populations, blockage, solid_mask, cotangent, lead)
    tx, ax, sx, *faces = call(first_kernel, [BIG, BIG, ONE, face_shape(37), face_shape(37)], name="first")(
        populations, blockage, solid_mask, cotangent, cut
    )
    cut = lax.ppermute(cut, "gz", [(0, 1), (1, 0)])
    tm, am, sm, *by_y = call(strip_kernel, [STRIP, STRIP, STRIP1, side_shape(37), side_shape(37)], name="strip")(cut, tx, ax, sx)
    by_y = swaps(by_y, "gy")
    faces, _ = lax.optimization_barrier((faces, tm))
    faces = swaps(faces, "gx")
    edges = call(
        edge_kernel, [edge_shape(True)] * 2, scratch=[HALO, HALO, HALO1, STRIP, STRIP, STRIP1], name="edge", mib=12
    )(tm, am, sm, *by_y)
    edges = swaps(edges, "gx")
    inner = call(
        inner_kernel,
        [QUAD, QUAD, (4, 32, 128), QUAD],
        scratch=[BIG, BIG, HALO, HALO, HALO1, STRIP, STRIP, STRIP1, BIG, BIG],
        name="inner",
        mib=20,
        cost=6_000_000,
    )(tx, ax, sx, tm, am, sm, *by_y)
    a2, a2m, f1, u_own, u_rows, u_strip, s_own, s_rows, s_strip, q2, *out = call(
        middle_kernel,
        [BIG, STRIP, BIG, (4, ROWS, 128), (4, 4, 16, 128), (4, 8, 128), ONE, HALO1, STRIP1, (64, 128)]
        + [(440, 128)] * 2
        + [face_shape(27)] * 2,
        scratch=[BIG, BIG, HALO, HALO, STRIP, STRIP, HALO, STRIP, BIG, HALO, STRIP, BIG, BIG],
        name="middle",
        mib=24,
    )(tx, ax, sx, tm, am, sm, *by_y, *faces, *edges, *inner)
    by_y = swaps(out[:2], "gy")
    faces = swaps(out[2:], "gx")
    edges = call(edge_kernel_2, [edge_shape(False)] * 2, scratch=[HALO, STRIP], name="edge2", mib=8)(a2m, *by_y)
    edges = swaps(edges, "gx")
    inner = call(
        inner_kernel_2, [QUAD, (1, 32, 128)], scratch=[BIG, HALO, STRIP, BIG], name="inner2", mib=14, cost=6_000_000
    )(a2, a2m, f1, u_own, s_own, *by_y)
    adjoint, grad = call(
        last_kernel,
        [populations.shape, blockage.shape],
        scratch=[BIG, HALO, STRIP, BIG, HALO, STRIP, BIG, HALO, STRIP, ONE],
        name="last",
        mib=20,
    )(a2, a2m, populations, solid_mask, f1, u_own, u_rows, u_strip, s_own, s_rows, s_strip, q2, *by_y, *faces, *edges, *inner)
    return adjoint, grad


def solution(mesh):
    placed = (P(None, "gx", "gy", "gz"), P("gx", "gy", "gz"), P("gx", "gy", "gz"), P(None, "gx", "gy", "gz"))
    return jax.shard_map(
        body, mesh=mesh, in_specs=placed, out_specs=(P(None, "gx", "gy", "gz"), P("gx", "gy", "gz")), check_vma=False
    )
```

```python
import functools
import jax
import jax.numpy as jnp
from jax import lax
from jax.experimental import pallas as pl
from jax.experimental.pallas import tpu as pltpu
from jax.sharding import PartitionSpec as P

DIRS = [(a, b, d) for a in (-1, 0, 1) for b in (-1, 0, 1) for d in (-1, 0, 1)]
WEIGHTS = [(8.0 / 27.0, 2.0 / 27.0, 1.0 / 54.0, 1.0 / 216.0)[abs(a) + abs(b) + abs(d)] for a, b, d in DIRS]
OMEGA = 1.25
ROWS = 144
MINI = pl.ds(0, 8)
F32 = jnp.float32


def octet(n):
    return pl.ds(n * 8, 8) if isinstance(n, int) else pl.ds(pl.multiple_of(n * 8, 8), 8)


def tile(n):
    return octet(n + 1)


def lanes():
    return lax.broadcasted_iota(jnp.int32, (8, 128), 1)


def subs():
    return lax.broadcasted_iota(jnp.int32, (8, 128), 0)


def roll_l(v, k):
    return pltpu.roll(v, k, 1)


def roll_s(v, k):
    return pltpu.roll(v, k, 0)


def mod128(k):
    return lax.rem(k + 256, 128)


def sides(axis):
    parity = lax.rem(lax.axis_index(axis), 2)
    return (1 - 2 * parity, 2 * parity - 1)


class Later:
    def __init__(self, group):
        self.group, self.held = group, []

    def put(self, ref, at, value):
        self.held.append((ref, at, value))
        if len(self.held) >= self.group:
            self.flush()

    def flush(self):
        for ref, at, value in self.held:
            ref[at] = value
        self.held = []


ALL = slice(None)
OWN_GROUP, ROW_GROUP, STRIP_GROUP, PACK_GROUP = 18, 12, 12, 16


def moments(f):
    rho = f[13]
    mom = [None, None, None]
    for i in range(13):
        plus, minus = f[i] + f[26 - i], f[26 - i] - f[i]
        rho = rho + plus
        for k in range(3):
            c = DIRS[26 - i][k]
            if c:
                term = minus if c > 0 else -minus
                mom[k] = term if mom[k] is None else (mom[k] + minus if c > 0 else mom[k] - minus)
    inv = 1.0 / rho
    return rho, [m * inv for m in mom]


def dot_c(vec, comps):
    out = None
    for c, v in zip(vec, comps):
        if c:
            if out is None:
                out = v if c > 0 else -v
            else:
                out = out + v if c > 0 else out - v
    return out


def collide(f, solid, rho, u):
    fluid = 1.0 - solid
    own = (1.0 - OMEGA) * fluid
    base = OMEGA * fluid * rho
    rest = base * (1.0 - 1.5 * (u[0] * u[0] + u[1] * u[1] + u[2] * u[2]))
    out = [None] * 27
    for i in range(13):
        j = 26 - i
        w = WEIGHTS[i]
        cu = dot_c(DIRS[j], u)
        bc = base * cu
        even = w * (rest + 4.5 * (bc * cu))
        odd = (3.0 * w) * bc
        out[j] = own * f[j] + solid * f[i] + (even + odd)
        out[i] = own * f[i] + solid * f[j] + (even - odd)
    out[13] = (own + solid) * f[13] + WEIGHTS[13] * rest
    return out


def pull_back(p, solid, u, f=None, rho=None):
    w0 = WEIGHTS[13] * p[13]
    w1 = [None] * 3
    w2 = {}
    add = lambda x, y: y if x is None else x + y
    by_class = {}
    for i in range(13):
        j = 26 - i
        plus, minus = WEIGHTS[i] * (p[j] + p[i]), WEIGHTS[i] * (p[j] - p[i])
        w0 = w0 + plus
        c = DIRS[j]
        for k in range(3):
            if c[k]:
                w1[k] = add(w1[k], minus if c[k] > 0 else -minus)
            for m in range(k, 3):
                cc = c[k] * c[m]
                if cc:
                    w2[(k, m)] = add(w2.get((k, m)), plus if cc > 0 else -plus)
    at = lambda k, m: w2[(min(k, m), max(k, m))]
    w2u = [at(k, 0) * u[0] + at(k, 1) * u[1] + at(k, 2) * u[2] for k in range(3)]
    uwu = u[0] * w2u[0] + u[1] * w2u[1] + u[2] * w2u[2]
    uu = u[0] * u[0] + u[1] * u[1] + u[2] * u[2]
    fluid = 1.0 - solid
    own = (1.0 - OMEGA) * fluid
    gain = OMEGA * fluid
    g_rho = gain * (w0 * (1.0 + 1.5 * uu) - 4.5 * uwu)
    g_mom = [gain * (3.0 * w1[k] + 9.0 * w2u[k] - 3.0 * (u[k] * w0)) for k in range(3)]
    out = [None] * 27
    for i in range(13):
        j = 26 - i
        odd = dot_c(DIRS[j], g_mom)
        out[j] = own * p[j] + solid * p[i] + (g_rho + odd)
        out[i] = own * p[i] + solid * p[j] + (g_rho - odd)
    out[13] = (own + solid) * p[13] + g_rho
    if f is None:
        return out, None
    blame = OMEGA * (p[13] * f[13])
    for i in range(13):
        j = 26 - i
        blame = blame + (p[i] * (f[j] - (1.0 - OMEGA) * f[i]) + p[j] * (f[i] - (1.0 - OMEGA) * f[j]))
    w1u = w1[0] * u[0] + w1[1] * u[1] + w1[2] * u[2]
    blame = blame - (OMEGA * rho) * (w0 * (1.0 - 1.5 * uu) + 3.0 * w1u + 4.5 * uwu)
    return out, blame


STRIP_ROW = (7, 6, 0, 1)


def sources(bp, ext):
    if bp == 0:
        return [(0, None, 0, None), (2, None, 2, None)] if ext else []
    if bp == 1:
        return [(0, None, None, 0)] + ([(1, None, 0, None), (None, 7, 2, None)] if ext else [])
    return [(2, None, None, 7)] + ([(3, None, 2, None), (None, 0, 0, None)] if ext else [])


def shift_z(t0, t1, dp, ins, lane):
    if dp == 1:
        return jnp.where(lane == 0, ins, roll_l(t0, 1)), roll_l(jnp.where(lane == 127, t0, t1), 1)
    if dp == -1:
        return roll_l(jnp.where(lane == 0, t1, t0), 127), jnp.where(lane == 127, ins, roll_l(t1, 127))
    return t0, t1


def fan_out(line, sub, gz):
    v = roll_l(jnp.broadcast_to(line, (8, 128)), 127 - 2 * gz)
    for bit in (1, 2, 4):
        v = jnp.where((sub & bit) != 0, roll_l(v, 128 - 4 * bit), v)
    return v


def direction(a, b, d):
    return 9 * (a + 1) + 3 * (b + 1) + d + 1


def stream(own, rows, strip_rows, out, out_rows, out_strip_rows, orient, gz, low, high, inner=True, strip=True):
    lane, sub = lanes(), subs()
    ext = out_rows is not None

    def body(n, carry):
        x = n if inner else jnp.where(n < 3, n, n + 2)
        later = Later(OWN_GROUP)
        for a in (-1, 0, 1):
            for b in (-1, 0, 1):
                xs = x - orient * a
                bp = orient * b
                into = direction(a, b, 0) + orient * (2 * gz - 1)
                ins = roll_l(own[into, MINI, :], 127 - 2 * gz - 4 * xs)
                if bp:
                    ins = roll_s(ins, bp % 8)
                for d in (-1, 0, 1):
                    i = direction(a, b, d)
                    t0, t1 = (own[i, pl.ds(16 * xs + 8 * half + 8 - bp, 8), :] for half in (0, 1))
                    pair = shift_z(t0, t1, orient * d, ins, lane)
                    for half in (0, 1):
                        later.put(out, (i, tile(2 * x + half), ALL), pair[half])
        later.flush()
        return carry

    lax.fori_loop(low, high if inner else high - 2, body, 0)

    jobs = []
    for a in (-1, 0, 1):
        for b in (-1, 0, 1):
            bp, ap = orient * b, orient * a
            into = direction(a, b, 0) + orient * (2 * gz - 1)
            for k_in, row_in, k_out, row_out in sources(bp, ext):
                if k_in is None:
                    line = own[into, pl.ds(row_in, 1), :]
                else:
                    line = strip_rows[into, pl.ds(STRIP_ROW[k_in], 1), :]
                jobs.append((a, b, ap, k_in, row_in, k_out, row_out, jnp.sum(jnp.where(lane == 4 * sub + 3 * gz, jnp.broadcast_to(line, (8, 128)), 0.0), axis=1, keepdims=True)))
    later = Later(ROW_GROUP)
    for a, b, ap, k_in, row_in, k_out, row_out, ins in jobs:
        for d in (-1, 0, 1):
            i = direction(a, b, d)
            if k_in is None:
                t0, t1 = (own[i, pl.ds(8 + 8 * half + row_in, 8, stride=16), :] for half in (0, 1))
            else:
                t0, t1 = rows[i, k_in, 0:8, :], rows[i, k_in, 8:16, :]
            pair = shift_z(t0, t1, orient * d, ins, lane)
            for half in (0, 1):
                v = pair[half]
                if ap:
                    v = roll_s(v, ap % 8)
                if k_out is None:
                    later.put(out, (i, pl.ds(8 + 8 * half + row_out, 8, stride=16), ALL), v)
                else:
                    later.put(out_rows, (i, k_out, octet(half), ALL), v)
    later.flush()

    wall = lane == 127 * gz
    later = Later(ROW_GROUP)
    for a in (-1, 0, 1):
        for b in (-1, 0, 1):
            i = direction(a, b, 0) + orient * (1 - 2 * gz)
            for x in range(low, high):
                if not inner and x in (3, 4):
                    continue
                here = tile(2 * x + gz)
                later.put(out, (i, here, ALL), jnp.where(wall, own[26 - i, here, :], out[i, here, :]))
            if ext:
                for k in (0, 2):
                    here = octet(gz)
                    later.put(out_rows, (i, k, here, ALL), jnp.where(wall, rows[26 - i, k, here, :], out_rows[i, k, here, :]))
    later.flush()

    if not strip:
        return
    slot = lax.rem(lane, 4)
    edge = 1 - gz
    later = Later(STRIP_GROUP)
    rims = []
    for a in (-1, 0, 1):
        for b in (-1, 0, 1):
            bp, ap = orient * b, orient * a
            outof = direction(a, b, 0) + orient * (1 - 2 * gz)
            need = [k for k, _, _, _ in sources(bp, ext) if k is not None]
            rim = jnp.zeros((8, 128), F32)
            for xe in range(low - ap, high - ap):
                src = own[outof, tile(2 * xe + edge), :]
                rim = jnp.where(lane == 4 * xe + 3 * gz, roll_l(src, 4 * xe + 1 + 2 * gz), rim)
            rim_rows = jnp.zeros((8, 128), F32)
            for k in need:
                src = pltpu.roll(roll_l(rows[outof, k, octet(edge), :], 1 + 2 * gz), 0, 1, stride=4, stride_axis=0)
                line = jnp.sum(jnp.where(lane == 4 * sub + 3 * gz, src, 0.0), axis=0, keepdims=True)
                rim_rows = jnp.where(sub == STRIP_ROW[k], line, rim_rows)
            rims.append((a, b, bp, ap, need, rim, rim_rows))
    for a, b, bp, ap, need, rim, rim_rows in rims:
        for d in (-1, 0, 1):
            i = direction(a, b, d)
            dp = orient * d

            def shifted(v, edge_values):
                if dp == 1:
                    v = jnp.where(slot == 0, edge_values, roll_l(v, 1))
                if dp == -1:
                    v = jnp.where(slot == 3, edge_values, roll_l(v, 127))
                return roll_l(v, (4 * ap) % 128) if ap else v

            vo = shifted(own[i, MINI, :], rim)
            vy = shifted(strip_rows[i], rim_rows) if need else None
            if bp == 0:
                later.put(out, (i, MINI, ALL), vo)
                if ext:
                    later.put(out_strip_rows, i, vy)
            else:
                last = 7 if bp == 1 else 0
                later.put(out, (i, MINI, ALL), roll_s(jnp.where(sub == last, vy, vo), bp % 8))
                if ext:
                    later.put(out_strip_rows, i, roll_s(jnp.where(sub == last, vo, vy), bp % 8))
    later.flush()


def entries(e, orient, stride, extra):
    others = [(r // 3, r % 3) for r in range(9)]
    number = lambda across, d: 3 * across + d if stride == 9 else 9 * across + d
    inward, outward = stride * (orient * e + 1), stride * (1 - orient * e)
    out = [(0, inward + number(c, d), 1, None, orient * (c - 1), 0) for c, d in others]
    out += [(0, stride + number(c, d), 1, None, orient * (c - 1), 0) for c, d in others]
    out += [(0, inward + number(c, d), 2, outward + number(c, d) if d != 1 else None, orient * (c - 1), orient * (d - 1)) for c, d in others]
    if extra:
        out += [(1, stride * (1 - e) + number(c, d), 1, None, 1 - c, 0) for c, d in others]
        out += [(2, 0, 1, None, 0, 0)]
    return out


def row_kinds(which, bp):
    if which == 1:
        return {1: (0,), 0: (), -1: (2,)}[bp]
    return {1: (0, 1), 0: (0, 2), -1: (2, 3)}[bp]


def near_plane(e):
    return 2 + 3 * ((e + 1) // 2)


def pack_faces(msg, e, orient, gz, arrays):
    later = Later(PACK_GROUP)
    near = near_plane(e)
    walls = {-1: (lanes() == 0) & (gz == 0), 1: (lanes() == 127) & (gz == 1)}
    for n, (which, i, layer, stash, _, dp) in enumerate(entries(e, orient, 9, len(arrays) > 1)):
        ref, plane = arrays[which], near if layer == 1 else near - e
        for half in (0, 1):
            v = ref[i, tile(2 * plane + half), :]
            if stash is not None and half == (dp + 1) // 2:
                v = jnp.where(walls[dp], ref[stash, tile(2 * near + half), :], v)
            later.put(msg, (slice((2 * n + half) * 8, (2 * n + half) * 8 + 8), ALL), v)
    later.flush()


def unpack_faces(msg, s, orient, arrays):
    later = Later(PACK_GROUP)
    near = near_plane(s) + s
    for n, (which, i, layer, stash, _, dp) in enumerate(entries(-s, orient, 9, len(arrays) > 1)):
        ref, plane = arrays[which], near if layer == 1 else near + s
        for half in (0, 1):
            v = msg[(2 * n + half) * 8 : (2 * n + half) * 8 + 8, :]
            later.put(ref, (i, tile(2 * plane + half), ALL), v)
            if stash is not None and half == (dp + 1) // 2:
                later.put(ref, (stash, tile(2 * near + half), ALL), v)
    later.flush()


def pack_sides(msg, e, orient, gz, arrays, strips):
    later = Later(PACK_GROUP)
    near = 7 * ((e + 1) // 2)
    lane = lax.broadcasted_iota(jnp.int32, (4, 128), 1)
    walls = {-1: (lane == 0) & (gz == 0), 1: (lane == 127) & (gz == 1)}
    items = entries(e, orient, 3, len(arrays) > 1)
    for n, (which, i, layer, stash, _, dp) in enumerate(items):
        ref, row = arrays[which], near if layer == 1 else near - e
        for half in (0, 1):
            v = ref[i, pl.ds(40 + 8 * half + row, 4, stride=16), :]
            if stash is not None and half == (dp + 1) // 2:
                v = jnp.where(walls[dp], ref[stash, pl.ds(40 + 8 * half + near, 4, stride=16), :], v)
            later.put(msg, (slice(8 * n + 4 * half, 8 * n + 4 * half + 4), ALL), v)
        later.put(msg, (slice(8 * len(items) + n, 8 * len(items) + n + 1), ALL), strips[which][i, pl.ds(row, 1), :])
    later.flush()


def unpack_sides(msg, s, orient, rows, strip_rows):
    k = s + 1
    later = Later(PACK_GROUP)
    near = 7 * ((1 - s) // 2)
    items = entries(-s, orient, 3, len(rows) > 1)
    for n, (which, i, layer, _, _, _) in enumerate(items):
        for half in (0, 1):
            later.put(rows[which], (i, k + layer - 1, slice(8 * half + 2, 8 * half + 6), ALL), msg[8 * n + 4 * half : 8 * n + 4 * half + 4, :])
        row = near if layer == 1 else near + s
        later.put(strip_rows[which], (i, pl.ds(row, 1), ALL), msg[8 * len(items) + n : 8 * len(items) + n + 1, :])
    later.flush()


def edge_rows(e, orient, extra):
    return 2 * sum(len(row_kinds(item[0], item[4])) for item in entries(e, orient, 9, extra))


def pack_edges(msg, e, orient, gz, rows, strips, strip_rows):
    later = Later(PACK_GROUP)
    near = near_plane(e)
    lane = lanes()
    lane2 = lax.broadcasted_iota(jnp.int32, (2, 128), 1)
    half2 = lax.broadcasted_iota(jnp.int32, (2, 128), 0)
    walls = {-1: (lane2 == 0) & (half2 == 0) & (gz == 0), 1: (lane2 == 127) & (half2 == 1) & (gz == 1)}
    items = entries(e, orient, 9, len(rows) > 1)
    at = 0
    tiles = (len(items) + 31) // 32
    packed = [[jnp.zeros((8, 128), F32) for _ in range(tiles)] for _ in range(2)]
    for n, (which, i, layer, stash, bp, dp) in enumerate(items):
        plane = near if layer == 1 else near - e
        for k in row_kinds(which, bp):
            v = rows[which][i, k, pl.ds(plane, 2, stride=8), :]
            if stash is not None:
                v = jnp.where(walls[dp], rows[which][stash, k, pl.ds(near, 2, stride=8), :], v)
            later.put(msg, (slice(at, at + 2), ALL), v)
            at += 2
        s = 4 * (n % 32)
        for kind, v in enumerate((strips[which][i], strip_rows[which][i])):
            moved = roll_l(v, mod128(s - 4 * plane))
            packed[kind][n // 32] = jnp.where((lane >= s) & (lane < s + 4), moved, packed[kind][n // 32])
    at = -(-at // 8) * 8
    for v in packed[0] + packed[1]:
        later.put(msg, (slice(at, at + 8), ALL), v)
        at += 8
    later.flush()


def unpack_edges(msg, s, orient, rows, owns, strip_rows):
    near = near_plane(s) + s
    plane_of = lax.div(lanes(), 4)
    items = entries(-s, orient, 9, len(rows) > 1)
    at = 0
    base = -(-edge_rows(1, orient, len(rows) > 1) // 8) * 8
    tiles = (len(items) + 31) // 32
    for n, (which, i, layer, stash, bp, _) in enumerate(items):
        plane = near if layer == 1 else near + s
        for k in row_kinds(which, bp):
            v = msg[at : at + 2, :]
            at += 2
            rows[which][i, k, pl.ds(plane, 2, stride=8), :] = v
            if stash is not None:
                rows[which][stash, k, pl.ds(near, 2, stride=8), :] = v
        for kind in (0, 1):
            r = base + 8 * (tiles * kind + n // 32)
            moved = roll_l(msg[r : r + 8, :], mod128(4 * plane - 4 * (n % 32)))
            if kind:
                strip_rows[which][i] = jnp.where(plane_of == plane, moved, strip_rows[which][i])
            else:
                owns[which][i, MINI, :] = jnp.where(plane_of == plane, moved, owns[which][i, MINI, :])


def reflect_rows(rows, orient):
    for a in range(3):
        for d in (0, 2):
            for k, b in ((0, 1 + orient), (2, 1 - orient)):
                rows[9 * a + 3 * (2 - b) + d, k] = rows[9 * a + 3 * b + d, k + 1]


def solid_of(blockage, mask):
    m = mask.astype(F32)
    return blockage * (1.0 - m) + m


def lead_kernel(out):
    out[...] = jnp.zeros((8, 128), F32)


def cut_kernel(pops, block, mask, cot, after, msg):
    gz = lax.axis_index("gz")
    lane = lanes()
    top = gz == 0
    for n in range(7):
        acc = jnp.zeros((8, 128), F32)
        for j in range(8):
            slot = 8 * n + j
            if slot > 54:
                break
            for x in range(4):
                if slot == 54:
                    hi = solid_of(block[x, :, 128:256], mask[x, :, 128:256])
                    lo = solid_of(block[x, :, 0:128], mask[x, :, 0:128])
                else:
                    ref, i = (pops, slot) if slot < 27 else (cot, slot - 27)
                    hi, lo = ref[i, x, :, 128:256], ref[i, x, :, 0:128]
                at = 16 * j + 4 * x
                moved = roll_l(jnp.where(top, hi, lo), mod128(at + 4 - 4 * gz))
                acc = jnp.where((lane >= at) & (lane < at + 4), moved, acc)
        msg[8 * n : 8 * n + 8, :] = acc


def first_kernel(pops, block, mask, cot, after, tx, ax, sx, msg0, msg1):
    gz = lax.axis_index("gz")

    def body(x, carry):
        for half in (0, 1):
            z = pl.ds(128 * half, 128)
            here = tile(2 * (x + 2) + half)
            s = solid_of(block[x, :, z], mask[x, :, z])
            sx[0, here, :] = s
            f = [pops[i, x, :, z] for i in range(27)]
            rho, u = moments(f)
            out = collide(f, s, rho, u)
            for i in range(27):
                tx[i, here, :] = out[i]
                ax[i, here, :] = cot[i, x, :, z]
        return carry

    lax.fori_loop(0, 4, body, 0)
    for msg, e in zip((msg0, msg1), sides("gx")):
        pack_faces(msg, e, 1, gz, (tx, ax, sx))


def strip_kernel(cut, tx, ax, sx, tm, am, sm, msg0, msg1):
    gz = lax.axis_index("gz")

    def slot(n):
        return roll_l(cut[8 * (n // 8) : 8 * (n // 8) + 8, :], (8 - 16 * (n % 8)) % 128)

    s = slot(54)
    sm[0] = s
    f = [slot(i) for i in range(27)]
    rho, u = moments(f)
    out = collide(f, s, rho, u)
    for i in range(27):
        tm[i] = out[i]
        am[i] = slot(27 + i)
    for msg, e in zip((msg0, msg1), sides("gy")):
        pack_sides(msg, e, 1, gz, (tx, ax, sx), (tm, am, sm))


def edge_kernel(tm, am, sm, got0, got1, msg0, msg1, tr, ar, sr, tmr, amr, smr):
    gz = lax.axis_index("gz")
    rows, strip_rows = (tr, ar, sr), (tmr, amr, smr)
    for msg, s in zip((got0, got1), sides("gy")):
        unpack_sides(msg, s, 1, rows, strip_rows)
    for msg, e in zip((msg0, msg1), sides("gx")):
        pack_edges(msg, e, 1, gz, rows, (tm, am, sm), strip_rows)


def edge_kernel_2(tm, got0, got1, msg0, msg1, tr, tmr):
    gz = lax.axis_index("gz")
    for msg, s in zip((got0, got1), sides("gy")):
        unpack_sides(msg, s, -1, (tr,), (tmr,))
    for msg, e in zip((msg0, msg1), sides("gx")):
        pack_edges(msg, e, -1, gz, (tr,), (tm,), (tmr,))


def gather_in(pairs, strips):
    def body(n, carry):
        later = Later(PACK_GROUP)
        for src, dst in pairs:
            for i in range(src.shape[0]):
                later.put(dst, (i, tile(n), ALL), src[i, tile(n), :])
        later.flush()
        return carry

    lax.fori_loop(4, 12, body, 0)
    for (_, dst), strip in zip(pairs, strips):
        for i in range(strip.shape[0]):
            dst[i, MINI, :] = strip[i]


def receive(orient, owns, rows, strip_rows, by_y, faces, edges):
    for msg, s in zip(by_y, sides("gy")):
        unpack_sides(msg, s, orient, rows, strip_rows)
    for face, edge, s in zip(faces, edges, sides("gx")):
        unpack_faces(face, s, orient, owns)
        unpack_edges(edge, s, orient, rows, owns, strip_rows)
    reflect_rows(rows[0], orient)


def insert(pairs):
    def body(k, carry):
        later = Later(PACK_GROUP)
        for src, dst in pairs:
            for i in range(src.shape[0]):
                later.put(dst, (i, tile(k + 6), ALL), src[i, octet(k), :])
        later.flush()
        return carry

    lax.fori_loop(0, 4, body, 0)


def inner_kernel(tx, ax, sx, tm, am, sm, y0, y1, f_in, c_in, u_in, p_in, t, a, tr, ar, sr, tmr, amr, smr, f, p):
    gz = lax.axis_index("gz")
    gather_in(((tx, t), (ax, a)), (tm, am))
    for msg, s in zip((y0, y1), sides("gy")):
        unpack_sides(msg, s, 1, (tr, ar, sr), (tmr, amr, smr))
    stream(t, tr, tmr, f, None, None, 1, gz, 3, 5, strip=False)
    stream(a, ar, amr, p, None, None, -1, gz, 3, 5, strip=False)

    def body(k, carry):
        here, there = tile(k + 6), octet(k)
        pops = [f[i, here, :] for i in range(27)]
        rho, u = moments(pops)
        for n, v in enumerate([rho] + u):
            u_in[n, there, :] = v
        out = collide(pops, sx[0, here, :], rho, u)
        for i in range(27):
            f_in[i, there, :] = pops[i]
            c_in[i, there, :] = out[i]
            p_in[i, there, :] = p[i, here, :]
        return carry

    lax.fori_loop(0, 4, body, 0)


def inner_kernel_2(a2, a2m, f1, u_own, s_own, y0, y1, c_in, q_in, t, tr, tmr, p):
    gz = lax.axis_index("gz")
    gather_in(((a2, t),), (a2m,))
    for msg, s in zip((y0, y1), sides("gy")):
        unpack_sides(msg, s, -1, (tr,), (tmr,))
    stream(t, tr, tmr, p, None, None, -1, gz, 3, 5, strip=False)

    def body(k, carry):
        here, there = tile(k + 6), octet(k)
        u = [u_own[n, here, :] for n in (1, 2, 3)]
        out, blame = pull_back([p[i, here, :] for i in range(27)], s_own[0, here, :], u, [f1[i, here, :] for i in range(27)], u_own[0, here, :])
        for i in range(27):
            c_in[i, there, :] = out[i]
        q_in[0, there, :] = blame
        return carry

    lax.fori_loop(0, 4, body, 0)


def outer_tile(k):
    return tile(jnp.where(k == 8, -1, jnp.where(k < 4, k + 2, k + 6)))


def middle_kernel(
    tx, ax, sx, tm, am, sm, y0, y1, x0, x1, e0, e1, f_in, c_in, u_in, p_in,
    a2, a2m, f1, u_own, u_rows, u_strip, s_own, s_rows, s_strip, q2, ym0, ym1, xm0, xm1,
    t, a, tr, ar, tmr, amr, fr, fmr, c, cr, cmr, f2, p,
):
    gz = lax.axis_index("gz")
    gather_in(((tx, t), (ax, a), (sx, s_own)), (tm, am, sm))
    receive(1, (t, a, s_own), (tr, ar, s_rows), (tmr, amr, s_strip), (y0, y1), (x0, x1), (e0, e1))
    stream(t, tr, tmr, f1, fr, fmr, 1, gz, 1, 7, inner=False)
    insert(((f_in, f1), (c_in, c), (u_in, u_own)))

    def collide_at(load, solid, store, store_u):
        f = [load(i) for i in range(27)]
        rho, u = moments(f)
        for n, v in enumerate([rho] + u):
            store_u(n, v)
        out = collide(f, solid, rho, u)
        for i in range(27):
            store(i, out[i])

    def again(k, carry):
        here = outer_tile(k)

        def put(i, v):
            c[i, here, :] = v

        def put_u(n, v):
            u_own[n, here, :] = v

        collide_at(lambda i: f1[i, here, :], s_own[0, here, :], put, put_u)
        return carry

    lax.fori_loop(0, 9, again, 0)

    def again_rows(k, carry):
        for half in (0, 1):
            here = octet(half)

            def put(i, v):
                cr[i, 2 * k, here, :] = v

            def put_u(n, v):
                u_rows[n, 2 * k, here, :] = v

            collide_at(lambda i: fr[i, 2 * k, here, :], s_rows[0, 2 * k, here, :], put, put_u)
        return carry

    lax.fori_loop(0, 2, again_rows, 0)

    def put_strip(i, v):
        cmr[i] = v

    def put_strip_u(n, v):
        u_strip[n] = v

    collide_at(lambda i: fmr[i], s_strip[0], put_strip, put_strip_u)
    stream(c, cr, cmr, f2, None, None, 1, gz, 2, 6)
    stream(a, ar, amr, p, None, None, -1, gz, 2, 6, inner=False)
    insert(((p_in, p),))

    def back(here):
        f = [f2[i, here, :] for i in range(27)]
        rho, u = moments(f)
        return pull_back([p[i, here, :] for i in range(27)], s_own[0, here, :], u, f, rho)

    def back_own(k, carry):
        here = tile(k + 4)
        out, blame = back(here)
        for i in range(27):
            a2[i, here, :] = out[i]
        q2[octet(k), :] = blame
        return carry

    lax.fori_loop(0, 8, back_own, 0)
    out, _ = back(MINI)
    for i in range(27):
        a2m[i] = out[i]
    for msg, e in zip((ym0, ym1), sides("gy")):
        pack_sides(msg, e, -1, gz, (a2,), (a2m,))
    for msg, e in zip((xm0, xm1), sides("gx")):
        pack_faces(msg, e, -1, gz, (a2,))


def last_kernel(
    a2, a2m, pops, mask, f1, u_own, u_rows, u_strip, s_own, s_rows, s_strip, q2, y0, y1, x0, x1, e0, e1, c_in, q_in,
    adjoint, grad,
    t, tr, tmr, p, pr, pmr, c, cr, cmr, q1,
):
    gz = lax.axis_index("gz")
    gather_in(((a2, t),), (a2m,))
    receive(-1, (t,), (tr,), (tmr,), (y0, y1), (x0, x1), (e0, e1))
    stream(t, tr, tmr, p, pr, pmr, -1, gz, 1, 7, inner=False)
    insert(((c_in, c), (q_in, q1)))

    def again(k, carry):
        here = outer_tile(k)
        u = [u_own[n, here, :] for n in (1, 2, 3)]
        out, blame = pull_back([p[i, here, :] for i in range(27)], s_own[0, here, :], u, [f1[i, here, :] for i in range(27)], u_own[0, here, :])
        for i in range(27):
            c[i, here, :] = out[i]
        q1[0, here, :] = blame
        return carry

    def again_outside(k, carry):
        here = outer_tile(jnp.where(k < 2, k, k + 4))
        out, _ = pull_back([p[i, here, :] for i in range(27)], s_own[0, here, :], [u_own[n, here, :] for n in (1, 2, 3)])
        for i in range(27):
            c[i, here, :] = out[i]
        return carry

    lax.fori_loop(2, 6, again, 0)
    lax.fori_loop(0, 5, again_outside, 0)

    def again_rows(k, carry):
        for half in (0, 1):
            here = octet(half)
            u = [u_rows[n, 2 * k, here, :] for n in (1, 2, 3)]
            out, _ = pull_back([pr[i, 2 * k, here, :] for i in range(27)], s_rows[0, 2 * k, here, :], u)
            for i in range(27):
                cr[i, 2 * k, here, :] = out[i]
        return carry

    lax.fori_loop(0, 2, again_rows, 0)
    out, _ = pull_back([pmr[i] for i in range(27)], s_strip[0], [u_strip[n] for n in (1, 2, 3)])
    for i in range(27):
        cmr[i] = out[i]
    stream(c, cr, cmr, p, None, None, -1, gz, 2, 6)

    def back(x, carry):
        for half in (0, 1):
            z = pl.ds(128 * half, 128)
            here = tile(2 * x + 4 + half)
            f = [pops[i, x, :, z] for i in range(27)]
            rho, u = moments(f)
            out, blame = pull_back([p[i, here, :] for i in range(27)], s_own[0, here, :], u, f, rho)
            for i in range(27):
                adjoint[i, x, :, z] = out[i]
            grad[x, :, z] = (1.0 - mask[x, :, z].astype(F32)) * (q1[0, here, :] + q2[octet(2 * x + half), :] + blame)
        return carry

    lax.fori_loop(0, 4, back, 0)


def call(kernel, outs, scratch=(), name=None, mib=8, in_specs=None, cost=None):
    return pl.pallas_call(
        kernel,
        out_shape=[jax.ShapeDtypeStruct(s, F32) for s in outs],
        scratch_shapes=[pltpu.VMEM(s, F32) if isinstance(s, tuple) else s for s in scratch],
        **({} if in_specs is None else {"in_specs": in_specs}),
        compiler_params=pltpu.CompilerParams(vmem_limit_bytes=mib * 1024 * 1024),
        name=name,
        cost_estimate=None if cost is None else pl.CostEstimate(flops=2000 * cost if name == "lead" else 0, bytes_accessed=cost, transcendentals=0),
    )


def swap(x, axis, odd):
    n = lax.axis_size(axis)
    pairs = [(i, (i ^ 1) if not odd else ((i + 1) % n if i % 2 else (i - 1) % n)) for i in range(n)]
    return lax.ppermute(x, axis, pairs)


BIG = (27, ROWS, 128)
ONE = (1, ROWS, 128)
QUAD = (27, 32, 128)
STRIP = (27, 8, 128)
STRIP1 = (1, 8, 128)
HALO = (27, 4, 16, 128)
HALO1 = (1, 4, 16, 128)


def face_shape(n):
    return (16 * n, 128)


def side_shape(n):
    return (8 * n + -(-n // 8) * 8, 128)


def edge_shape(extra):
    n = 37 if extra else 27
    return (-(-edge_rows(1, 1, extra) // 8) * 8 + 16 * (-(-n // 32)), 128)


def swaps(pair, axis):
    return [swap(pair[0], axis, False), swap(pair[1], axis, True)]


def body(populations, blockage, solid_mask, cotangent):
    (lead,) = call(lead_kernel, [(8, 128)], name="lead", cost=12_000_000)()
    (cut,) = call(cut_kernel, [(56, 128)], name="cut")(populations, blockage, solid_mask, cotangent, lead)
    tx, ax, sx, *faces = call(first_kernel, [BIG, BIG, ONE, face_shape(37), face_shape(37)], name="first")(
        populations, blockage, solid_mask, cotangent, cut
    )
    cut = lax.ppermute(cut, "gz", [(0, 1), (1, 0)])
    tm, am, sm, *by_y = call(strip_kernel, [STRIP, STRIP, STRIP1, side_shape(37), side_shape(37)], name="strip")(cut, tx, ax, sx)
    by_y = swaps(by_y, "gy")
    faces, _ = lax.optimization_barrier((faces, tm))
    faces = swaps(faces, "gx")
    edges = call(
        edge_kernel, [edge_shape(True)] * 2, scratch=[HALO, HALO, HALO1, STRIP, STRIP, STRIP1], name="edge", mib=12
    )(tm, am, sm, *by_y)
    edges = swaps(edges, "gx")
    inner = call(
        inner_kernel,
        [QUAD, QUAD, (4, 32, 128), QUAD],
        scratch=[BIG, BIG, HALO, HALO, HALO1, STRIP, STRIP, STRIP1, BIG, BIG],
        name="inner",
        mib=20,
        cost=6_000_000,
    )(tx, ax, sx, tm, am, sm, *by_y)
    a2, a2m, f1, u_own, u_rows, u_strip, s_own, s_rows, s_strip, q2, *out = call(
        middle_kernel,
        [BIG, STRIP, BIG, (4, ROWS, 128), (4, 4, 16, 128), (4, 8, 128), ONE, HALO1, STRIP1, (64, 128)]
        + [(440, 128)] * 2
        + [face_shape(27)] * 2,
        scratch=[BIG, BIG, HALO, HALO, STRIP, STRIP, HALO, STRIP, BIG, HALO, STRIP, BIG, BIG],
        name="middle",
        mib=24,
    )(tx, ax, sx, tm, am, sm, *by_y, *faces, *edges, *inner)
    by_y = swaps(out[:2], "gy")
    faces = swaps(out[2:], "gx")
    edges = call(edge_kernel_2, [edge_shape(False)] * 2, scratch=[HALO, STRIP], name="edge2", mib=8)(a2m, *by_y)
    edges = swaps(edges, "gx")
    inner = call(
        inner_kernel_2, [QUAD, (1, 32, 128)], scratch=[BIG, HALO, STRIP, BIG], name="inner2", mib=14, cost=6_000_000
    )(a2, a2m, f1, u_own, s_own, *by_y)
    adjoint, grad = call(
        last_kernel,
        [populations.shape, blockage.shape],
        scratch=[BIG, HALO, STRIP, BIG, HALO, STRIP, BIG, HALO, STRIP, ONE],
        name="last",
        mib=20,
    )(a2, a2m, populations, solid_mask, f1, u_own, u_rows, u_strip, s_own, s_rows, s_strip, q2, *by_y, *faces, *edges, *inner)
    return adjoint, grad


def solution(mesh):
    placed = (P(None, "gx", "gy", "gz"), P("gx", "gy", "gz"), P("gx", "gy", "gz"), P(None, "gx", "gy", "gz"))
    return jax.shard_map(
        body, mesh=mesh, in_specs=placed, out_specs=(P(None, "gx", "gy", "gz"), P("gx", "gy", "gz")), check_vma=False
    )
```
